32 devices in a mesh: seq: 8 (over y, x, core), mp: 4 (over z).
Axes of the slice: x: 2, y: 2, z: 4, core: 2. Of those that a mesh axis runs over, the one named last changes fastest.
Arguments:
- tokens: bfloat16 [2088, 1024], P('seq', 'mp'), may hold values from -6 to 6
- grad_out: bfloat16 [2088, 1024], P('seq', 'mp'), may hold values from -6 to 6
- frame_counts: int32 [2], replicated, may hold values from 1 to 7, as said below
- slot_frames: int32 [8], replicated, may hold values from 0 to 7, as said below
- block_norm_multiplier: float32 [2, 2, 1024], P(None, None, 'mp'), may hold values from 0.25 to 1.75
- block_norm_bias: float32 [2, 2, 1024], P(None, None, 'mp'), may hold values from -3 to 3
- qk_gain: float32 [2, 2, 64], replicated, may hold values from 0.25 to 1.75
- qk_bias: float32 [2, 2, 64], replicated, may hold values from -3 to 3
- w_qkv: bfloat16 [2, 3, 1024, 1024], P(None, None, None, 'mp'), may hold values from -0.1875 to 0.1875
- w_out: bfloat16 [2, 1024, 1024], P(None, 'mp'), may hold values from -0.75 to 0.75
- w_up: bfloat16 [2, 1024, 4096], P(None, None, 'mp'), may hold values from -1 to 1
- w_down: bfloat16 [2, 4096, 1024], P(None, 'mp'), may hold values from -0.09375 to 0.09375
- layer_scale: float32 [2, 2, 1024], P(None, None, 'mp'), may hold values from 0.3 to 1.5
Outputs:
- out_tokens: bfloat16 [2088, 1024], P('seq', 'mp')
- grad_tokens: float32 [2088, 1024], P('seq', 'mp')
- grad_norm_gain: float32 [2, 2, 1024], P(None, None, 'mp')
- grad_norm_bias: float32 [2, 1024], P(None, 'mp')
- grad_mlp_norm_bias: float32 [2, 1024], P(None, 'mp')
- grad_qk_gain: float32 [2, 2, 64], replicated
- grad_qk_bias: float32 [2, 2, 64], replicated
- grad_w_qkv: float32 [2, 3, 1024, 1024], P(None, None, 'seq', 'mp')
- grad_w_out: float32 [2, 1024, 1024], P(None, 'mp', 'seq')
- grad_w_up: float32 [2, 1024, 4096], P(None, 'seq', 'mp')
- grad_w_down: float32 [2, 4096, 1024], P(None, 'mp', 'seq')
- grad_layer_scale: float32 [2, 2, 1024], P(None, None, 'mp')
The draws below stay inside these ranges and needn't reach their ends.
Inputs may be any that keep to these rules, and one draw needn't show every extreme that they name: `frame_counts`: scenes 2j and 2j + 1 together hold 8 frames, so the counts sum to 8; one scene holds exactly 7 frames. A permutation of the 8 frames: slot s, on device s // 1 of seq, holds frame slot_frames[s]; frames are numbered scene after scene.
All inputs are finite; a program needn't handle non-finite values.
Results may differ from the reference program's by a relative error of at most 0.018.
Values may be sent and summed in bfloat16 or wider, within the bound.
A program may use at most 192 MiB of HBM per device.

```python
import math
import jax
import jax.numpy as jnp
from jax import lax

D = 1024
HEADS = 16
HD = 64
FF = 4096
TOK = 261
SCENE_FRAMES = 7
F_DEV = 1
FRAMES = 8
ROWS = 2088


def scene_plan(key):
    group = SCENE_FRAMES + 1
    pair_count = FRAMES // group
    first_counts = jax.random.randint(jax.random.fold_in(key, 11), (pair_count,), 1, SCENE_FRAMES + 1)
    widest = jax.random.randint(jax.random.fold_in(key, 12), (), 0, pair_count)
    first_counts = jnp.where(jnp.arange(pair_count) == widest, SCENE_FRAMES, first_counts)
    counts = jnp.stack([first_counts, group - first_counts], axis=1).reshape(2 * pair_count)
    return (counts.astype(jnp.int32), widest.astype(jnp.int32))


def draw_frame_counts(key, part):
    return scene_plan(key)[0]


def draw_slot_frames(key, part):
    counts, widest = scene_plan(key)
    group = SCENE_FRAMES + 1
    ordering = jax.random.permutation(jax.random.fold_in(key, 13), FRAMES).astype(jnp.int32)
    positions = jnp.arange(FRAMES, dtype=jnp.int32)
    base_frame = widest * group
    chosen_slots = (0, FRAMES // F_DEV // 2 * F_DEV, FRAMES - 1)
    for offset_id, slot_id in enumerate(chosen_slots):
        target = (base_frame + offset_id).astype(jnp.int32)
        place_now = jnp.sum(jnp.where(ordering == target, positions, 0))
        held_frame = ordering[slot_id]
        ordering = ordering.at[slot_id].set(target)
        ordering = ordering.at[place_now].set(held_frame)
    return ordering


def draw_w_up(key, part):
    key = jax.random.fold_in(key, 21)
    spread_key = jax.random.fold_in(key, 1)
    fan_scale = D ** (-0.5)
    values = jax.random.truncated_normal(spread_key, -4.0, 4.0, (2, D, FF), jnp.float32) * fan_scale
    return values.astype(jnp.bfloat16)


def shard_levels(stream_key, dims, cuts, least, largest):
    loudness, own = 1.0, jax.random.fold_in(stream_key, 6)
    for dim, shards_of in cuts:
        heights = jnp.exp(jax.random.uniform(jax.random.fold_in(own, dim), (shards_of,), jnp.float32, least / len(cuts), largest / len(cuts)))
        loudness = loudness * jnp.repeat(heights, dims[dim] // shards_of).reshape([-1 if axis == dim else 1 for axis in range(len(dims))])
    return loudness


def bell_draw(stream_key, dims, scale, reach, pieces=(), kind=jnp.bfloat16):
    values = scale * jax.random.normal(stream_key, dims, jnp.float32)
    if pieces:
        values = values * shard_levels(stream_key, dims, pieces, -0.22, 0.18)
    return jnp.clip(values, -reach, reach).astype(kind)


def setup_inputs(seed: int = 0) -> dict:
    streams_of = jax.random.split(jax.random.key(seed), 14)
    tokens = bell_draw(streams_of[0], (ROWS, D), 1.0, 6.0, ((0, 8), (1, 4)))
    grad_out = bell_draw(streams_of[1], (ROWS, D), 1.0, 6.0, ((0, 8), (1, 4)))
    frame_counts = draw_frame_counts(jax.random.fold_in(streams_of[13], 71), 0)
    slot_frames = draw_slot_frames(jax.random.fold_in(streams_of[13], 71), 0)
    block_norm_multiplier = jnp.clip(1.0 + 0.15 * jax.random.normal(streams_of[4], (2, 2, D), jnp.float32), 0.25, 1.75)
    block_norm_bias = bell_draw(streams_of[5], (2, 2, D), 0.3, 3.0, ((2, 4),), jnp.float32)
    qk_gain = jnp.clip(1.0 + 0.15 * jax.random.normal(streams_of[6], (2, 2, HD), jnp.float32), 0.25, 1.75)
    qk_bias = bell_draw(streams_of[7], (2, 2, HD), 0.3, 3.0, (), jnp.float32)
    w_qkv = bell_draw(streams_of[8], (2, 3, D, D), D ** -0.5, 0.1875, ((3, 4),))
    w_out = bell_draw(streams_of[9], (2, D, D), (D // 16) ** -0.5, 0.75, ((1, 4),))
    w_up = draw_w_up(jax.random.fold_in(streams_of[13], 71), 0)
    w_down = bell_draw(streams_of[11], (2, FF, D), FF ** -0.5, 0.09375, ((1, 4),))
    layer_scale = jnp.clip(jnp.exp(math.log(1.5) - 1.60943787 * jax.random.uniform(streams_of[12], (2, 2, D), jnp.float32) ** shard_levels(streams_of[12], (2, 2, D), ((2, 4),), -0.2, 0.2)), 0.3, 1.5)
    return dict(tokens=tokens, grad_out=grad_out, frame_counts=frame_counts, slot_frames=slot_frames, block_norm_multiplier=block_norm_multiplier, block_norm_bias=block_norm_bias, qk_gain=qk_gain, qk_bias=qk_bias, w_qkv=w_qkv, w_out=w_out, w_up=w_up, w_down=w_down, layer_scale=layer_scale)


EPS = 1e-06
HIGH = lax.Precision.HIGHEST

@jax.custom_vjp
def low(v):
    return lax.optimization_barrier(v.astype(jnp.bfloat16)).astype(jnp.float32)

@jax.custom_vjp
def low_back(v):
    return v

def low_keep(v):
    return (low(v), None)

def low_pass(kept, grad):
    return (grad,)

def back_keep(v):
    return (v, None)

def back_low(kept, grad):
    return (low(grad),)
low.defvjp(low_keep, low_pass)
low_back.defvjp(back_keep, back_low)

def layer_norm(value, norm_multiplier, shift_bias):
    feature_mean = lax.optimization_barrier(jnp.mean(value, axis=-1, keepdims=True))
    centered_input = value - feature_mean
    variance = lax.optimization_barrier(jnp.mean(centered_input * centered_input, axis=-1, keepdims=True))
    return centered_input * lax.rsqrt(variance + EPS) * norm_multiplier + shift_bias

def attend(query_rows, key_rows, value_rows, allowed):
    scores = low_back(jnp.einsum('qhd,khd->hqk', query_rows, key_rows, precision=HIGH))
    scores = jnp.where(allowed[None], scores, -1e+30)
    peak = lax.optimization_barrier(jnp.max(scores, axis=-1, keepdims=True))
    expo = jnp.exp(scores - peak)
    probs = low(expo / lax.optimization_barrier(jnp.sum(expo, axis=-1, keepdims=True)))
    return jnp.einsum('hqk,khd->qhd', probs, value_rows, precision=HIGH)

def pair_attend(group_items):
    return attend(group_items[0], group_items[1], group_items[2], group_items[3])

def reference(tokens, grad_out, frame_counts, slot_frames, block_norm_multiplier, block_norm_bias, qk_gain, qk_bias, w_qkv, w_out, w_up, w_down, layer_scale):
    frame_ids = jnp.arange(FRAMES, dtype=jnp.int32)
    slot_of_frame = jnp.zeros((FRAMES,), jnp.int32).at[slot_frames].set(frame_ids)
    scene_ends = jnp.cumsum(frame_counts).astype(jnp.int32)
    scene_of_frame = lax.optimization_barrier(jnp.sum((scene_ends[None, :] <= frame_ids[:, None]).astype(jnp.int32), axis=1))
    group = SCENE_FRAMES + 1
    pair_count = FRAMES // group
    scene_rows = jnp.repeat(scene_of_frame, TOK).reshape(pair_count, group * TOK)
    allowed_global = scene_rows[:, :, None] == scene_rows[:, None, :]
    allowed_frame = jnp.ones((TOK, TOK), dtype=bool)
    start_input = tokens.astype(jnp.float32).reshape(FRAMES, TOK, D)[slot_of_frame].reshape(ROWS, D)
    incoming_gradient = grad_out.astype(jnp.float32).reshape(FRAMES, TOK, D)[slot_of_frame].reshape(ROWS, D)

    def forward(residual_stream, gains, biases, qgains, qbiases, wqkv, wout, wup, wdown, scales):
        for block_number in range(2):
            hidden_units = low(layer_norm(residual_stream, gains[block_number, 0], biases[block_number, 0]))
            query_raw = low_back(jnp.dot(hidden_units, wqkv[block_number, 0], precision=HIGH)).reshape(ROWS, HEADS, HD)
            key_raw = low_back(jnp.dot(hidden_units, wqkv[block_number, 1], precision=HIGH)).reshape(ROWS, HEADS, HD)
            value_rows = low(low_back(jnp.dot(hidden_units, wqkv[block_number, 2], precision=HIGH))).reshape(ROWS, HEADS, HD)
            query_rows = low(layer_norm(query_raw, qgains[block_number, 0], qbiases[block_number, 0]) * HD ** (-0.5))
            key_rows = low(layer_norm(key_raw, qgains[block_number, 1], qbiases[block_number, 1]))
            if block_number == 0:
                shaped = (FRAMES, TOK, HEADS, HD)
                attended = jax.vmap(attend, in_axes=(0, 0, 0, None))(query_rows.reshape(shaped), key_rows.reshape(shaped), value_rows.reshape(shaped), allowed_frame)
            else:
                shaped = (pair_count, group * TOK, HEADS, HD)
                attended = lax.map(jax.checkpoint(pair_attend), (query_rows.reshape(shaped), key_rows.reshape(shaped), value_rows.reshape(shaped), allowed_global))
            attended = low(low_back(attended.reshape(ROWS, D)))
            branch = low_back(jnp.dot(attended, wout[block_number], precision=HIGH))
            residual_stream = residual_stream + scales[block_number, 0] * branch
            mlp_in = low(layer_norm(residual_stream, gains[block_number, 1], biases[block_number, 1]))
            pre_act = low_back(jnp.dot(mlp_in, wup[block_number], precision=HIGH))
            activated = low(jax.nn.gelu(pre_act, approximate=False))
            mlp_out = low_back(jnp.dot(activated, wdown[block_number], precision=HIGH))
            residual_stream = residual_stream + scales[block_number, 1] * mlp_out
        return residual_stream
    result, pullback = jax.vjp(forward, start_input, block_norm_multiplier.astype(jnp.float32), block_norm_bias.astype(jnp.float32), qk_gain.astype(jnp.float32), qk_bias.astype(jnp.float32), w_qkv.astype(jnp.float32), w_out.astype(jnp.float32), w_up.astype(jnp.float32), w_down.astype(jnp.float32), layer_scale.astype(jnp.float32))
    grads = pullback(incoming_gradient)
    out_slots = result.reshape(FRAMES, TOK, D)[slot_frames].reshape(ROWS, D)
    grad_slots = grads[0].reshape(FRAMES, TOK, D)[slot_frames].reshape(ROWS, D)
    return (out_slots.astype(jnp.bfloat16), grad_slots, grads[1], grads[2][:, 0], grads[2][:, 1], grads[3], grads[4], grads[5], grads[6], grads[7], grads[8], grads[9])
```

```python
from functools import partial

import jax
import jax.numpy as jnp
from jax import lax
from jax.experimental import pallas as pl
from jax.experimental.pallas import tpu as pltpu
from jax.sharding import PartitionSpec as P

HD = 64
TOK = 261
EPS = 1e-06
NEG = -1e30

RP = 272
CH = 64
RO = 80
NZ = 4
WIDE = 256
F32 = jnp.float32
BF = jnp.bfloat16
MESH = pl.DeviceIdType.MESH
HIGH = lax.Precision.HIGHEST


def dot(left, right):
    return jnp.dot(left, right, preferred_element_type=F32)


def dot_cols(left, right):
    return lax.dot_general(left, right, (((1,), (1,)), ((), ())), preferred_element_type=F32)


def dot_rows(left, right):
    return lax.dot_general(left, right, (((0,), (0,)), ((), ())), preferred_element_type=F32)


def tile(index, width=WIDE):
    return pl.ds(pl.multiple_of(index * width, width), width)


def standardize(x):
    mean = jnp.mean(x, axis=1, keepdims=True)
    centered = x - mean
    variance = jnp.mean(centered * centered, axis=1, keepdims=True)
    rstd = lax.rsqrt(variance + EPS)
    return centered * rstd, rstd


def norm_back(dnorm, x, multiplier, valid):
    xhat, rstd = standardize(x)
    gain = jnp.sum(jnp.where(valid, dnorm * xhat, 0.0), axis=0, keepdims=True)
    bias = jnp.sum(jnp.where(valid, dnorm, 0.0), axis=0, keepdims=True)
    e = dnorm * multiplier
    dv = rstd * (
        e - jnp.mean(e, axis=1, keepdims=True) - xhat * jnp.mean(e * xhat, axis=1, keepdims=True)
    )
    return dv, gain, bias


def head_means():
    row = lax.broadcasted_iota(jnp.int32, (WIDE, WIDE), 0)
    col = lax.broadcasted_iota(jnp.int32, (WIDE, WIDE), 1)
    same = lax.shift_right_logical(row, 6) == lax.shift_right_logical(col, 6)
    return jnp.where(same, 1.0 / HD, 0.0).astype(F32)


def mean_heads(x, means):
    return jnp.dot(x, means, precision=HIGH, preferred_element_type=F32)


def head_standardize(raw, means):
    centered = raw - mean_heads(raw, means)
    rstd = lax.rsqrt(mean_heads(centered * centered, means) + EPS)
    return centered * rstd, rstd


def head_back(dy, xhat, rstd, gain, means):
    e = dy * gain
    raw = rstd * (e - mean_heads(e, means) - xhat * mean_heads(e * xhat, means))
    return (
        raw,
        jnp.sum(dy * xhat, axis=0, keepdims=True),
        jnp.sum(dy, axis=0, keepdims=True),
    )


def lane_head(rows, width=WIDE):
    return lax.shift_right_logical(lax.broadcasted_iota(jnp.int32, (rows, width), 1), 6)


def key_valid():
    return lax.broadcasted_iota(jnp.int32, (RP, RP), 1) < TOK


def own_valid(z):
    row = lax.broadcasted_iota(jnp.int32, (RO, 1), 0)
    return (row < CH) | ((z == NZ - 1) & (row < TOK - (NZ - 1) * CH))


def remote(src, dst, send, recv, device):
    return pltpu.make_async_remote_copy(
        src_ref=src, dst_ref=dst, send_sem=send, recv_sem=recv, device_id=device, device_id_type=MESH
    )


def greet(devices):
    barrier = pltpu.get_barrier_semaphore()
    for device in devices:
        pl.semaphore_signal(barrier, inc=1, device_id=device, device_id_type=MESH)
    pl.semaphore_wait(barrier, len(devices))


def line(s, z):
    return [(s, lax.rem(z + d, NZ)) for d in range(1, NZ)]


def sized(last, act):
    pl.when(last)(lambda: act(RO))
    pl.when(jnp.logical_not(last))(lambda: act(CH))


def block(z, rows):
    return pl.ds(pl.multiple_of(z * CH, CH), rows)


def own_rows(z):
    return pl.ds(pl.multiple_of(z * CH, CH), RO)


def put_own(full, z, value):
    full[block(z, CH)] = value[:CH]

    @pl.when(z == NZ - 1)
    def _():
        full[pl.ds(NZ * CH, RO - CH)] = value[CH:]


def gather_start(full, s, z, send, recv):
    for d in range(1, NZ):
        peer = lax.rem(z + d, NZ)

        def act(rows, d=d, peer=peer):
            mine = full.at[block(z, rows)]
            remote(mine, mine, send.at[d - 1], recv.at[d - 1], (s, peer)).start()

        sized(z == NZ - 1, act)


def gather_wait(full, s, z, send, recv):
    for d in range(1, NZ):
        source = lax.rem(z + NZ - d, NZ)

        def act(rows, d=d, source=source):
            theirs = full.at[block(source, rows)]
            remote(theirs, theirs, send.at[d - 1], recv.at[d - 1], (s, source)).wait_recv()

        sized(source == NZ - 1, act)
    for d in range(1, NZ):
        peer = lax.rem(z + d, NZ)

        def act(rows, d=d, peer=peer):
            mine = full.at[block(z, rows)]
            remote(mine, mine, send.at[d - 1], recv.at[d - 1], (s, peer)).wait_send()

        sized(z == NZ - 1, act)


def scatter_start(part, inbox, s, z, send, recv):
    for d in range(1, NZ):
        peer = lax.rem(z + d, NZ)

        def act(rows, d=d, peer=peer):
            remote(
                part.at[block(peer, rows)],
                inbox.at[d - 1, pl.ds(0, rows)],
                send.at[d - 1],
                recv.at[d - 1],
                (s, peer),
            ).start()

        sized(peer == NZ - 1, act)


def scatter_wait(part, inbox, s, z, send, recv):
    for d in range(1, NZ):
        source = lax.rem(z + NZ - d, NZ)
        peer = lax.rem(z + d, NZ)

        def act_in(rows, d=d, source=source):
            remote(
                part.at[block(z, rows)],
                inbox.at[d - 1, pl.ds(0, rows)],
                send.at[d - 1],
                recv.at[d - 1],
                (s, source),
            ).wait_recv()

        def act_out(rows, d=d, peer=peer):
            remote(
                part.at[block(peer, rows)],
                inbox.at[d - 1, pl.ds(0, rows)],
                send.at[d - 1],
                recv.at[d - 1],
                (s, peer),
            ).wait_send()

        sized(z == NZ - 1, act_in)
        sized(peer == NZ - 1, act_out)
    total = part[own_rows(z)].astype(F32)
    for d in range(1, NZ):
        total = total + inbox[d - 1].astype(F32)
    return total


def features_start(rows_ref, full, s, z, send, recv):
    for d in range(1, NZ):
        peer = lax.rem(z + d, NZ)

        def act(rows, d=d, peer=peer):
            remote(
                rows_ref.at[pl.ds(0, rows), tile(peer)],
                full.at[block(z, rows)],
                send.at[d - 1],
                recv.at[d - 1],
                (s, peer),
            ).start()

        sized(z == NZ - 1, act)
    put_own(full, z, rows_ref[:, tile(z)])


def features_wait(rows_ref, full, s, z, send, recv):
    for d in range(1, NZ):
        source = lax.rem(z + NZ - d, NZ)
        peer = lax.rem(z + d, NZ)

        def act_in(rows, d=d, source=source):
            remote(
                rows_ref.at[pl.ds(0, rows), tile(z)],
                full.at[block(source, rows)],
                send.at[d - 1],
                recv.at[d - 1],
                (s, source),
            ).wait_recv()

        def act_out(rows, d=d, peer=peer):
            remote(
                rows_ref.at[pl.ds(0, rows), tile(peer)],
                full.at[block(z, rows)],
                send.at[d - 1],
                recv.at[d - 1],
                (s, peer),
            ).wait_send()

        sized(source == NZ - 1, act_in)
        sized(z == NZ - 1, act_out)


def columns_start(block_ref, full, s, z, send, recv):
    width = block_ref.shape[1]
    full[:, tile(z, width)] = block_ref[...]
    for d in range(1, NZ):
        peer = lax.rem(z + d, NZ)
        remote(
            block_ref, full.at[:, tile(z, width)], send.at[d - 1], recv.at[d - 1], (s, peer)
        ).start()


def columns_wait(block_ref, full, s, z, send, recv):
    width = block_ref.shape[1]
    for d in range(1, NZ):
        source = lax.rem(z + NZ - d, NZ)
        remote(
            block_ref, full.at[:, tile(source, width)], send.at[d - 1], recv.at[d - 1], (s, source)
        ).wait()


def fetch(sources, targets, sems):
    return [
        pltpu.make_async_copy(source, target, sems.at[number])
        for number, (source, target) in enumerate(zip(sources, targets))
    ]


def project(hidden, weights, raw, queries, keys, values, head_params, block_number, means):
    gains = head_params
    scale = HD ** (-0.5)
    for c in range(3):
        product = dot(hidden[...], weights[c])
        if c == 2:
            values[...] = product.astype(BF)
            continue
        raw[c] = product
        xhat, _ = head_standardize(product, means)
        row = 2 * block_number + c
        normed = xhat * gains[row : row + 1] + gains[4 + row : 5 + row]
        if c == 0:
            queries[...] = (normed * scale).astype(BF)
        else:
            keys[...] = normed.astype(BF)


def apply_norm(x, params, b, j):
    xhat, _ = standardize(x)
    row = 2 * b + j
    return (xhat * params[row : row + 1] + params[4 + row : 5 + row]).astype(BF)


def up_gelu(hidden, w_up, act, slope):
    def step(j, carry):
        cols = tile(j)
        pre = dot(hidden[...], w_up[:, cols])
        cdf = 0.5 * (1.0 + lax.erf(pre * (0.5**0.5)))
        act[:, cols] = (pre * cdf).astype(BF)
        slope[:, cols] = cdf + pre * jnp.exp(-0.5 * pre * pre) * 0.3989422804014327
        return carry

    lax.fori_loop(0, w_up.shape[1] // WIDE, step, 0)


def times(left, weights, part):
    def step(j, carry):
        cols = tile(j)
        part[:, cols] = dot(left[...], weights[:, cols]).astype(BF)
        return carry

    lax.fori_loop(0, weights.shape[1] // WIDE, step, 0)


def times_turned(left, weights, part):
    def step(j, carry):
        part[:, tile(j)] = dot_cols(left[...], weights[tile(j), :]).astype(BF)
        return carry

    lax.fori_loop(0, weights.shape[0] // WIDE, step, 0)


def weight_grad(left, right, out):
    def step(j, carry):
        out[tile(j), :] = dot_rows(left[:, tile(j)], right[...]).astype(BF)
        return carry

    lax.fori_loop(0, left.shape[1] // WIDE, step, 0)


def mlp_back(dmlp, w_down, slope, dpre):
    def step(j, carry):
        cols = tile(j)
        dact = dot_cols(dmlp[...], w_down[cols, :])
        dpre[:, cols] = (dact * slope[:, cols]).astype(BF)
        return carry

    lax.fori_loop(0, w_down.shape[0] // WIDE, step, 0)


def attention_input_back(dproj, w_qkv, part):
    def step(j, carry):
        rows = tile(j)
        total = dot_cols(dproj[0], w_qkv[0, rows, :])
        total = total + dot_cols(dproj[1], w_qkv[1, rows, :])
        total = total + dot_cols(dproj[2], w_qkv[2, rows, :])
        part[:, rows] = total.astype(BF)
        return carry

    lax.fori_loop(0, w_qkv.shape[1] // WIDE, step, 0)


def qkv_weight_grad(hidden, dproj, out):
    def step(j, carry):
        left = hidden[:, tile(j)]
        for c in range(3):
            out[c, tile(j), :] = dot_rows(left, dproj[c]).astype(BF)
        return carry

    lax.fori_loop(0, hidden.shape[1] // WIDE, step, 0)


def heads_back(raw, dq, dk, dv, head_params, block_number, means, dproj, head_sums):
    row = 2 * block_number
    gains = head_params
    for c, dy in ((0, dq * (HD ** (-0.5))), (1, dk)):
        xhat, rstd = head_standardize(raw[c], means)
        draw, gain, bias = head_back(dy, xhat, rstd, gains[row + c : row + c + 1], means)
        dproj[c] = draw.astype(BF)
        head_sums[c : c + 1] = gain
        head_sums[2 + c : 3 + c] = bias
    dproj[2] = dv.astype(BF)


def first_kernel(
    tokens,
    params,
    head_params,
    w_qkv,
    w_out,
    w_up,
    w_down,
    params_full,
    x0,
    h0,
    raw0,
    q0,
    k0,
    v0,
    att0,
    x1,
    br0,
    m0,
    act0,
    slope0,
    mo0,
    x2,
    h1,
    raw1,
    q1,
    k1,
    v1,
    padded,
    every,
    part,
    inbox,
    wq0,
    wq1,
    wo,
    wu,
    wd,
    fetch_sem,
    send,
    recv,
):
    s, z = lax.axis_index("seq"), lax.axis_index("mp")
    copies = fetch(
        (w_qkv.at[0], w_out.at[0], w_up.at[0], w_down.at[0], w_qkv.at[1]),
        (wq0, wo, wu, wd, wq1),
        fetch_sem,
    )
    for copy in copies:
        copy.start()
    padded[pl.ds(CH * NZ, RP - CH * NZ)] = jnp.zeros((RP - CH * NZ, WIDE), BF)
    padded[pl.ds(0, TOK)] = tokens[...]
    greet(line(s, z))
    columns_start(padded, every, s, z, send.at[0], recv.at[0])
    columns_start(params, params_full, s, z, send.at[1], recv.at[1])
    means = head_means()
    columns_wait(params, params_full, s, z, send.at[1], recv.at[1])
    columns_wait(padded, every, s, z, send.at[0], recv.at[0])

    h0[...] = apply_norm(every[...].astype(F32), params_full, 0, 0)
    x0[...] = every[own_rows(z)].astype(F32)
    copies[0].wait()
    project(h0, wq0, raw0, q0, k0, v0, head_params, 0, means)

    heads = lane_head(RP)
    keep = key_valid()
    queries = q0[...].astype(F32)
    attended = jnp.zeros((RP, WIDE), F32)
    for h in range(WIDE // HD):
        qh = jnp.where(heads == h, queries, 0.0).astype(BF)
        scores = jnp.where(keep, dot_cols(qh, k0[...]), NEG)
        expo = jnp.exp(scores - jnp.max(scores, axis=1, keepdims=True))
        probs = (expo * (1.0 / jnp.sum(expo, axis=1, keepdims=True))).astype(BF)
        attended = jnp.where(heads == h, dot(probs, v0[...]), attended)
    att0[...] = attended.astype(BF)

    copies[1].wait()
    times(att0, wo, part)
    scatter_start(part, inbox.at[0], s, z, send.at[2], recv.at[2])
    branch = scatter_wait(part, inbox.at[0], s, z, send.at[2], recv.at[2])
    br0[...] = branch
    mid = x0[...] + params_full[8:9] * branch
    x1[...] = mid
    put_own(m0, z, apply_norm(mid, params_full, 0, 1))
    gather_start(m0, s, z, send.at[3], recv.at[3])
    copies[2].wait()
    copies[3].wait()
    gather_wait(m0, s, z, send.at[3], recv.at[3])
    up_gelu(m0, wu, act0, slope0)
    times(act0, wd, part)
    scatter_start(part, inbox.at[1], s, z, send.at[4], recv.at[4])
    branch = scatter_wait(part, inbox.at[1], s, z, send.at[4], recv.at[4])
    mo0[...] = branch
    result = x1[...] + params_full[9:10] * branch
    x2[...] = result
    put_own(h1, z, apply_norm(result, params_full, 1, 0))
    gather_start(h1, s, z, send.at[5], recv.at[5])
    copies[4].wait()
    gather_wait(h1, s, z, send.at[5], recv.at[5])
    project(h1, wq1, raw1, q1, k1, v1, head_params, 1, means)


def chips(s):
    return lax.shift_right_logical(s, 1), lax.rem(s, 2)


def place(first, second):
    row = lax.broadcasted_iota(jnp.int32, (WIDE, 2 * WIDE), 0)
    col = lax.broadcasted_iota(jnp.int32, (WIDE, 2 * WIDE), 1)
    within = lax.bitwise_and(col, 127)
    head = lax.shift_right_logical(col, 7)
    left = jnp.where((within < HD) & (row == head * HD + within), 1.0, 0.0).astype(BF)
    right = jnp.where((within >= HD) & (row == head * HD + within - HD), 1.0, 0.0).astype(BF)
    return left if first else right


def swap_halves():
    row = lax.broadcasted_iota(jnp.int32, (2 * HD, 2 * HD), 0)
    col = lax.broadcasted_iota(jnp.int32, (2 * HD, 2 * HD), 1)
    return jnp.where(lax.bitwise_and(row + HD, 127) == col, 1.0, 0.0).astype(BF)


def global_peers(s, z):
    a, core = chips(s)
    return [(2 * lax.rem(a + d, 4) + core, z) for d in range(1, 4)]


def global_forward_kernel(
    queries,
    keys,
    values,
    grad_out,
    bias,
    qk,
    vv,
    ks,
    lse,
    att,
    grad_full,
    slabs,
    pairs,
    outs,
    ins,
    padded,
    send,
    recv,
    core_send,
    core_recv,
    back_send,
    back_recv,
    z_send,
    z_recv,
):
    s, z = lax.axis_index("seq"), lax.axis_index("mp")
    a, core = chips(s)
    sibling = (2 * a + 1 - core, z)
    packed = dot(queries[...], place(True, False)) + dot(keys[...], place(False, True))
    for c in range(4):
        slabs[c] = packed[:, 128 * c : 128 * c + 128].astype(BF)
    for p in range(2):
        pairs[p] = values[:, 128 * p : 128 * p + 128]
    padded[pl.ds(CH * NZ, RP - CH * NZ)] = jnp.zeros((RP - CH * NZ, WIDE), BF)
    padded[pl.ds(0, TOK)] = grad_out[...]
    greet(global_peers(s, z) + [sibling] + line(s, z))

    def toward(d):
        c = lax.rem(a + d, 4)
        target = (2 * c + core, z)
        return (
            remote(slabs.at[c], qk.at[s], send.at[0, d - 1], recv.at[0, d - 1], target),
            remote(
                pairs.at[lax.shift_right_logical(c, 1)],
                vv.at[s],
                send.at[1, d - 1],
                recv.at[1, d - 1],
                target,
            ),
        )

    def arriving(d):
        source = 2 * lax.rem(a + 4 - d, 4) + core
        return (
            remote(qk.at[source], qk.at[source], send.at[0, d - 1], recv.at[0, d - 1], (source, z)),
            remote(vv.at[source], vv.at[source], send.at[1, d - 1], recv.at[1, d - 1], (source, z)),
            source,
        )

    def relay(d, frame):
        return (
            remote(qk.at[frame], qk.at[frame], core_send.at[0, d], core_recv.at[0, d], sibling),
            remote(vv.at[frame], vv.at[frame], core_send.at[1, d], core_recv.at[1, d], sibling),
        )

    for d in (2, 1, 3):
        for copy in toward(d):
            copy.start()
    columns_start(padded, grad_full, s, z, z_send, z_recv)
    qk[s] = slabs[a]
    vv[s] = pairs[lax.shift_right_logical(a, 1)]
    for copy in relay(0, s):
        copy.start()
    for d in (1, 3, 2):
        first, second, source = arriving(d)
        first.wait_recv()
        second.wait_recv()
        for copy in relay(d, source):
            copy.start()
    for d in range(4):
        frame = 2 * lax.rem(a + 4 - d, 4) + 1 - core
        for copy in relay(d, frame):
            copy.wait_recv()
    swap = swap_halves()

    def turn(f, carry):
        ks[pl.ds(pl.multiple_of(f * RP, 16), RP), :] = dot(qk[f], swap).astype(BF)
        return carry

    lax.fori_loop(0, 8, turn, 0)
    low_half = lane_head(RP, 2 * HD) == 0

    def attend(i, carry):
        f = 2 * i + core
        qf = jnp.where(low_half, qk[f].astype(F32), 0.0).astype(BF)
        scores = dot_cols(qf, ks[...]) + bias[pl.ds(f, 1), :]
        peak = jnp.max(scores, axis=1, keepdims=True)
        expo = jnp.exp(scores - peak)
        total = jnp.sum(expo, axis=1, keepdims=True)
        product = dot(expo.astype(BF), vv[...].reshape(8 * RP, 2 * HD))
        outs[i] = (product * (1.0 / total)).astype(BF)
        lse[i] = jnp.broadcast_to(peak + jnp.log(total), (RP, 2 * HD))
        return carry

    lax.fori_loop(0, 4, attend, 0)

    def back(d):
        target = lax.rem(a + d, 4)
        return remote(
            outs.at[target], ins.at[a], back_send.at[d - 1], back_recv.at[d - 1], (2 * target + core, z)
        )

    for d in (2, 1, 3):
        back(d).start()
    ins[a] = outs[a]
    for d in (1, 3, 2):
        source = lax.rem(a + 4 - d, 4)
        remote(
            ins.at[source], ins.at[source], back_send.at[d - 1], back_recv.at[d - 1], (2 * source + core, z)
        ).wait_recv()
    for p in range(2):
        att[:, 128 * p : 128 * p + 128] = jnp.where(
            low_half, ins[2 * p].astype(F32), ins[2 * p + 1].astype(F32)
        ).astype(BF)
    columns_wait(padded, grad_full, s, z, z_send, z_recv)
    for d in (1, 2, 3):
        for copy in toward(d):
            copy.wait_send()
        back(d).wait_send()
    for copy in relay(0, s):
        copy.wait_send()
    for d in (1, 2, 3):
        for copy in relay(d, 2 * lax.rem(a + 4 - d, 4) + core):
            copy.wait_send()


def middle_kernel(
    att1,
    x2,
    grad_full,
    params,
    w_out,
    w_up,
    w_down,
    out_rows,
    g_out,
    x3,
    br1,
    dbr1,
    datt1,
    d_up,
    d_down,
    sums,
    part,
    part_out,
    inbox,
    m1,
    act,
    slope,
    dmlp,
    dpre,
    final,
    wo,
    wu,
    wd,
    fetch_sem,
    send,
    recv,
):
    s, z = lax.axis_index("seq"), lax.axis_index("mp")
    copies = fetch((w_out.at[1], w_up.at[1], w_down.at[1]), (wo, wu, wd), fetch_sem)
    for copy in copies:
        copy.start()
    valid = own_valid(z)
    copies[0].wait()
    times(att1, wo, part)
    greet(line(s, z))
    scatter_start(part, inbox.at[0], s, z, send.at[0], recv.at[0])
    dmlp[...] = (grad_full[...].astype(F32) * params[11:12]).astype(BF)
    branch = scatter_wait(part, inbox.at[0], s, z, send.at[0], recv.at[0])
    br1[...] = branch
    mid = x2[...] + params[10:11] * branch
    x3[...] = mid
    put_own(m1, z, apply_norm(mid, params, 1, 1))
    gather_start(m1, s, z, send.at[1], recv.at[1])
    copies[1].wait()
    copies[2].wait()
    gather_wait(m1, s, z, send.at[1], recv.at[1])
    up_gelu(m1, wu, act, slope)
    mlp_back(dmlp, wd, slope, dpre)
    times_turned(dpre, wu, part)
    scatter_start(part, inbox.at[1], s, z, send.at[2], recv.at[2])
    times(act, wd, part_out)
    scatter_start(part_out, inbox.at[2], s, z, send.at[3], recv.at[3])
    weight_grad(act, dmlp, d_down)
    weight_grad(m1, dpre, d_up)
    g = jnp.where(valid, grad_full[own_rows(z)].astype(F32), 0.0)
    dnorm = scatter_wait(part, inbox.at[1], s, z, send.at[2], recv.at[2])
    dv, gain, bias = norm_back(dnorm, x3[...], params[3:4], valid)
    sums[0:1] = gain
    sums[1:2] = bias
    after = jnp.where(valid, g + dv, 0.0)
    g_out[...] = after
    put_own(dbr1, z, (after * params[10:11]).astype(BF))
    gather_start(dbr1, s, z, send.at[4], recv.at[4])
    sums[2:3] = jnp.sum(jnp.where(valid, after * br1[...], 0.0), axis=0, keepdims=True)
    out_branch = scatter_wait(part_out, inbox.at[2], s, z, send.at[3], recv.at[3])
    sums[3:4] = jnp.sum(jnp.where(valid, g * out_branch, 0.0), axis=0, keepdims=True)
    sums[4:8] = jnp.zeros((4, sums.shape[1]), F32)
    final[...] = (x3[...] + params[11:12] * out_branch).astype(BF)
    gather_wait(dbr1, s, z, send.at[4], recv.at[4])
    features_start(final, out_rows, s, z, send.at[5], recv.at[5])
    datt1[...] = dot_cols(dbr1[...], wo[...]).astype(BF)
    features_wait(final, out_rows, s, z, send.at[5], recv.at[5])


def global_backward_kernel(
    datt,
    att,
    dbr,
    qk,
    vv,
    ks,
    lse,
    bias,
    dq_out,
    dk_out,
    dv_out,
    d_out,
    pairs,
    dos,
    dkt,
    dvt,
    dq_mine,
    dk_sum,
    dv_sum,
    dkv_send,
    dkv_in,
    ready,
    dqk_in,
    dv_in,
    send,
    recv,
    core_send,
    core_recv,
    back_send,
    back_recv,
):
    s, z = lax.axis_index("seq"), lax.axis_index("mp")
    a, core = chips(s)
    sibling = (2 * a + 1 - core, z)
    for p in range(2):
        pairs[p] = datt[:, 128 * p : 128 * p + 128]
    greet(global_peers(s, z) + [sibling])

    def toward(d):
        c = lax.rem(a + d, 4)
        return remote(
            pairs.at[lax.shift_right_logical(c, 1)],
            dos.at[a],
            send.at[d - 1],
            recv.at[d - 1],
            (2 * c + core, z),
        )

    for d in (2, 1, 3):
        toward(d).start()
    dos[a] = pairs[lax.shift_right_logical(a, 1)]
    d_out[...] = dot_rows(att[...], dbr[...]).astype(BF)
    dkt[...] = jnp.zeros_like(dkt)
    dvt[...] = jnp.zeros_like(dvt)
    for d in (1, 3, 2):
        source = lax.rem(a + 4 - d, 4)
        remote(
            dos.at[source], dos.at[source], send.at[d - 1], recv.at[d - 1], (2 * source + core, z)
        ).wait_recv()
    half = lane_head(RP, 2 * HD)
    low_half = half == 0
    mine = half == lax.rem(a, 2)

    def step(i, carry):
        f = 2 * i + core
        qf = jnp.where(low_half, qk[f].astype(F32), 0.0).astype(BF)
        do = jnp.where(mine, dos[i].astype(F32), 0.0).astype(BF)
        scores = dot_cols(qf, ks[...]) + bias[pl.ds(f, 1), :]
        probs = jnp.exp(scores - lse[i][:, 0:1])
        dprobs = dot_cols(do, vv[...].reshape(8 * RP, 2 * HD))
        delta = jnp.sum(probs * dprobs, axis=1, keepdims=True)
        dscores = (probs * (dprobs - delta)).astype(BF)
        dq_mine[i] = dot(dscores, ks[...])
        dkt[...] += dot_rows(qf, dscores)
        dvt[...] += dot_rows(do, probs.astype(BF))
        return carry

    lax.fori_loop(0, 4, step, 0)
    dk_sum[...] = jnp.transpose(dkt[...])
    dv_sum[...] = jnp.transpose(dvt[...])

    def rows_of(frame):
        return pl.ds(pl.multiple_of(frame * RP, 16), RP)

    for i in range(4):
        theirs = rows_of(2 * i + 1 - core)
        dkv_send[0, i] = dk_sum[theirs, :].astype(BF)
        dkv_send[1, i] = dv_sum[theirs, :].astype(BF)
    across = remote(dkv_send, dkv_in, core_send.at[0], core_recv.at[0], sibling)
    across.start()
    across.wait()
    swap = swap_halves()
    for i in range(4):
        own = rows_of(2 * i + core)
        dk = (dk_sum[own, :] + dkv_in[0, i].astype(F32)).astype(BF)
        dv = dv_sum[own, :] + dkv_in[1, i].astype(F32)
        ready[0, i] = jnp.where(low_half, dq_mine[i], dot(dk, swap)).astype(BF)
        ready[1, i] = dv.astype(BF)

    def back(d):
        target = lax.rem(a + d, 4)
        device = (2 * target + core, z)
        return (
            remote(ready.at[0, target], dqk_in.at[a], back_send.at[0, d - 1], back_recv.at[0, d - 1], device),
            remote(ready.at[1, target], dv_in.at[a], back_send.at[1, d - 1], back_recv.at[1, d - 1], device),
        )

    for d in (2, 1, 3):
        for copy in back(d):
            copy.start()
    dqk_in[a] = ready[0, a]
    dv_in[a] = ready[1, a]
    for d in (1, 3, 2):
        source = lax.rem(a + 4 - d, 4)
        device = (2 * source + core, z)
        for number, box in ((0, dqk_in), (1, dv_in)):
            there = box.at[source]
            remote(
                there, there, back_send.at[number, d - 1], back_recv.at[number, d - 1], device
            ).wait_recv()
    to_q, to_k = place(True, False), place(False, True)
    dq = jnp.zeros((RP, WIDE), F32)
    dk = jnp.zeros((RP, WIDE), F32)
    for c in range(4):
        cols = slice(128 * c, 128 * c + 128)
        dq = dq + dot_cols(dqk_in[c], to_q[:, cols])
        dk = dk + dot_cols(dqk_in[c], to_k[:, cols])
    dq_out[...] = dq
    dk_out[...] = dk
    for p in range(2):
        dv_out[:, 128 * p : 128 * p + 128] = jnp.where(
            low_half, dv_in[2 * p].astype(F32), dv_in[2 * p + 1].astype(F32)
        )
    for d in (1, 2, 3):
        toward(d).wait_send()
        for copy in back(d):
            copy.wait_send()


def attention_back_kernel(
    dq,
    dk,
    dv,
    raw,
    h1,
    x2,
    g_in,
    mo0,
    params,
    head_params,
    w_qkv,
    g_out,
    dm0,
    d_qkv,
    sums,
    head_sums,
    part,
    inbox,
    dproj,
    wq,
    fetch_sem,
    send,
    recv,
):
    s, z = lax.axis_index("seq"), lax.axis_index("mp")
    copies = fetch((w_qkv.at[1],), (wq,), fetch_sem)
    for copy in copies:
        copy.start()
    valid = own_valid(z)
    means = head_means()
    head_sums[...] = jnp.zeros_like(head_sums)
    heads_back(raw, dq[...], dk[...], dv[...], head_params, 1, means, dproj, head_sums)
    copies[0].wait()
    attention_input_back(dproj, wq, part)
    greet(line(s, z))
    scatter_start(part, inbox, s, z, send.at[0], recv.at[0])
    qkv_weight_grad(h1, dproj, d_qkv)
    dnorm = scatter_wait(part, inbox, s, z, send.at[0], recv.at[0])
    dvalue, gain, bias = norm_back(dnorm, x2[...], params[2:3], valid)
    after = jnp.where(valid, g_in[...] + dvalue, 0.0)
    g_out[...] = after
    put_own(dm0, z, (after * params[9:10]).astype(BF))
    gather_start(dm0, s, z, send.at[1], recv.at[1])
    sums[...] = jnp.zeros_like(sums)
    sums[0:1] = gain
    sums[1:2] = bias
    sums[2:3] = jnp.sum(jnp.where(valid, after * mo0[...], 0.0), axis=0, keepdims=True)
    gather_wait(dm0, s, z, send.at[1], recv.at[1])


def mlp_back_kernel(
    dm0,
    act,
    slope,
    m0,
    x1,
    g_in,
    br0,
    params,
    w_up,
    w_down,
    g_out,
    dbr0,
    d_up,
    d_down,
    sums,
    part,
    inbox,
    dpre,
    wu,
    wd,
    fetch_sem,
    send,
    recv,
):
    s, z = lax.axis_index("seq"), lax.axis_index("mp")
    copies = fetch((w_down.at[0], w_up.at[0]), (wd, wu), fetch_sem)
    for copy in copies:
        copy.start()
    valid = own_valid(z)
    copies[0].wait()
    mlp_back(dm0, wd, slope, dpre)
    copies[1].wait()
    times_turned(dpre, wu, part)
    greet(line(s, z))
    scatter_start(part, inbox, s, z, send.at[0], recv.at[0])
    weight_grad(act, dm0, d_down)
    weight_grad(m0, dpre, d_up)
    dnorm = scatter_wait(part, inbox, s, z, send.at[0], recv.at[0])
    dvalue, gain, bias = norm_back(dnorm, x1[...], params[1:2], valid)
    after = jnp.where(valid, g_in[...] + dvalue, 0.0)
    g_out[...] = after
    put_own(dbr0, z, (after * params[8:9]).astype(BF))
    gather_start(dbr0, s, z, send.at[1], recv.at[1])
    sums[...] = jnp.zeros_like(sums)
    sums[0:1] = gain
    sums[1:2] = bias
    sums[2:3] = jnp.sum(jnp.where(valid, after * br0[...], 0.0), axis=0, keepdims=True)
    gather_wait(dbr0, s, z, send.at[1], recv.at[1])


def last_kernel(
    dbr,
    att,
    raw,
    q0,
    k0,
    v0,
    h0,
    x0,
    g_in,
    params,
    head_params,
    sums3,
    sums5,
    sums6,
    head_sums1,
    w_out,
    w_qkv,
    grad_rows,
    d_qkv,
    d_out,
    small,
    part,
    inbox,
    dproj,
    final,
    messages,
    letters,
    head_sums,
    wo,
    wq,
    fetch_sem,
    send,
    recv,
):
    s, z = lax.axis_index("seq"), lax.axis_index("mp")
    copies = fetch((w_out.at[0], w_qkv.at[0]), (wo, wq), fetch_sem)
    for copy in copies:
        copy.start()
    valid = own_valid(z)
    means = head_means()
    head_sums[...] = jnp.zeros_like(head_sums)
    copies[0].wait()
    datt = dot_cols(dbr[...], wo[...]).astype(BF).astype(F32)
    heads = lane_head(RP)
    keep = key_valid()
    queries = q0[...].astype(F32)
    dq = jnp.zeros((RP, WIDE), F32)
    dk = jnp.zeros((RP, WIDE), F32)
    dv = jnp.zeros((RP, WIDE), F32)
    for h in range(WIDE // HD):
        here = heads == h
        qh = jnp.where(here, queries, 0.0).astype(BF)
        do = jnp.where(here, datt, 0.0).astype(BF)
        scores = jnp.where(keep, dot_cols(qh, k0[...]), NEG)
        expo = jnp.exp(scores - jnp.max(scores, axis=1, keepdims=True))
        probs = expo * (1.0 / jnp.sum(expo, axis=1, keepdims=True))
        dprobs = dot_cols(do, v0[...])
        delta = jnp.sum(probs * dprobs, axis=1, keepdims=True)
        dscores = (probs * (dprobs - delta)).astype(BF)
        dq = jnp.where(here, dot(dscores, k0[...]), dq)
        dk = dk + dot_rows(dscores, qh)
        dv = dv + dot_rows(probs.astype(BF), do)
    heads_back(raw, dq, dk, dv, head_params, 0, means, dproj, head_sums)
    copies[1].wait()
    attention_input_back(dproj, wq, part)
    greet(line(s, z))
    scatter_start(part, inbox, s, z, send.at[0], recv.at[0])
    qkv_weight_grad(h0, dproj, d_qkv)
    d_out[...] = dot_rows(att[...], dbr[...]).astype(BF)
    dnorm = scatter_wait(part, inbox, s, z, send.at[0], recv.at[0])
    dvalue, gain, bias = norm_back(dnorm, x0[...], params[0:1], valid)
    final[...] = jnp.where(valid, g_in[...] + dvalue, 0.0)
    features_start(final, grad_rows, s, z, send.at[1], recv.at[1])
    rows = (
        gain,
        sums6[0:1],
        sums5[0:1],
        sums3[0:1],
        bias,
        sums5[1:2],
        sums6[1:2],
        sums3[1:2],
        sums6[2:3],
        sums5[2:3],
        sums3[2:3],
        sums3[3:4],
    )
    for p in range(NZ):
        cols = slice(WIDE * p, WIDE * p + WIDE)
        for number, row in enumerate(rows):
            messages[p, number : number + 1] = row[:, cols]
        messages[p, 12:16] = jnp.zeros((4, WIDE), F32)
        messages[p, 16:20] = head_sums[0:4]
        messages[p, 20:24] = head_sums1[0:4]

    def note(d):
        peer = lax.rem(z + d, NZ)
        return remote(messages.at[peer], letters.at[d - 1], send.at[2, d - 1], recv.at[2, d - 1], (s, peer))

    for d in range(1, NZ):
        note(d).start()
    for d in range(1, NZ):
        note(d).wait()
    small[...] = messages[z] + letters[0] + letters[1] + letters[2]
    features_wait(final, grad_rows, s, z, send.at[1], recv.at[1])


def frame_scores(query_rows, key_rows, allowed):
    scores = jnp.einsum("qhd,khd->hqk", query_rows, key_rows, preferred_element_type=F32)
    return jnp.where(allowed[None, None, :], scores, NEG)


def gather_frames(rows):
    return lax.all_gather(rows, "seq", axis=0)


def global_forward_plain(query_rows, key_rows, value_rows, allowed_frames):
    head_count = query_rows.shape[1]
    state = (
        jnp.full((head_count, TOK), NEG, F32),
        jnp.zeros((head_count, TOK), F32),
        jnp.zeros((head_count, TOK, HD), F32),
    )

    def advance(running, item):
        key_block, value_block, allowed = item

        def update(current):
            peak, totals, weighted = current
            scores = jnp.einsum("qhd,khd->hqk", query_rows, key_block, preferred_element_type=F32)
            new_peak = jnp.maximum(peak, jnp.max(scores, axis=-1))
            expo = jnp.exp(scores - new_peak[..., None])
            factor = jnp.exp(peak - new_peak)
            totals = totals * factor + jnp.sum(expo, axis=-1)
            weighted = weighted * factor[..., None] + jnp.einsum(
                "hqk,khd->hqd", expo.astype(BF), value_block, preferred_element_type=F32
            )
            return (new_peak, totals, weighted)

        return (lax.cond(allowed, update, lambda current: current, running), None)

    (peak, totals, weighted), _ = lax.scan(
        advance, state, (gather_frames(key_rows), gather_frames(value_rows), allowed_frames)
    )
    attended = jnp.transpose(weighted / totals[..., None], (1, 0, 2))
    return attended, peak + jnp.log(totals)


def global_backward_plain(query_rows, key_rows, value_rows, out_grad, attended, lse, allowed_frames):
    delta = jnp.transpose(jnp.sum(attended * out_grad.astype(F32), axis=-1))
    zero = jnp.zeros(query_rows.shape, F32)

    def pieces(q, do, stat, row_sum, k, v):
        scores = jnp.einsum("qhd,khd->hqk", q, k, preferred_element_type=F32)
        probs = jnp.exp(scores - stat[..., None])
        dprobs = jnp.einsum("qhd,khd->hqk", do, v, preferred_element_type=F32)
        return probs.astype(BF), (probs * (dprobs - row_sum[..., None])).astype(BF)

    def advance_query(total, item):
        k, v, allowed = item

        def update(current):
            _, dscores = pieces(query_rows, out_grad, lse, delta, k, v)
            return current + jnp.einsum("hqk,khd->qhd", dscores, k, preferred_element_type=F32)

        return (lax.cond(allowed, update, lambda current: current, total), None)

    dq, _ = lax.scan(
        advance_query, zero, (gather_frames(key_rows), gather_frames(value_rows), allowed_frames)
    )

    def advance_keys(totals, item):
        q, do, stat, row_sum, allowed = item

        def update(current):
            probs, dscores = pieces(q, do, stat, row_sum, key_rows, value_rows)
            return (
                current[0] + jnp.einsum("hqk,qhd->khd", dscores, q, preferred_element_type=F32),
                current[1] + jnp.einsum("hqk,qhd->khd", probs, do, preferred_element_type=F32),
            )

        return (lax.cond(allowed, update, lambda current: current, totals), None)

    (dk, dv), _ = lax.scan(
        advance_keys,
        (zero, zero),
        (
            gather_frames(query_rows),
            gather_frames(out_grad),
            gather_frames(lse),
            gather_frames(delta),
            allowed_frames,
        ),
    )
    return dq, dk, dv


def call(name, body, ins, in_hbm, outs, scratch, collective_id, vmem_mib):
    return pl.pallas_call(
        body,
        name=name,
        out_shape=[jax.ShapeDtypeStruct(shape, kind) for shape, kind in outs],
        in_specs=[
            pl.BlockSpec(memory_space=pl.ANY if where in in_hbm else pltpu.VMEM)
            for where in range(len(ins))
        ],
        out_specs=[pl.BlockSpec(memory_space=pltpu.VMEM)] * len(outs),
        scratch_shapes=scratch,
        compiler_params=pltpu.CompilerParams(
            collective_id=collective_id, has_side_effects=True, vmem_limit_bytes=vmem_mib * 2**20
        ),
    )(*ins)


def dma_sems(*shape):
    return pltpu.SemaphoreType.DMA(shape)


def per_device(
    tokens,
    grad_out,
    frame_counts,
    slot_frames,
    block_norm_multiplier,
    block_norm_bias,
    qk_gain,
    qk_bias,
    w_qkv,
    w_out,
    w_up,
    w_down,
    layer_scale,
):
    seq_count = lax.axis_size("seq")
    depth = w_qkv.shape[2]
    hidden = w_up.shape[2]
    heads_here = WIDE // HD
    frame_total = slot_frames.shape[0]
    frame_ids = jnp.arange(frame_total, dtype=jnp.int32)
    scene_ends = jnp.cumsum(frame_counts)
    scene_of_frame = jnp.sum((scene_ends[None, :] <= frame_ids[:, None]).astype(jnp.int32), axis=1)
    scene_table = jnp.sum(
        jnp.where(slot_frames[:, None] == frame_ids[None, :], scene_of_frame[None, :], 0), axis=1
    )
    params = jnp.concatenate(
        [
            block_norm_multiplier.reshape(4, WIDE),
            block_norm_bias.reshape(4, WIDE),
            layer_scale.reshape(4, WIDE),
            jnp.zeros((4, WIDE), F32),
        ]
    )
    head_params = jnp.tile(jnp.concatenate([qk_gain.reshape(4, HD), qk_bias.reshape(4, HD)]), (1, heads_here))

    rows_d = ((RP, depth), BF)
    own_d = ((RO, depth), F32)
    rows_w = ((RP, WIDE), BF)
    raw_pair = ((2, RP, WIDE), F32)
    scratch_inbox = (NZ - 1, RO, depth)
    (
        params_full,
        x0,
        h0,
        raw0,
        q0,
        k0,
        v0,
        att0,
        x1,
        br0,
        m0,
        act0,
        slope0,
        mo0,
        x2,
        h1,
        raw1,
        q1,
        k1,
        v1,
    ) = call(
        "first",
        first_kernel,
        (tokens, params, head_params, w_qkv, w_out, w_up, w_down),
        (3, 4, 5, 6),
        [
            ((16, depth), F32),
            own_d,
            rows_d,
            raw_pair,
            rows_w,
            rows_w,
            rows_w,
            rows_w,
            own_d,
            own_d,
            rows_d,
            ((RP, hidden), BF),
            ((RP, hidden), F32),
            own_d,
            own_d,
            rows_d,
            raw_pair,
            rows_w,
            rows_w,
            rows_w,
        ],
        [
            pltpu.VMEM((RP, WIDE), BF),
            pltpu.VMEM((RP, depth), BF),
            pltpu.VMEM((RP, depth), BF),
            pltpu.VMEM((2,) + scratch_inbox, BF),
            pltpu.VMEM((3, depth, WIDE), BF),
            pltpu.VMEM((3, depth, WIDE), BF),
            pltpu.VMEM((WIDE, depth), BF),
            pltpu.VMEM((depth, hidden), BF),
            pltpu.VMEM((hidden, depth), BF),
            dma_sems(5),
            dma_sems(6, 3),
            dma_sems(6, 3),
        ],
        0,
        40,
    )

    fast = seq_count == 8
    same_scene = scene_table[:, None] == scene_table[None, :]
    if fast:
        key_rows_ok = jnp.arange(RP, dtype=jnp.int32) < TOK
        bias = jnp.where(same_scene[:, :, None] & key_rows_ok[None, None, :], 0.0, NEG)
        bias = bias.astype(F32).reshape(frame_total, frame_total * RP)
        slab = (RP, 2 * HD)
        qk, vv, ks, lse, att1, grad_full = call(
            "global_forward",
            global_forward_kernel,
            (q1, k1, v1, grad_out, bias),
            (),
            [
                ((8,) + slab, BF),
                ((8,) + slab, BF),
                ((8 * RP, 2 * HD), BF),
                ((4,) + slab, F32),
                rows_w,
                rows_d,
            ],
            [
                pltpu.VMEM((4,) + slab, BF),
                pltpu.VMEM((2,) + slab, BF),
                pltpu.VMEM((4,) + slab, BF),
                pltpu.VMEM((4,) + slab, BF),
                pltpu.VMEM((RP, WIDE), BF),
                dma_sems(2, 3),
                dma_sems(2, 3),
                dma_sems(2, 4),
                dma_sems(2, 4),
                dma_sems(3),
                dma_sems(3),
                dma_sems(3),
                dma_sems(3),
            ],
            1,
            40,
        )
    else:
        allowed = same_scene[lax.axis_index("seq")]

        def plain(rows):
            return rows[:TOK].reshape(TOK, heads_here, HD)

        def padded(rows):
            return jnp.pad(rows.reshape(TOK, -1), ((0, RP - TOK), (0, 0)))

        attended, lse = global_forward_plain(plain(q1), plain(k1), plain(v1), allowed)
        att1 = padded(attended.astype(BF))
        grad_full = padded(lax.all_gather(grad_out, "mp", axis=1, tiled=True))

    out_rows, g3, x3, br1, dbr1, datt1, d_up1, d_down1, sums3 = call(
        "middle",
        middle_kernel,
        (att1, x2, grad_full, params_full, w_out, w_up, w_down),
        (4, 5, 6),
        [
            rows_w,
            own_d,
            own_d,
            own_d,
            rows_d,
            rows_w,
            ((depth, hidden), BF),
            ((hidden, depth), BF),
            ((8, depth), F32),
        ],
        [
            pltpu.VMEM((RP, depth), BF),
            pltpu.VMEM((RP, depth), BF),
            pltpu.VMEM((3,) + scratch_inbox, BF),
            pltpu.VMEM((RP, depth), BF),
            pltpu.VMEM((RP, hidden), BF),
            pltpu.VMEM((RP, hidden), F32),
            pltpu.VMEM((RP, depth), BF),
            pltpu.VMEM((RP, hidden), BF),
            pltpu.VMEM((RO, depth), BF),
            pltpu.VMEM((WIDE, depth), BF),
            pltpu.VMEM((depth, hidden), BF),
            pltpu.VMEM((hidden, depth), BF),
            dma_sems(3),
            dma_sems(6, 3),
            dma_sems(6, 3),
        ],
        2,
        40,
    )
    d_up1 = lax.psum_scatter(d_up1, "seq", scatter_dimension=0, tiled=True)
    d_down1 = lax.psum_scatter(d_down1, "seq", scatter_dimension=1, tiled=True)

    if fast:
        dq, dk, dv, d_out1 = call(
            "global_backward",
            global_backward_kernel,
            (datt1, att1, dbr1, qk, vv, ks, lse, bias),
            (),
            [((RP, WIDE), F32)] * 3 + [((WIDE, depth), BF)],
            [
                pltpu.VMEM((2,) + slab, BF),
                pltpu.VMEM((4,) + slab, BF),
                pltpu.VMEM((2 * HD, 8 * RP), F32),
                pltpu.VMEM((2 * HD, 8 * RP), F32),
                pltpu.VMEM((4,) + slab, F32),
                pltpu.VMEM((8 * RP, 2 * HD), F32),
                pltpu.VMEM((8 * RP, 2 * HD), F32),
                pltpu.VMEM((2, 4) + slab, BF),
                pltpu.VMEM((2, 4) + slab, BF),
                pltpu.VMEM((2, 4) + slab, BF),
                pltpu.VMEM((4,) + slab, BF),
                pltpu.VMEM((4,) + slab, BF),
                dma_sems(3),
                dma_sems(3),
                dma_sems(1),
                dma_sems(1),
                dma_sems(2, 3),
                dma_sems(2, 3),
            ],
            3,
            40,
        )
    else:
        dq, dk, dv = (
            padded(part)
            for part in global_backward_plain(
                plain(q1), plain(k1), plain(v1), plain(datt1), attended, lse, allowed
            )
        )
        d_out1 = lax.dot_general(att1, dbr1, (((0,), (0,)), ((), ())), preferred_element_type=F32).astype(BF)

    g5, dm0, d_qkv1, sums5, head_sums1 = call(
        "attention_back",
        attention_back_kernel,
        (dq, dk, dv, raw1, h1, x2, g3, mo0, params_full, head_params, w_qkv),
        (10,),
        [own_d, rows_d, ((3, depth, WIDE), BF), ((8, depth), F32), ((8, WIDE), F32)],
        [
            pltpu.VMEM((RP, depth), BF),
            pltpu.VMEM(scratch_inbox, BF),
            pltpu.VMEM((3, RP, WIDE), BF),
            pltpu.VMEM((3, depth, WIDE), BF),
            dma_sems(1),
            dma_sems(2, 3),
            dma_sems(2, 3),
        ],
        4,
        40,
    )
    d_qkv1 = lax.psum_scatter(d_qkv1, "seq", scatter_dimension=1, tiled=True)
    d_out1 = lax.psum_scatter(d_out1, "seq", scatter_dimension=1, tiled=True)

    g6, dbr0, d_up0, d_down0, sums6 = call(
        "mlp_back",
        mlp_back_kernel,
        (dm0, act0, slope0, m0, x1, g5, br0, params_full, w_up, w_down),
        (8, 9),
        [own_d, rows_d, ((depth, hidden), BF), ((hidden, depth), BF), ((8, depth), F32)],
        [
            pltpu.VMEM((RP, depth), BF),
            pltpu.VMEM(scratch_inbox, BF),
            pltpu.VMEM((RP, hidden), BF),
            pltpu.VMEM((depth, hidden), BF),
            pltpu.VMEM((hidden, depth), BF),
            dma_sems(2),
            dma_sems(2, 3),
            dma_sems(2, 3),
        ],
        5,
        40,
    )
    d_up0 = lax.psum_scatter(d_up0, "seq", scatter_dimension=0, tiled=True)
    d_down0 = lax.psum_scatter(d_down0, "seq", scatter_dimension=1, tiled=True)

    grad_rows, d_qkv0, d_out0, small = call(
        "last",
        last_kernel,
        (
            dbr0,
            att0,
            raw0,
            q0,
            k0,
            v0,
            h0,
            x0,
            g6,
            params_full,
            head_params,
            sums3,
            sums5,
            sums6,
            head_sums1,
            w_out,
            w_qkv,
        ),
        (15, 16),
        [((RP, WIDE), F32), ((3, depth, WIDE), BF), ((WIDE, depth), BF), ((24, WIDE), F32)],
        [
            pltpu.VMEM((RP, depth), BF),
            pltpu.VMEM(scratch_inbox, BF),
            pltpu.VMEM((3, RP, WIDE), BF),
            pltpu.VMEM((RO, depth), F32),
            pltpu.VMEM((NZ, 24, WIDE), F32),
            pltpu.VMEM((NZ - 1, 24, WIDE), F32),
            pltpu.VMEM((8, WIDE), F32),
            pltpu.VMEM((WIDE, depth), BF),
            pltpu.VMEM((3, depth, WIDE), BF),
            dma_sems(2),
            dma_sems(3, 3),
            dma_sems(3, 3),
        ],
        6,
        40,
    )
    d_qkv0 = lax.psum_scatter(d_qkv0, "seq", scatter_dimension=1, tiled=True)
    d_out0 = lax.psum_scatter(d_out0, "seq", scatter_dimension=1, tiled=True)
    small = lax.psum(small, "seq")
    head_grads = small[16:24].reshape(2, 2, 2, heads_here, HD).sum(axis=3)

    def both(first, second):
        return jnp.stack([first, second]).astype(F32)

    return (
        out_rows[:TOK],
        grad_rows[:TOK],
        small[0:4].reshape(2, 2, WIDE),
        small[4:6],
        small[6:8],
        head_grads[:, 0],
        head_grads[:, 1],
        both(d_qkv0, d_qkv1),
        both(d_out0, d_out1),
        both(d_up0, d_up1),
        both(d_down0, d_down1),
        small[8:12].reshape(2, 2, WIDE),
    )


def solution(mesh):
    in_specs = (
        P("seq", "mp"),
        P("seq", "mp"),
        P(),
        P(),
        P(None, None, "mp"),
        P(None, None, "mp"),
        P(),
        P(),
        P(None, None, None, "mp"),
        P(None, "mp", None),
        P(None, None, "mp"),
        P(None, "mp", None),
        P(None, None, "mp"),
    )
    out_specs = (
        P("seq", "mp"),
        P("seq", "mp"),
        P(None, None, "mp"),
        P(None, "mp"),
        P(None, "mp"),
        P(),
        P(),
        P(None, None, "seq", "mp"),
        P(None, "mp", "seq"),
        P(None, "seq", "mp"),
        P(None, "mp", "seq"),
        P(None, None, "mp"),
    )
    return jax.shard_map(
        per_device, mesh=mesh, in_specs=in_specs, out_specs=out_specs, check_vma=False
    )
```

```python
from functools import partial

import jax
import jax.numpy as jnp
from jax import lax
from jax.experimental import pallas as pl
from jax.experimental.pallas import tpu as pltpu
from jax.sharding import PartitionSpec as P

HD = 64
TOK = 261
EPS = 1e-06
NEG = -1e30

RP = 272
CH = 64
RO = 80
NZ = 4
WIDE = 256
F32 = jnp.float32
BF = jnp.bfloat16
MESH = pl.DeviceIdType.MESH
HIGH = lax.Precision.HIGHEST


def dot(left, right):
    return jnp.dot(left, right, preferred_element_type=F32)


def dot_cols(left, right):
    return lax.dot_general(left, right, (((1,), (1,)), ((), ())), preferred_element_type=F32)


def dot_rows(left, right):
    return lax.dot_general(left, right, (((0,), (0,)), ((), ())), preferred_element_type=F32)


def tile(index, width=WIDE):
    return pl.ds(pl.multiple_of(index * width, width), width)


def standardize(x):
    mean = jnp.mean(x, axis=1, keepdims=True)
    centered = x - mean
    variance = jnp.mean(centered * centered, axis=1, keepdims=True)
    rstd = lax.rsqrt(variance + EPS)
    return centered * rstd, rstd


def norm_back(dnorm, x, multiplier, valid):
    xhat, rstd = standardize(x)
    gain = jnp.sum(jnp.where(valid, dnorm * xhat, 0.0), axis=0, keepdims=True)
    bias = jnp.sum(jnp.where(valid, dnorm, 0.0), axis=0, keepdims=True)
    e = dnorm * multiplier
    dv = rstd * (
        e - jnp.mean(e, axis=1, keepdims=True) - xhat * jnp.mean(e * xhat, axis=1, keepdims=True)
    )
    return dv, gain, bias


def head_means():
    row = lax.broadcasted_iota(jnp.int32, (WIDE, WIDE), 0)
    col = lax.broadcasted_iota(jnp.int32, (WIDE, WIDE), 1)
    same = lax.shift_right_logical(row, 6) == lax.shift_right_logical(col, 6)
    return jnp.where(same, 1.0 / HD, 0.0).astype(BF)


def mean_heads(x, means):
    high = x.astype(BF)
    rest = x - high.astype(F32)
    middle = rest.astype(BF)
    low = (rest - middle.astype(F32)).astype(BF)
    return dot(high, means) + (dot(middle, means) + dot(low, means))


def head_standardize(raw, means):
    centered = raw - mean_heads(raw, means)
    rstd = lax.rsqrt(mean_heads(centered * centered, means) + EPS)
    return centered * rstd, rstd


def head_back(dy, xhat, rstd, gain, means):
    e = dy * gain
    raw = rstd * (e - mean_heads(e, means) - xhat * mean_heads(e * xhat, means))
    return (
        raw,
        jnp.sum(dy * xhat, axis=0, keepdims=True),
        jnp.sum(dy, axis=0, keepdims=True),
    )


def lane_head(rows, width=WIDE):
    return lax.shift_right_logical(lax.broadcasted_iota(jnp.int32, (rows, width), 1), 6)


def key_valid():
    return lax.broadcasted_iota(jnp.int32, (RP, RP), 1) < TOK


def own_valid(z):
    row = lax.broadcasted_iota(jnp.int32, (RO, 1), 0)
    return (row < CH) | ((z == NZ - 1) & (row < TOK - (NZ - 1) * CH))


def remote(src, dst, send, recv, device):
    return pltpu.make_async_remote_copy(
        src_ref=src, dst_ref=dst, send_sem=send, recv_sem=recv, device_id=device, device_id_type=MESH
    )


def greet(devices):
    barrier = pltpu.get_barrier_semaphore()
    for device in devices:
        pl.semaphore_signal(barrier, inc=1, device_id=device, device_id_type=MESH)
    pl.semaphore_wait(barrier, len(devices))


def line(s, z):
    return [(s, lax.rem(z + d, NZ)) for d in range(1, NZ)]


def sized(last, act):
    pl.when(last)(lambda: act(RO))
    pl.when(jnp.logical_not(last))(lambda: act(CH))


def block(z, rows):
    return pl.ds(pl.multiple_of(z * CH, CH), rows)


def own_rows(z):
    return pl.ds(pl.multiple_of(z * CH, CH), RO)


def put_own(full, z, value):
    full[block(z, CH)] = value[:CH]

    @pl.when(z == NZ - 1)
    def _():
        full[pl.ds(NZ * CH, RO - CH)] = value[CH:]


class Line:
    def __init__(self, z):
        self.z = z
        self.near = lax.bitwise_xor(z, 1)
        self.is_end = (z == 0) | (z == NZ - 1)
        self.is_middle = jnp.logical_not(self.is_end)
        self.other_middle = jnp.where(z < 2, 2, 1)
        self.other_end = jnp.where(z < 2, 3, 0)


def by_rows(full):
    def view(owner, act):
        sized(owner == NZ - 1, lambda rows: act(full.at[block(owner, rows)]))

    return view


def by_columns(full):
    def view(owner, act):
        act(full.at[:, tile(owner)])

    return view


class Gather:
    def __init__(self, view, s, z, send, recv):
        self.view, self.s, self.line = view, s, Line(z)
        self.send, self.recv = send, recv

    def copy(self, ref, sent, arrived, target):
        return remote(ref, ref, self.send.at[sent], self.recv.at[arrived], (self.s, target))

    def own(self, sent, arrived, target, act):
        self.view(self.line.z, lambda ref: act(self.copy(ref, sent, arrived, target)))

    def start(self):
        line = self.line

        @pl.when(line.is_end)
        def _():
            self.own(1, 2, line.other_middle, lambda copy: copy.start())

        self.own(0, 0, line.near, lambda copy: copy.start())

        @pl.when(line.is_middle)
        def _():
            self.own(1, 1, line.other_middle, lambda copy: copy.start())
            self.own(2, 1, line.other_end, lambda copy: copy.start())

    def sent(self):
        line = self.line
        self.own(0, 0, line.near, lambda copy: copy.wait_send())
        self.own(1, 1, line.other_middle, lambda copy: copy.wait_send())

        @pl.when(line.is_middle)
        def _():
            self.own(2, 1, line.other_end, lambda copy: copy.wait_send())

    def arrive(self, number, owner):
        self.view(owner, lambda ref: self.copy(ref, 0, number, self.line.near).wait_recv())

    def take_and_pass(self):
        line = self.line
        self.arrive(2, line.other_end)
        self.view(line.other_end, lambda ref: self.copy(ref, 3, 2, line.near).start())

    def passed_on(self):
        line = self.line

        @pl.when(line.is_middle)
        def _():
            self.view(line.other_end, lambda ref: self.copy(ref, 3, 2, line.near).wait_send())

    def finish(self):
        line = self.line
        pl.when(line.is_middle)(self.take_and_pass)
        self.arrive(0, line.near)
        self.arrive(1, line.other_middle)
        self.passed_on()
        pl.when(line.is_end)(lambda: self.arrive(2, line.other_end))


class Scatter:
    def __init__(self, part, inbox, s, z, send, recv):
        self.part, self.inbox, self.s, self.line = part, inbox, s, Line(z)
        self.send, self.recv = send, recv

    def copy(self, owner, box, sent, target, act):
        def go(rows):
            act(
                remote(
                    self.part.at[block(owner, rows)],
                    self.inbox.at[box, pl.ds(0, rows)],
                    self.send.at[sent],
                    self.recv.at[box],
                    (self.s, target),
                )
            )

        sized(owner == NZ - 1, go)

    def direct(self, act):
        line = self.line

        @pl.when(line.is_end)
        def _():
            self.copy(line.other_end, 3, 1, line.near, act)
            self.copy(line.other_middle, 2, 2, line.other_middle, act)

        @pl.when(line.is_middle)
        def _():
            self.copy(line.other_middle, 1, 2, line.other_middle, act)

        self.copy(line.near, 0, 0, line.near, act)

    def start(self):
        self.direct(lambda copy: copy.start())

    def sent(self):
        self.direct(lambda copy: copy.wait_send())

    def across(self, act):
        line = self.line

        def go(rows):
            act(
                remote(
                    self.inbox.at[3, pl.ds(0, rows)],
                    self.inbox.at[1, pl.ds(0, rows)],
                    self.send.at[3],
                    self.recv.at[1],
                    (self.s, line.other_end),
                )
            )

        sized(line.other_end == NZ - 1, go)

    def arrive(self, owner, box):
        self.copy(owner, box, 0, self.line.near, lambda copy: copy.wait_recv())

    def relay(self):
        line = self.line

        @pl.when(line.is_middle)
        def _():
            self.arrive(line.other_end, 3)
            total = self.inbox[3].astype(F32) + self.part[own_rows(line.other_end)].astype(F32)
            self.inbox[3] = total.astype(BF)
            self.across(lambda copy: copy.start())

    def finish(self):
        line = self.line
        total = self.part[own_rows(line.z)].astype(F32)
        for box in (0, 1):
            self.arrive(line.z, box)
            total = total + self.inbox[box].astype(F32)

        @pl.when(line.is_middle)
        def _():
            self.arrive(line.z, 2)
            self.across(lambda copy: copy.wait_send())

        return total + jnp.where(line.is_middle, self.inbox[2].astype(F32), 0.0)


def features_start(rows_ref, full, s, z, send, recv):
    for d in range(1, NZ):
        peer = lax.rem(z + d, NZ)

        def act(rows, d=d, peer=peer):
            remote(
                rows_ref.at[pl.ds(0, rows), tile(peer)],
                full.at[block(z, rows)],
                send.at[d - 1],
                recv.at[d - 1],
                (s, peer),
            ).start()

        sized(z == NZ - 1, act)
    put_own(full, z, rows_ref[:, tile(z)])


def features_wait(rows_ref, full, s, z, send, recv):
    for d in range(1, NZ):
        source = lax.rem(z + NZ - d, NZ)
        peer = lax.rem(z + d, NZ)

        def act_in(rows, d=d, source=source):
            remote(
                rows_ref.at[pl.ds(0, rows), tile(z)],
                full.at[block(source, rows)],
                send.at[d - 1],
                recv.at[d - 1],
                (s, source),
            ).wait_recv()

        def act_out(rows, d=d, peer=peer):
            remote(
                rows_ref.at[pl.ds(0, rows), tile(peer)],
                full.at[block(z, rows)],
                send.at[d - 1],
                recv.at[d - 1],
                (s, peer),
            ).wait_send()

        sized(source == NZ - 1, act_in)
        sized(z == NZ - 1, act_out)


def rows_start(heads_ref, full, s, z, send, recv):
    for d in range(1, NZ):
        peer = lax.rem(z + d, NZ)

        def act(rows, d=d, peer=peer):
            remote(
                heads_ref.at[block(peer, rows)],
                full.at[pl.ds(0, rows), tile(z)],
                send.at[d - 1],
                recv.at[d - 1],
                (s, peer),
            ).start()

        sized(peer == NZ - 1, act)
    full[:, tile(z)] = heads_ref[own_rows(z)]


def rows_wait(heads_ref, full, s, z, send, recv):
    for d in range(1, NZ):
        source = lax.rem(z + NZ - d, NZ)
        peer = lax.rem(z + d, NZ)

        def act_in(rows, d=d, source=source):
            remote(
                heads_ref.at[block(z, rows)],
                full.at[pl.ds(0, rows), tile(source)],
                send.at[d - 1],
                recv.at[d - 1],
                (s, source),
            ).wait_recv()

        def act_out(rows, d=d, peer=peer):
            remote(
                heads_ref.at[block(peer, rows)],
                full.at[pl.ds(0, rows), tile(z)],
                send.at[d - 1],
                recv.at[d - 1],
                (s, peer),
            ).wait_send()

        sized(z == NZ - 1, act_in)
        sized(peer == NZ - 1, act_out)


class Refs:
    WEIGHTS = {"wq": "w_qkv", "wo": "w_out", "wu": "w_up", "wd": "w_down"}

    def __init__(self, names, refs, fast):
        self.__dict__.update(zip(names, refs))
        self.fast = fast
        self.s, self.z = lax.axis_index("seq"), lax.axis_index("mp")
        self.a, self.core = lax.shift_right_logical(self.s, 1), lax.rem(self.s, 2)
        self.sibling = (2 * self.a + 1 - self.core, self.z)
        self.held = {}

    def weight_copy(self, name, b):
        number = list(self.WEIGHTS).index(name)
        source = getattr(self, self.WEIGHTS[name])
        return pltpu.make_async_copy(source.at[b], getattr(self, name), self.fetch_sem.at[number])

    def prefetch(self, name, b):
        self.weight_copy(name, b).start()
        self.held[name] = (b, False)

    def need(self, name, b):
        held, waited = self.held.get(name, (None, False))
        if held != b:
            self.prefetch(name, b)
            waited = False
        if not waited:
            self.weight_copy(name, b).wait()
        self.held[name] = (b, True)
        return getattr(self, name)

    def line_sems(self, number):
        return (self.s, self.z, self.z_send.at[number], self.z_recv.at[number])

    def chip(self, d):
        return lax.rem(self.a + d, 4)

    def chip_device(self, chip):
        return (2 * chip + self.core, self.z)


def project(r, b, hidden, weights, raw, queries, keys, values, rows=pl.ds(0, RP)):
    means = head_means()
    for c in range(3):
        product = dot(hidden[rows, :], weights[c])
        if c == 2:
            values[rows, :] = product.astype(BF)
            continue
        raw[c, rows, :] = product
        xhat, _ = head_standardize(product, means)
        row = 2 * b + c
        normed = xhat * r.head_params[row : row + 1] + r.head_params[4 + row : 5 + row]
        if c == 0:
            queries[rows, :] = (normed * (HD ** (-0.5))).astype(BF)
        else:
            keys[rows, :] = normed.astype(BF)


def share_rows(r, full, at):
    gather = Gather(by_rows(full), *at)
    gather.start()
    gather.sent()
    gather.finish()


def pass_rows(r, full, at, compute, sum_at=None, meanwhile=()):
    gather = Gather(by_rows(full), *at)
    line = gather.line
    scatter = Scatter(r.part, r.inbox.at[0], *sum_at) if sum_at else None
    own_half = jnp.where(line.z < 2, 0, 1)
    gather.start()

    def step(number, carry):
        half = jnp.where(number == 0, own_half, 1 - own_half)
        first, second = number == 0, number == 1

        @pl.when(first)
        def _():
            pl.when(line.is_middle)(gather.take_and_pass)
            gather.arrive(0, line.near)

        @pl.when(second)
        def _():
            gather.arrive(1, line.other_middle)
            pl.when(line.is_end)(lambda: gather.arrive(2, line.other_end))

        pl.when(half == 0)(lambda: compute(pl.ds(0, 2 * CH)))
        pl.when(half == 1)(lambda: compute(pl.ds(2 * CH, RP - 2 * CH)))
        if scatter is not None:

            def send(owner, box, sent, target):
                scatter.copy(owner, box, sent, target, lambda copy: copy.start())

            @pl.when(first)
            def _():
                send(line.near, 0, 0, line.near)

            @pl.when(second & line.is_end)
            def _():
                send(line.other_end, 3, 1, line.near)
                send(line.other_middle, 2, 2, line.other_middle)

            @pl.when(second & line.is_middle)
            def _():
                send(line.other_middle, 1, 2, line.other_middle)

        return carry

    lax.fori_loop(0, 2, step, 0)
    for work in meanwhile[:1]:
        work()
    gather.sent()
    gather.passed_on()
    if scatter is None:
        return None
    scatter.sent()
    scatter.relay()
    for work in meanwhile[1:]:
        work()
    return scatter.finish()


def sum_rows(r, at, meanwhile=(), box=0):
    scatter = Scatter(r.part, r.inbox.at[box], *at)
    scatter.start()
    for work in meanwhile[:1]:
        work()
    scatter.sent()
    scatter.relay()
    for work in meanwhile[1:]:
        work()
    return scatter.finish()


def apply_norm(x, params, b, j):
    xhat, _ = standardize(x)
    row = 2 * b + j
    return (xhat * params[row : row + 1] + params[4 + row : 5 + row]).astype(BF)


ALL_ROWS = pl.ds(0, RP)


def up_gelu(hidden, w_up, act, slope, rows=ALL_ROWS):
    def step(j, carry):
        cols = tile(j)
        pre = dot(hidden[rows, :], w_up[:, cols])
        cdf = 0.5 * (1.0 + lax.erf(pre * (0.5**0.5)))
        act[rows, cols] = (pre * cdf).astype(BF)
        slope[rows, cols] = cdf + pre * jnp.exp(-0.5 * pre * pre) * 0.3989422804014327
        return carry

    lax.fori_loop(0, w_up.shape[1] // WIDE, step, 0)


def times(left, weights, part, rows=ALL_ROWS):
    def step(j, carry):
        cols = tile(j)
        part[rows, cols] = dot(left[rows, :], weights[:, cols]).astype(BF)
        return carry

    lax.fori_loop(0, weights.shape[1] // WIDE, step, 0)


def times_turned(left, weights, part, rows=ALL_ROWS):
    def step(j, carry):
        part[rows, tile(j)] = dot_cols(left[rows, :], weights[tile(j), :]).astype(BF)
        return carry

    lax.fori_loop(0, weights.shape[0] // WIDE, step, 0)


def mlp_back(dmlp, w_down, slope, dpre, rows=ALL_ROWS):
    def step(j, carry):
        cols = tile(j)
        dact = dot_cols(dmlp[rows, :], w_down[cols, :])
        dpre[rows, cols] = (dact * slope[rows, cols]).astype(BF)
        return carry

    lax.fori_loop(0, w_down.shape[0] // WIDE, step, 0)


def attention_input_back(dproj, w_qkv, part):
    def step(j, carry):
        rows = tile(j)
        total = dot_cols(dproj[0], w_qkv[0, rows, :])
        total = total + dot_cols(dproj[1], w_qkv[1, rows, :])
        total = total + dot_cols(dproj[2], w_qkv[2, rows, :])
        part[:, rows] = total.astype(BF)
        return carry

    lax.fori_loop(0, w_qkv.shape[1] // WIDE, step, 0)


def up_grad(r, left, right, out):
    def step(j, carry):
        value = dot_rows(left[:, tile(j)], right[...]).astype(BF)
        if r.fast:
            out[0, j] = value[: WIDE // 2]
            out[1, j] = value[WIDE // 2 :]
        else:
            out[tile(j), :] = value
        return carry

    lax.fori_loop(0, left.shape[1] // WIDE, step, 0)


def down_grad(r, left, right, out):
    def step(j, carry):
        value = dot_rows(left[:, tile(j)], right[...]).astype(BF)
        if r.fast:
            for piece in range(8):
                out[piece % 2, piece // 2, tile(j), :] = value[:, 128 * piece : 128 * piece + 128]
        else:
            out[tile(j), :] = value
        return carry

    lax.fori_loop(0, left.shape[1] // WIDE, step, 0)


def qkv_grad(r, hidden, dproj, out):
    def step(j, carry):
        left = hidden[:, tile(j)]
        for c in range(3):
            value = dot_rows(left, dproj[c]).astype(BF)
            if r.fast:
                out[0, j, c] = value[: WIDE // 2]
                out[1, j, c] = value[WIDE // 2 :]
            else:
                out[c, tile(j), :] = value
        return carry

    lax.fori_loop(0, hidden.shape[1] // WIDE, step, 0)


class SeqSum:
    def __init__(self, r, name, b, number):
        self.r, self.name, self.b = r, name, b
        self.mine = getattr(r, "d_" + name)
        self.first = getattr(r, "first_" + name)
        self.second = getattr(r, "second_" + name).at[b]
        self.sems = (r.sum_send.at[number], r.sum_recv.at[number])

    def across(self):
        r = self.r
        send, recv = self.sems
        return remote(self.mine.at[1 - r.core], self.first, send.at[0], recv.at[0], r.sibling)

    def toward(self, d):
        r = self.r
        send, recv = self.sems
        chip = r.chip(d)
        return remote(
            self.mine.at[r.core, chip], self.second.at[d - 1], send.at[d], recv.at[d], r.chip_device(chip)
        )

    def start(self):
        self.across().start()

    def pass_on(self):
        self.across().wait()
        core = self.r.core
        for chip in range(4):
            total = self.mine[core, chip].astype(F32) + self.first[chip].astype(F32)
            self.mine[core, chip] = total.astype(BF)
        for d in (2, 1, 3):
            self.toward(d).start()

    def finish(self, out):
        for d in (1, 3, 2):
            self.toward(d).wait()
        total = self.mine[self.r.core, self.r.a].astype(F32)
        for d in range(3):
            total = total + self.second[d].astype(F32)
        out[self.b] = total


class WholeOut:
    def __init__(self, r, number):
        self.r = r
        self.full = r.wof
        self.z_sems = r.line_sems(number)
        self.sems = (r.wo_send.at[number - 20], r.wo_recv.at[number - 20])

    def fetch(self, b):
        r = self.r
        part = r.wo_part.shape[0]
        rows = r.w_out.at[b, pl.ds(pl.multiple_of(r.s * part, part), part)]
        return pltpu.make_async_copy(rows, r.wo_part, r.fetch_sem.at[4])

    def line_copy(self, d, source):
        s, z, send, recv = self.z_sems
        owner = lax.rem(z + NZ - d, NZ) if source else z
        device = (s, owner if source else lax.rem(z + d, NZ))
        return remote(self.r.wo_part, self.full.at[owner, s], send.at[d - 1], recv.at[d - 1], device)

    def start(self, b):
        r = self.r
        self.fetch(b).wait()
        self.full[r.z, r.s] = r.wo_part[...]
        for d in range(1, NZ):
            self.line_copy(d, False).start()

    def chip_copy(self, d):
        send, recv = self.sems
        mine = self.full.at[:, self.r.s]
        return remote(mine, mine, send.at[d - 1], recv.at[d - 1], self.r.chip_device(self.r.chip(d)))

    def core_copy(self, d):
        send, recv = self.sems
        held = self.full.at[:, 2 * self.r.chip(4 - d) + self.r.core]
        return remote(held, held, send.at[3 + d], recv.at[3 + d], self.r.sibling)

    def pass_on(self):
        for d in range(1, NZ):
            self.line_copy(d, True).wait_recv()
        for d in (2, 1, 3):
            self.chip_copy(d).start()
        self.core_copy(0).start()
        for d in range(1, NZ):
            self.line_copy(d, False).wait_send()

    def cross(self):
        send, recv = self.sems
        for d in (1, 3, 2):
            there = self.full.at[:, 2 * self.r.chip(4 - d) + self.r.core]
            device = self.r.chip_device(self.r.chip(4 - d))
            remote(there, there, send.at[d - 1], recv.at[d - 1], device).wait_recv()
            self.core_copy(d).start()

    def finish(self):
        send, recv = self.sems
        for d in range(4):
            there = self.full.at[:, 2 * self.r.chip(4 - d) + 1 - self.r.core]
            remote(there, there, send.at[3 + d], recv.at[3 + d], self.r.sibling).wait_recv()
        for d in range(1, 4):
            self.chip_copy(d).wait_send()
        for d in range(4):
            self.core_copy(d).wait_send()


def own_branch(r, rows, out):
    def step(j, carry):
        cols = tile(j)
        out[:, cols] = dot(rows[...], r.wof[:, :, :, cols].reshape(NZ * WIDE, WIDE))
        return carry

    lax.fori_loop(0, r.wof.shape[3] // WIDE, step, 0)


def own_attended_grad(r, value, out):
    for part in range(NZ):
        weights = r.wof[part].reshape(WIDE, r.wof.shape[3])
        out[:, WIDE * part : WIDE * part + WIDE] = dot_cols(value, weights).astype(BF)


def heads_back(r, raw, dq, dk, dv, b, dproj):
    means = head_means()
    row = 2 * b
    for c, dy in ((0, dq * (HD ** (-0.5))), (1, dk)):
        xhat, rstd = head_standardize(raw[c], means)
        gain_row = r.head_params[row + c : row + c + 1]
        draw, gain, bias = head_back(dy, xhat, rstd, gain_row, means)
        dproj[c] = draw.astype(BF)
        r.head_sums[4 * b + c : 4 * b + c + 1] = gain
        r.head_sums[4 * b + 2 + c : 4 * b + 3 + c] = bias
    dproj[2] = dv.astype(BF)


def scale_grad(r, b, j, g, branch):
    valid = own_valid(r.z)
    row = 8 + 2 * b + j
    r.sums[row : row + 1] = jnp.sum(jnp.where(valid, g * branch, 0.0), axis=0, keepdims=True)


def through_norm(r, b, j, x, dnorm, g):
    valid = own_valid(r.z)
    row = 2 * b + j
    dv, gain, bias = norm_back(dnorm, x[...], r.params_full[row : row + 1], valid)
    r.sums[row : row + 1] = gain
    r.sums[4 + 2 * j + b : 5 + 2 * j + b] = bias
    return jnp.where(valid, g + dv, 0.0)


def start_phase(r):
    for name in ("wq", "wo", "wu", "wd"):
        r.prefetch(name, 0)


def put_padded(r, source, full):
    full[pl.ds(CH * NZ, RP - CH * NZ), tile(r.z)] = jnp.zeros((RP - CH * NZ, WIDE), BF)
    full[pl.ds(0, TOK), tile(r.z)] = source[...]


def block_zero_phase(r, whole_out=None):
    s, z = r.s, r.z
    tokens_at, params_at, out_at, mid_at, mlp_at, next_at = (r.line_sems(i) for i in range(6))
    r.params_full[:, tile(z)] = r.params[...]
    put_padded(r, r.tokens, r.every)
    line_params = Gather(by_columns(r.params_full), *params_at)
    line_tokens = Gather(by_columns(r.every), *tokens_at)
    line_params.start()
    line_tokens.start()
    line_tokens.sent()
    line_params.sent()
    line_params.finish()
    line_tokens.finish()
    if r.fast:
        whole_out.start(1)
    params = r.params_full

    r.h0[...] = apply_norm(r.every[...].astype(F32), params, 0, 0)
    r.x0[...] = r.every[own_rows(z)].astype(F32)
    project(r, 0, r.h0, r.need("wq", 0), r.raw0, r.q0, r.k0, r.v0)
    r.prefetch("wq", 1)

    heads = lane_head(RP)
    keep = key_valid()
    queries = r.q0[...].astype(F32)
    attended = jnp.zeros((RP, WIDE), F32)
    for h in range(WIDE // HD):
        qh = jnp.where(heads == h, queries, 0.0).astype(BF)
        scores = jnp.where(keep, dot_cols(qh, r.k0[...]), NEG)
        expo = jnp.exp(scores - jnp.max(scores, axis=1, keepdims=True))
        probs = (expo * (1.0 / jnp.sum(expo, axis=1, keepdims=True))).astype(BF)
        attended = jnp.where(heads == h, dot(probs, r.v0[...]), attended)
    r.att0[...] = attended.astype(BF)

    times(r.att0, r.need("wo", 0), r.part)
    branch = sum_rows(r, out_at)
    if r.fast:
        whole_out.pass_on()
    r.br0[...] = branch
    mid = r.x0[...] + params[8:9] * branch
    r.x1[...] = mid
    put_own(r.m0, z, apply_norm(mid, params, 0, 1))
    w_up, w_down = r.need("wu", 0), r.need("wd", 0)

    def mlp(rows):
        up_gelu(r.m0, w_up, r.act0, r.slope0, rows)
        times(r.act0, w_down, r.part, rows)

    def fetch_next():
        if r.fast:
            r.prefetch("wu", 1)
            r.prefetch("wd", 1)
            whole_out.cross()

    branch = pass_rows(r, r.m0, mid_at, mlp, mlp_at, (fetch_next,))
    r.mo0[...] = branch
    result = r.x1[...] + params[9:10] * branch
    r.x2[...] = result
    put_own(r.h1, z, apply_norm(result, params, 1, 0))
    w_qkv = r.need("wq", 1)
    pass_rows(r, r.h1, next_at, lambda rows: project(r, 1, r.h1, w_qkv, r.raw1, r.q1, r.k1, r.v1, rows))
    if r.fast:
        whole_out.finish()


def place(first):
    row = lax.broadcasted_iota(jnp.int32, (WIDE, 2 * WIDE), 0)
    col = lax.broadcasted_iota(jnp.int32, (WIDE, 2 * WIDE), 1)
    within = lax.bitwise_and(col, 127)
    head = lax.shift_right_logical(col, 7)
    if first:
        return jnp.where((within < HD) & (row == head * HD + within), 1.0, 0.0).astype(BF)
    return jnp.where((within >= HD) & (row == head * HD + within - HD), 1.0, 0.0).astype(BF)


def swap_halves():
    row = lax.broadcasted_iota(jnp.int32, (2 * HD, 2 * HD), 0)
    col = lax.broadcasted_iota(jnp.int32, (2 * HD, 2 * HD), 1)
    return jnp.where(lax.bitwise_and(row + HD, 127) == col, 1.0, 0.0).astype(BF)


def pieces(x):
    high = x.astype(BF).astype(F32)
    middle = (x - high).astype(BF).astype(F32)
    return high, middle, x - high - middle


def key_lanes(r, f):
    count = r.frame_counts.shape[0]
    lane = lax.broadcasted_iota(jnp.int32, (RP, 2 * HD), 1) - HD
    row = lax.broadcasted_iota(jnp.int32, (RP, 2 * HD), 0)
    other_scene = (lane < count) & (lane != r.scenes[f])
    padding = (lane == count) & (row >= TOK)
    numbers = (lane > count) & (lane <= count + 3)
    return jnp.where(other_scene | padding, NEG, jnp.where(numbers, -1.0, 0.0))


def query_lanes(r, f, minus=None):
    count = r.frame_counts.shape[0]
    lane = lax.broadcasted_iota(jnp.int32, (RP, 2 * HD), 1) - HD
    lanes = jnp.where((lane == r.scenes[f]) | (lane == count), 1.0, 0.0)
    if minus is not None:
        for number, piece in enumerate(pieces(minus)):
            lanes = jnp.where(lane == count + 1 + number, piece, lanes)
    return lanes


HALF_ROWS = 144


def pack_heads(x, out):
    lower, upper = dot(x, place(True)), dot(x, place(False))
    for c in range(4):
        lanes = slice(128 * c, 128 * c + 128)
        out[c] = (lower[:HALF_ROWS, lanes] + upper[RP - HALF_ROWS :, lanes]).astype(BF)


def unpack_heads(packed, out):
    lower, upper = place(True), place(False)
    top, bottom = 0.0, 0.0
    for c in range(4):
        lanes = slice(128 * c, 128 * c + 128)
        top = top + dot_cols(packed[c], lower[:, lanes])
        bottom = bottom + dot_cols(packed[c], upper[:, lanes])
    out[pl.ds(0, HALF_ROWS), :] = top.astype(out.dtype)
    out[pl.ds(HALF_ROWS, RP - HALF_ROWS), :] = bottom[2 * HALF_ROWS - RP :].astype(out.dtype)


def pack(x, swap):
    low = lane_head(HALF_ROWS, 2 * HD) == 0
    upper = dot(x[RP - HALF_ROWS :], swap)
    return jnp.where(low, x[:HALF_ROWS].astype(F32), upper).astype(BF)


def unpack(packed, swap, out, lanes=None):
    low = lane_head(HALF_ROWS, 2 * HD) == 0
    top, bottom = packed.astype(F32), dot(packed, swap)
    if lanes is not None:
        top, bottom = jnp.where(low, top, lanes), jnp.where(low, bottom, lanes)
    out[pl.ds(0, HALF_ROWS), :] = top.astype(BF)
    out[pl.ds(HALF_ROWS, RP - HALF_ROWS), :] = bottom[2 * HALF_ROWS - RP :].astype(BF)


def global_forward_phase(r):
    s, z, a, core, sibling = r.s, r.z, r.a, r.core, r.sibling
    qk, vv, ks = r.qk, r.vv, r.ks
    packed = dot(r.q1[...], place(True)) + dot(r.k1[...], place(False))
    for c in range(4):
        r.slabs[c] = packed[:, 128 * c : 128 * c + 128].astype(BF)
    pack_heads(r.v1[...], r.pairs)
    packed_values = r.packed_values

    def toward(d):
        c = r.chip(d)
        target = r.chip_device(c)
        return (
            remote(r.slabs.at[c], qk.at[s], r.f_send.at[0, d - 1], r.f_recv.at[0, d - 1], target),
            remote(r.pairs.at[c], packed_values.at[s], r.f_send.at[1, d - 1], r.f_recv.at[1, d - 1], target),
        )

    def arriving(d):
        source = 2 * r.chip(4 - d) + core
        device = (source, z)
        return (
            remote(qk.at[source], qk.at[source], r.f_send.at[0, d - 1], r.f_recv.at[0, d - 1], device),
            remote(packed_values.at[source], packed_values.at[source], r.f_send.at[1, d - 1], r.f_recv.at[1, d - 1], device),
            source,
        )

    def relay(d, frame):
        return (
            remote(qk.at[frame], qk.at[frame], r.fc_send.at[0, d], r.fc_recv.at[0, d], sibling),
            remote(packed_values.at[frame], packed_values.at[frame], r.fc_send.at[1, d], r.fc_recv.at[1, d], sibling),
        )

    for d in (2, 1, 3):
        for copy in toward(d):
            copy.start()
    put_padded(r, r.grad_out, r.grad_full)
    line_grads = Gather(by_columns(r.grad_full), *r.line_sems(6))
    line_grads.start()
    qk[s] = r.slabs[a]
    packed_values[s] = r.pairs[a]
    for copy in relay(0, s):
        copy.start()
    for d in (1, 3, 2):
        first, second, source = arriving(d)
        first.wait_recv()
        second.wait_recv()
        for copy in relay(d, source):
            copy.start()
    for d in range(4):
        frame = 2 * r.chip(4 - d) + 1 - core
        for copy in relay(d, frame):
            copy.wait_recv()
    line_grads.finish()
    swap = swap_halves()
    low_half = lane_head(RP, 2 * HD) == 0

    lane = lax.broadcasted_iota(jnp.int32, (HALF_ROWS, 2 * HD), 1)
    value_lanes = jnp.where((lane >= HD) & (lane < HD + 3), -1.0, 0.0)

    def turn(f, carry):
        turned = jnp.where(low_half, dot(qk[f], swap), key_lanes(r, f))
        ks[pl.ds(pl.multiple_of(f * RP, 16), RP), :] = turned.astype(BF)
        unpack(packed_values[f], swap, vv.at[f], value_lanes)
        return carry

    lax.fori_loop(0, 8, turn, 0)

    def back(d):
        target = r.chip(d)
        device = r.chip_device(target)
        return remote(r.outs.at[target], r.ins.at[a], r.fb_send.at[d - 1], r.fb_recv.at[d - 1], device)

    def attend(i):
        f = 2 * i + core
        qf = jnp.where(low_half, qk[f].astype(F32), query_lanes(r, f)).astype(BF)
        scores = dot_cols(qf, ks[...])
        peak = jnp.max(scores, axis=1, keepdims=True)
        expo = jnp.exp(scores - peak)
        total = jnp.sum(expo, axis=1, keepdims=True)
        product = dot(expo.astype(BF), vv[...].reshape(8 * RP, 2 * HD))
        attended = product * (1.0 / total)
        r.outs_full[i] = attended
        r.outs[i] = pack(attended.astype(BF), swap)
        r.lse[i] = jnp.broadcast_to(peak + jnp.log(total), (RP, 2 * HD))

    def attend_and_send(d, carry):
        attend(r.chip(d))
        back(d).start()
        return carry

    lax.fori_loop(1, 4, attend_and_send, 0)
    attend(a)
    r.ins[a] = r.outs[a]
    for d in (1, 3, 2):
        source = r.chip(4 - d)
        there = r.ins.at[source]
        remote(there, there, r.fb_send.at[d - 1], r.fb_recv.at[d - 1], r.chip_device(source)).wait_recv()
    unpack_heads(r.ins, r.att1)
    line_grads.sent()
    for d in (1, 2, 3):
        for copy in toward(d):
            copy.wait_send()
        back(d).wait_send()
    for copy in relay(0, s):
        copy.wait_send()
    for d in (1, 2, 3):
        for copy in relay(d, 2 * r.chip(4 - d) + core):
            copy.wait_send()


def middle_phase(r, sums_of=None):
    s, z = r.s, r.z
    params = r.params_full
    out_at, mid_at, dnorm_at, next_at = (r.line_sems(i) for i in (7, 8, 9, 11))
    valid = own_valid(z)
    if r.fast:
        rows_start(r.att1, r.att_in, *out_at)
        r.dmlp[...] = (r.grad_full[...].astype(F32) * params[11:12]).astype(BF)
        rows_wait(r.att1, r.att_in, *out_at)
        own_branch(r, r.att_in, r.br1)
        branch = r.br1[...]
    else:
        w_out = r.need("wo", 1)
        times(r.att1, w_out, r.part)
        r.dmlp[...] = (r.grad_full[...].astype(F32) * params[11:12]).astype(BF)
        branch = sum_rows(r, out_at)
        r.br1[...] = branch
    mid = r.x2[...] + params[10:11] * branch
    r.x3[...] = mid
    put_own(r.m1, z, apply_norm(mid, params, 1, 1))
    w_up, w_down = r.need("wu", 1), r.need("wd", 1)

    def mlp(rows):
        up_gelu(r.m1, w_up, r.act1, r.slope1, rows)
        mlp_back(r.dmlp, w_down, r.slope1, r.dpre, rows)
        times_turned(r.dpre, w_up, r.part, rows)

    def first():
        down_grad(r, r.act1, r.dmlp, r.d_down)
        if r.fast:
            sums_of["down"].start()

    def second():
        up_grad(r, r.m1, r.dpre, r.d_up)
        if r.fast:
            sums_of["up"].start()
            r.prefetch("wu", 0)
            sums_of["down"].pass_on()

    dnorm = pass_rows(r, r.m1, mid_at, mlp, dnorm_at, (first, second))
    g = jnp.where(valid, r.grad_full[own_rows(z)].astype(F32), 0.0)
    after = through_norm(r, 1, 1, r.x3, dnorm, g)
    r.g3[...] = after
    dbranch = (after * params[10:11]).astype(BF)
    put_own(r.dbr1, z, dbranch)
    if r.fast:
        own_attended_grad(r, dbranch, r.datt_own)
        features_start(r.datt_own, r.datt1, *r.line_sems(10))
        Gather(by_rows(r.dbr1), *next_at).start()
    scale_grad(r, 1, 0, after, r.br1[...])
    times(r.act1, w_down, r.part_out)
    if r.fast:
        r.prefetch("wd", 0)
        features_wait(r.datt_own, r.datt1, *r.line_sems(10))
    else:
        share_rows(r, r.dbr1, next_at)
        r.datt1[...] = dot_cols(r.dbr1[...], w_out[...]).astype(BF)
        result_start(r)
        result_relay(r)
        result_end(r)


def result_start(r):
    Scatter(r.part_out, r.inbox.at[1], *r.line_sems(22)).start()


def result_relay(r):
    scatter = Scatter(r.part_out, r.inbox.at[1], *r.line_sems(22))
    scatter.sent()
    scatter.relay()


def result_end(r):
    z = r.z
    rows_at = r.line_sems(12)
    out_branch = Scatter(r.part_out, r.inbox.at[1], *r.line_sems(22)).finish()
    g = jnp.where(own_valid(z), r.grad_full[own_rows(z)].astype(F32), 0.0)
    scale_grad(r, 1, 1, g, out_branch)
    r.final_low[...] = (r.x3[...] + r.params_full[11:12] * out_branch).astype(BF)
    features_start(r.final_low, r.out_rows, *rows_at)
    if not r.fast:
        features_wait(r.final_low, r.out_rows, *rows_at)


def global_backward_phase(r, sums_of):
    s, z, a, core, sibling = r.s, r.z, r.a, r.core, r.sibling
    pack_heads(r.datt1[...], r.pairs)

    def toward(d):
        c = r.chip(d)
        return remote(r.pairs.at[c], r.dos.at[a], r.b_send.at[d - 1], r.b_recv.at[d - 1], r.chip_device(c))

    for d in (2, 1, 3):
        toward(d).start()
    r.dos[a] = r.pairs[a]
    r.dkt[...] = jnp.zeros_like(r.dkt)
    r.dvt[...] = jnp.zeros_like(r.dvt)
    for d in (1, 3, 2):
        source = r.chip(4 - d)
        there = r.dos.at[source]
        remote(there, there, r.b_send.at[d - 1], r.b_recv.at[d - 1], r.chip_device(source)).wait_recv()
    half = lane_head(RP, 2 * HD)
    low_half = half == 0
    swap = swap_halves()
    ks, vv = r.ks, r.vv

    lane = lax.broadcasted_iota(jnp.int32, (RP, 2 * HD), 1)

    def step(i, carry):
        f = 2 * i + core
        lanes = query_lanes(r, f, r.lse[i][:, 0:1])
        qf = jnp.where(low_half, r.qk[f].astype(F32), lanes).astype(BF)
        unpack(r.dos[i], swap, r.do_rows, 0.0)
        do = r.do_rows[...].astype(F32)
        delta = jnp.sum(do * r.outs_full[i], axis=1, keepdims=True)
        for number, piece in enumerate(pieces(delta)):
            do = jnp.where(lane == HD + number, piece, do)
        do = do.astype(BF)
        probs = jnp.exp(dot_cols(qf, ks[...]))
        dprobs = dot_cols(do, vv[...].reshape(8 * RP, 2 * HD))
        dscores = (probs * dprobs).astype(BF)
        r.dq_mine[i] = dot(dscores, ks[...])
        r.dkt[...] += dot_rows(qf, dscores)
        r.dvt[...] += dot_rows(do, probs.astype(BF))
        return carry

    line_dbr = Gather(by_rows(r.dbr1), *r.line_sems(11))
    line_dbr.sent()
    lax.fori_loop(0, 2, step, 0)
    line_dbr.finish()
    result_start(r)
    lax.fori_loop(2, 4, step, 0)
    r.dk_sum[...] = jnp.transpose(r.dkt[...])
    r.dv_sum[...] = jnp.transpose(r.dvt[...])

    def rows_of(frame):
        return pl.ds(pl.multiple_of(frame * RP, 16), RP)

    for i in range(4):
        theirs = rows_of(2 * i + 1 - core)
        dv = dot(r.dv_sum[theirs, :].astype(BF), swap)
        r.dkv_send[i] = jnp.where(low_half, r.dk_sum[theirs, :], dv).astype(BF)
    across = remote(r.dkv_send, r.dkv_in, r.bc_send.at[0], r.bc_recv.at[0], sibling)
    across.start()
    down_grad(r, r.att1, r.dbr1, r.d_out)
    sums_of["out"].start()
    result_relay(r)
    across.wait()
    for i in range(4):
        own = rows_of(2 * i + core)
        dk = (r.dk_sum[own, :] + r.dkv_in[i].astype(F32)).astype(BF)
        dv = r.dv_sum[own, :] + dot(r.dkv_in[i], swap)
        r.ready[i] = jnp.where(low_half, r.dq_mine[i], dot(dk, swap)).astype(BF)
        r.ready_values[i] = pack(dv.astype(BF), swap)

    def back(d):
        target = r.chip(d)
        device = r.chip_device(target)
        return (
            remote(r.ready.at[target], r.dqk_in.at[a], r.bb_send.at[0, d - 1], r.bb_recv.at[0, d - 1], device),
            remote(r.ready_values.at[target], r.dv_in.at[a], r.bb_send.at[1, d - 1], r.bb_recv.at[1, d - 1], device),
        )

    for d in (2, 1, 3):
        for copy in back(d):
            copy.start()
    r.dqk_in[a] = r.ready[a]
    r.dv_in[a] = r.ready_values[a]
    for d in (1, 3, 2):
        source = r.chip(4 - d)
        for number, box in ((0, r.dqk_in), (1, r.dv_in)):
            there = box.at[source]
            sems = (r.bb_send.at[number, d - 1], r.bb_recv.at[number, d - 1])
            remote(there, there, *sems, r.chip_device(source)).wait_recv()
    to_q, to_k = place(True), place(False)
    dq = jnp.zeros((RP, WIDE), F32)
    dk = jnp.zeros((RP, WIDE), F32)
    for c in range(4):
        cols = slice(128 * c, 128 * c + 128)
        dq = dq + dot_cols(r.dqk_in[c], to_q[:, cols])
        dk = dk + dot_cols(r.dqk_in[c], to_k[:, cols])
    r.dq[...] = dq
    r.dk[...] = dk
    unpack_heads(r.dv_in, r.dv)
    for d in (1, 2, 3):
        toward(d).wait_send()
        for copy in back(d):
            copy.wait_send()


def attention_back_phase(r, sums_of=None):
    s, z = r.s, r.z
    if r.fast:
        sums_of["up"].pass_on()
    dnorm_at, next_at = r.line_sems(13), r.line_sems(14)
    heads_back(r, r.raw1, r.dq[...], r.dk[...], r.dv[...], 1, r.dproj)
    if r.fast:
        result_end(r)
    attention_input_back(r.dproj, r.need("wq", 1), r.part)

    def first():
        qkv_grad(r, r.h1, r.dproj, r.d_qkv)
        if r.fast:
            r.prefetch("wq", 0)
            sums_of["qkv"].start()

    def second():
        if r.fast:
            sums_of["out"].pass_on()

    dnorm = sum_rows(r, dnorm_at, (first, second))
    after = through_norm(r, 1, 0, r.x2, dnorm, r.g3[...])
    r.g5[...] = after
    put_own(r.dm0, z, (after * r.params_full[9:10]).astype(BF))
    if r.fast:
        sums_of["qkv"].pass_on()
    else:
        share_rows(r, r.dm0, next_at)
    scale_grad(r, 0, 1, after, r.mo0[...])


def mlp_back_phase(r, sums_of=None, earlier=None):
    s, z = r.s, r.z
    dnorm_at, next_at = r.line_sems(15), r.line_sems(16)
    w_down, w_up = r.need("wd", 0), r.need("wu", 0)

    def back(rows):
        mlp_back(r.dm0, w_down, r.slope0, r.dpre, rows)
        times_turned(r.dpre, w_up, r.part, rows)

    def first():
        if r.fast:
            earlier["down"].finish(r.grad_w_down)
        down_grad(r, r.act0, r.dm0, r.d_down)
        if r.fast:
            sums_of["down"].start()

    def second():
        if r.fast:
            earlier["up"].finish(r.grad_w_up)
        up_grad(r, r.m0, r.dpre, r.d_up)
        if r.fast:
            sums_of["up"].start()
            sums_of["down"].pass_on()

    if r.fast:
        dnorm = pass_rows(r, r.dm0, r.line_sems(14), back, dnorm_at, (first, second))
    else:
        back(ALL_ROWS)
        dnorm = sum_rows(r, dnorm_at, (first, second))
    after = through_norm(r, 0, 1, r.x1, dnorm, r.g5[...])
    r.g6[...] = after
    put_own(r.dbr0, z, (after * r.params_full[8:9]).astype(BF))
    gather = Gather(by_rows(r.dbr0), *next_at)
    gather.start()
    scale_grad(r, 0, 0, after, r.br0[...])
    if r.fast:
        sums_of["up"].pass_on()
    gather.sent()
    gather.finish()


def last_phase(r, sums_of=None, earlier=None):
    s, z = r.s, r.z
    dnorm_at, rows_at, notes_at = (r.line_sems(i) for i in range(17, 20))
    valid = own_valid(z)
    datt = dot_cols(r.dbr0[...], r.need("wo", 0)[...]).astype(BF).astype(F32)
    heads = lane_head(RP)
    keep = key_valid()
    queries = r.q0[...].astype(F32)
    dq = jnp.zeros((RP, WIDE), F32)
    dk = jnp.zeros((RP, WIDE), F32)
    dv = jnp.zeros((RP, WIDE), F32)
    for h in range(WIDE // HD):
        here = heads == h
        qh = jnp.where(here, queries, 0.0).astype(BF)
        do = jnp.where(here, datt, 0.0).astype(BF)
        scores = jnp.where(keep, dot_cols(qh, r.k0[...]), NEG)
        expo = jnp.exp(scores - jnp.max(scores, axis=1, keepdims=True))
        probs = expo * (1.0 / jnp.sum(expo, axis=1, keepdims=True))
        dprobs = dot_cols(do, r.v0[...])
        delta = jnp.sum(probs * dprobs, axis=1, keepdims=True)
        dscores = (probs * (dprobs - delta)).astype(BF)
        dq = jnp.where(here, dot(dscores, r.k0[...]), dq)
        dk = dk + dot_rows(dscores, qh)
        dv = dv + dot_rows(probs.astype(BF), do)
    heads_back(r, r.raw0, dq, dk, dv, 0, r.dproj)
    attention_input_back(r.dproj, r.need("wq", 0), r.part)

    def first():
        if r.fast:
            earlier["qkv"].finish(r.grad_w_qkv)
        qkv_grad(r, r.h0, r.dproj, r.d_qkv)
        if r.fast:
            sums_of["qkv"].start()

    def second():
        if r.fast:
            earlier["out"].finish(r.grad_w_out)
        down_grad(r, r.att0, r.dbr0, r.d_out)
        if r.fast:
            sums_of["out"].start()
            sums_of["qkv"].pass_on()
            sums_of["out"].pass_on()

    dnorm = sum_rows(r, dnorm_at, (first, second))
    r.final[...] = through_norm(r, 0, 0, r.x0, dnorm, r.g6[...]).astype(BF)
    features_start(r.final, r.grad_rows, *rows_at)
    for p in range(NZ):
        r.messages[p, 0:16] = r.sums[:, WIDE * p : WIDE * p + WIDE]
        r.messages[p, 16:24] = r.head_sums[...]

    def note(d):
        send, recv = notes_at[2:]
        peer = lax.rem(z + d, NZ)
        return remote(r.messages.at[peer], r.letters.at[d - 1], send.at[d - 1], recv.at[d - 1], (s, peer))

    for d in range(1, NZ):
        note(d).start()
    for d in range(1, NZ):
        note(d).wait()
    r.small[...] = r.messages[z] + r.letters[0] + r.letters[1] + r.letters[2]
    features_wait(r.final, r.grad_rows, *rows_at)


def small_phase(r):
    pair = remote(r.small, r.small_in.at[0], r.small_send.at[0], r.small_recv.at[0], r.sibling)
    pair.start()
    pair.wait()
    r.small_two[...] = r.small[...] + r.small_in[0]

    def toward(d):
        device = r.chip_device(r.chip(d))
        return remote(r.small_two, r.small_in.at[d], r.small_send.at[d], r.small_recv.at[d], device)

    for d in range(1, 4):
        toward(d).start()
    for d in range(1, 4):
        toward(d).wait()
    boxes = [r.small_two[...], r.small_in[1], r.small_in[2], r.small_in[3]]
    total = None
    for chip in range(4):
        distance = lax.rem(r.a + 4 - chip, 4)
        term = boxes[0]
        for d in range(1, 4):
            term = jnp.where(distance == d, boxes[d], term)
        total = term if total is None else total + term
    r.small_out[...] = total


def gather_params(r):
    for b in range(2):
        r.params[2 * b : 2 * b + 2] = r.block_norm_multiplier[b]
        r.params[4 + 2 * b : 6 + 2 * b] = r.block_norm_bias[b]
        r.params[8 + 2 * b : 10 + 2 * b] = r.layer_scale[b]
        for h in range(WIDE // HD):
            lanes = slice(HD * h, HD * h + HD)
            r.head_params[2 * b : 2 * b + 2, lanes] = r.qk_gain[b]
            r.head_params[4 + 2 * b : 6 + 2 * b, lanes] = r.qk_bias[b]
    r.params[12:16] = jnp.zeros((4, WIDE), F32)


def find_scenes(r):
    for slot in range(r.slot_frames.shape[0]):
        frame = r.slot_frames[slot]
        end, scene = 0, 0
        for number in range(r.frame_counts.shape[0]):
            end = end + r.frame_counts[number]
            scene = scene + jnp.where(end <= frame, 1, 0)
        r.scenes[slot] = scene


def whole_kernel(names, *refs):
    r = Refs(names, refs, True)
    gather_params(r)
    start_phase(r)
    greet(line(r.s, r.z) + [r.chip_device(r.chip(d)) for d in range(1, 4)] + [r.sibling])
    numbers = {"down": 0, "up": 1, "out": 2, "qkv": 3}
    later = {name: SeqSum(r, name, 1, number) for name, number in numbers.items()}
    sooner = {name: SeqSum(r, name, 0, 4 + number) for name, number in numbers.items()}
    r.sums[...] = jnp.zeros_like(r.sums)
    r.head_sums[...] = jnp.zeros_like(r.head_sums)
    find_scenes(r)
    whole_out = WholeOut(r, 20)
    whole_out.fetch(1).start()
    block_zero_phase(r, whole_out)
    global_forward_phase(r)
    middle_phase(r, later)
    global_backward_phase(r, later)
    attention_back_phase(r, later)
    features_wait(r.final_low, r.out_rows, *r.line_sems(12))
    mlp_back_phase(r, sooner, later)
    last_phase(r, sooner, later)
    small_phase(r)
    sooner["down"].finish(r.grad_w_down)
    sooner["up"].finish(r.grad_w_up)
    sooner["qkv"].finish(r.grad_w_qkv)
    sooner["out"].finish(r.grad_w_out)


def plain_kernel(phase, names, fresh, weights, *refs):
    r = Refs(names, refs, False)
    greet(line(r.s, r.z))
    for name in fresh:
        getattr(r, name)[...] = jnp.zeros_like(getattr(r, name))
    if phase is block_zero_phase:
        start_phase(r)
    if phase is last_phase:
        r.sums[...] = r.sums_in[...]
        r.head_sums[...] = r.head_sums_in[...]
    phase(r)


def results_kernel(
    out_rows,
    grad_rows,
    small,
    qkv_in,
    out_in,
    up_in,
    down_in,
    out_tokens,
    grad_tokens,
    gains,
    norm_bias,
    mlp_bias,
    head_gain,
    head_bias,
    scales,
    qkv,
    out,
    up,
    down,
    qkv_held,
    out_held,
    up_held,
    down_held,
    out_rows_held,
    grad_rows_held,
    small_held,
    sems,
):
    sources = (qkv_in, out_in, up_in, down_in, out_rows, grad_rows, small)
    held = (qkv_held, out_held, up_held, down_held, out_rows_held, grad_rows_held, small_held)
    loads = [pltpu.make_async_copy(sources[i], held[i], sems.at[0, i]) for i in range(7)]
    for copy in (loads[4], loads[5], loads[6], *loads[:4]):
        copy.start()
    stores = [
        pltpu.make_async_copy(held[i], target, sems.at[1, i]) for i, target in enumerate((qkv, out, up, down))
    ]
    for load, store in zip(loads, stores):
        load.wait()
        store.start()
    for copy in loads[4:]:
        copy.wait()
    out_rows, grad_rows, small = held[4:]
    out_tokens[...] = out_rows[pl.ds(0, TOK)]
    grad_tokens[...] = grad_rows[pl.ds(0, TOK)].astype(F32)
    for b in range(2):
        gains[b] = small[2 * b : 2 * b + 2]
        scales[b] = small[8 + 2 * b : 10 + 2 * b]
    norm_bias[...] = small[4:6]
    mlp_bias[...] = small[6:8]
    row = lax.broadcasted_iota(jnp.int32, (WIDE, HD), 0)
    col = lax.broadcasted_iota(jnp.int32, (WIDE, HD), 1)
    fold = jnp.where(lax.bitwise_and(row, HD - 1) == col, 1.0, 0.0).astype(F32)
    heads = jnp.dot(small[16:24], fold, precision=HIGH, preferred_element_type=F32)
    for b in range(2):
        head_gain[b] = heads[4 * b : 4 * b + 2]
        head_bias[b] = heads[4 * b + 2 : 4 * b + 4]
    for store in stores:
        store.wait()


def gather_frames(rows):
    return lax.all_gather(rows, "seq", axis=0)


def global_forward_plain(query_rows, key_rows, value_rows, allowed_frames):
    head_count = query_rows.shape[1]
    state = (
        jnp.full((head_count, TOK), NEG, F32),
        jnp.zeros((head_count, TOK), F32),
        jnp.zeros((head_count, TOK, HD), F32),
    )

    def advance(running, item):
        key_block, value_block, allowed = item

        def update(current):
            peak, totals, weighted = current
            scores = jnp.einsum("qhd,khd->hqk", query_rows, key_block, preferred_element_type=F32)
            new_peak = jnp.maximum(peak, jnp.max(scores, axis=-1))
            expo = jnp.exp(scores - new_peak[..., None])
            factor = jnp.exp(peak - new_peak)
            totals = totals * factor + jnp.sum(expo, axis=-1)
            weighted = weighted * factor[..., None] + jnp.einsum(
                "hqk,khd->hqd", expo.astype(BF), value_block, preferred_element_type=F32
            )
            return (new_peak, totals, weighted)

        return (lax.cond(allowed, update, lambda current: current, running), None)

    (peak, totals, weighted), _ = lax.scan(
        advance, state, (gather_frames(key_rows), gather_frames(value_rows), allowed_frames)
    )
    attended = jnp.transpose(weighted / totals[..., None], (1, 0, 2))
    return attended, peak + jnp.log(totals)


def global_backward_plain(query_rows, key_rows, value_rows, out_grad, attended, lse, allowed_frames):
    delta = jnp.transpose(jnp.sum(attended * out_grad.astype(F32), axis=-1))
    zero = jnp.zeros(query_rows.shape, F32)

    def pieces(q, do, stat, row_sum, k, v):
        scores = jnp.einsum("qhd,khd->hqk", q, k, preferred_element_type=F32)
        probs = jnp.exp(scores - stat[..., None])
        dprobs = jnp.einsum("qhd,khd->hqk", do, v, preferred_element_type=F32)
        return probs.astype(BF), (probs * (dprobs - row_sum[..., None])).astype(BF)

    def advance_query(total, item):
        k, v, allowed = item

        def update(current):
            _, dscores = pieces(query_rows, out_grad, lse, delta, k, v)
            return current + jnp.einsum("hqk,khd->qhd", dscores, k, preferred_element_type=F32)

        return (lax.cond(allowed, update, lambda current: current, total), None)

    dq, _ = lax.scan(
        advance_query, zero, (gather_frames(key_rows), gather_frames(value_rows), allowed_frames)
    )

    def advance_keys(totals, item):
        q, do, stat, row_sum, allowed = item

        def update(current):
            probs, dscores = pieces(q, do, stat, row_sum, key_rows, value_rows)
            return (
                current[0] + jnp.einsum("hqk,qhd->khd", dscores, q, preferred_element_type=F32),
                current[1] + jnp.einsum("hqk,qhd->khd", probs, do, preferred_element_type=F32),
            )

        return (lax.cond(allowed, update, lambda current: current, totals), None)

    (dk, dv), _ = lax.scan(
        advance_keys,
        (zero, zero),
        (
            gather_frames(query_rows),
            gather_frames(out_grad),
            gather_frames(lse),
            gather_frames(delta),
            allowed_frames,
        ),
    )
    return dq, dk, dv


def buffers(depth, hidden):
    rows_d = ((RP, depth), BF)
    rows_w = ((RP, WIDE), BF)
    wide_f = ((RP, WIDE), F32)
    own_f = ((RO, depth), F32)
    raw = ((2, RP, WIDE), F32)
    slab = (RP, 2 * HD)
    table = {
        "params_full": ((16, depth), F32),
        "every": rows_d,
        "wof": ((NZ, 8, WIDE // 8, depth), BF),
        "wo_part": ((WIDE // 8, depth), BF),
        "att_in": ((RO, depth), BF),
        "datt_own": ((RO, depth), BF),
        "part": rows_d,
        "part_out": rows_d,
        "inbox": ((2, 4, RO, depth), BF),
        "wq": ((3, depth, WIDE), BF),
        "wo": ((WIDE, depth), BF),
        "wu": ((depth, hidden), BF),
        "wd": ((hidden, depth), BF),
        "act0": ((RP, hidden), BF),
        "act1": ((RP, hidden), BF),
        "slope0": ((RP, hidden), F32),
        "slope1": ((RP, hidden), F32),
        "dpre": ((RP, hidden), BF),
        "final_low": ((RO, depth), BF),
        "final": ((RO, depth), BF),
        "dproj": ((3, RP, WIDE), BF),
        "sums": ((16, depth), F32),
        "head_sums": ((8, WIDE), F32),
        "messages": ((NZ, 24, WIDE), F32),
        "letters": ((NZ - 1, 24, WIDE), F32),
        "small": ((24, WIDE), F32),
        "small_two": ((24, WIDE), F32),
        "small_in": ((4, 24, WIDE), F32),
        "qk": ((8,) + slab, BF),
        "vv": ((8,) + slab, BF),
        "ks": ((8 * RP, 2 * HD), BF),
        "lse": ((4,) + slab, F32),
        "slabs": ((4,) + slab, BF),
        "pairs": ((4, HALF_ROWS, 2 * HD), BF),
        "outs": ((4, HALF_ROWS, 2 * HD), BF),
        "outs_full": ((4,) + slab, F32),
        "ins": ((4, HALF_ROWS, 2 * HD), BF),
        "dos": ((4, HALF_ROWS, 2 * HD), BF),
        "dkt": ((2 * HD, 8 * RP), F32),
        "dvt": ((2 * HD, 8 * RP), F32),
        "dq_mine": ((4,) + slab, F32),
        "dk_sum": ((8 * RP, 2 * HD), F32),
        "dv_sum": ((8 * RP, 2 * HD), F32),
        "dkv_send": ((4,) + slab, BF),
        "dkv_in": ((4,) + slab, BF),
        "ready": ((4,) + slab, BF),
        "ready_values": ((4, HALF_ROWS, 2 * HD), BF),
        "packed_values": ((8, HALF_ROWS, 2 * HD), BF),
        "do_rows": (slab, BF),
        "dqk_in": ((4,) + slab, BF),
        "dv_in": ((4, HALF_ROWS, 2 * HD), BF),
        "out_rows": rows_w,
        "grad_rows": rows_w,
    }
    for name in ("q0", "k0", "v0", "att0", "q1", "k1", "v1", "att1", "datt1"):
        table[name] = rows_w
    for name in ("dq", "dk", "dv"):
        table[name] = wide_f
    for name in ("h0", "m0", "h1", "m1", "grad_full", "dmlp", "dbr1", "dm0", "dbr0"):
        table[name] = rows_d
    for name in ("x0", "x1", "x2", "x3", "br0", "br1", "mo0", "g3", "g5", "g6"):
        table[name] = own_f
    for name in ("raw0", "raw1"):
        table[name] = raw
    piece = {
        "qkv": (3, depth // 8, WIDE),
        "out": (WIDE, depth // 8),
        "up": (depth // 8, hidden),
        "down": (hidden, depth // 8),
    }
    for name, shape in piece.items():
        table["d_" + name] = ((2, 4) + shape, BF)
        table["first_" + name] = ((4,) + shape, BF)
        table["second_" + name] = ((2, 3) + shape, BF)
    return table


SEMAPHORES = {
    "fetch_sem": (5,),
    "z_send": (24, 4),
    "z_recv": (24, 4),
    "wo_send": (1, 7),
    "wo_recv": (1, 7),
    "f_send": (2, 3),
    "f_recv": (2, 3),
    "fc_send": (2, 4),
    "fc_recv": (2, 4),
    "fb_send": (3,),
    "fb_recv": (3,),
    "b_send": (3,),
    "b_recv": (3,),
    "bc_send": (1,),
    "bc_recv": (1,),
    "bb_send": (2, 3),
    "bb_recv": (2, 3),
    "sum_send": (8, 4),
    "sum_recv": (8, 4),
    "small_send": (4,),
    "small_recv": (4,),
}
IN_HBM = ("w_qkv", "w_out", "w_up", "w_down")


def call(body, given, outs, scratch, collective_id, name, vmem_mib):
    names = list(given) + list(outs) + list(scratch)
    def room(shape, kind):
        if kind is None:
            return pltpu.SemaphoreType.DMA(shape)
        return pltpu.SMEM(shape, jnp.int32) if kind == "scalars" else pltpu.VMEM(shape, kind)

    def space(key):
        if key in IN_HBM:
            return pl.ANY
        return pltpu.SMEM if key in ("frame_counts", "slot_frames") else pltpu.VMEM

    scratch_shapes = [room(shape, kind) for shape, kind in scratch.values()]
    results = pl.pallas_call(
        partial(body, names),
        name=name,
        out_shape=[jax.ShapeDtypeStruct(shape, kind) for shape, kind in outs.values()],
        in_specs=[pl.BlockSpec(memory_space=space(key)) for key in given],
        out_specs=[pl.BlockSpec(memory_space=pltpu.VMEM)] * len(outs),
        scratch_shapes=scratch_shapes,
        compiler_params=pltpu.CompilerParams(
            collective_id=collective_id, has_side_effects=True, vmem_limit_bytes=vmem_mib * 2**20
        ),
    )(*given.values())
    return dict(zip(outs, results))


def whole(given, depth, hidden):
    table = buffers(depth, hidden)
    frame_total = given["slot_frames"].shape[0]
    table["params"] = ((16, WIDE), F32)
    table["head_params"] = ((8, WIDE), F32)
    outs = {
        "out_rows": table.pop("out_rows"),
        "grad_rows": table.pop("grad_rows"),
        "small_out": ((24, WIDE), F32),
        "grad_w_qkv": ((2, 3, depth // 8, WIDE), F32),
        "grad_w_out": ((2, WIDE, depth // 8), F32),
        "grad_w_up": ((2, depth // 8, hidden), F32),
        "grad_w_down": ((2, hidden, depth // 8), F32),
    }
    scratch = {**table, **{name: (shape, None) for name, shape in SEMAPHORES.items()}}
    scratch["scenes"] = ((frame_total,), "scalars")
    out = call(whole_kernel, given, outs, scratch, 0, "whole", 62)
    big = ("grad_w_qkv", "grad_w_out", "grad_w_up", "grad_w_down")
    shapes = [
        ((TOK, WIDE), BF),
        ((TOK, WIDE), F32),
        ((2, 2, WIDE), F32),
        ((2, WIDE), F32),
        ((2, WIDE), F32),
        ((2, 2, HD), F32),
        ((2, 2, HD), F32),
        ((2, 2, WIDE), F32),
    ] + [outs[name] for name in big]
    in_vmem, in_hbm = pl.BlockSpec(memory_space=pltpu.VMEM), pl.BlockSpec(memory_space=pl.ANY)
    results = pl.pallas_call(
        results_kernel,
        name="results",
        out_shape=[jax.ShapeDtypeStruct(shape, kind) for shape, kind in shapes],
        in_specs=[in_hbm] * 7,
        out_specs=[in_vmem] * 8 + [in_hbm] * 4,
        scratch_shapes=[pltpu.VMEM(*outs[name]) for name in big + ("out_rows", "grad_rows", "small_out")]
        + [pltpu.SemaphoreType.DMA((2, 7))],
        compiler_params=pltpu.CompilerParams(vmem_limit_bytes=60 * 2**20),
    )(out["out_rows"], out["grad_rows"], out["small_out"], *(out[name] for name in big))
    return tuple(results[:7]) + tuple(results[8:12]) + (results[7],)


def by_phases(given, same_scene, depth, hidden):
    heads_here = WIDE // HD
    table = buffers(depth, hidden)
    table["d_qkv"] = ((3, depth, WIDE), BF)
    table["d_out"] = ((WIDE, depth), BF)
    table["d_up"] = ((depth, hidden), BF)
    table["d_down"] = ((hidden, depth), BF)
    held = dict(given)

    def run(phase, ins, outs, scratch, fresh=()):
        ins = {name: held[name] for name in ins}
        outs = {name: table[name] for name in outs}
        scratch = {name: table[name] for name in scratch}
        for name in ("fetch_sem", "z_send", "z_recv"):
            scratch[name] = (SEMAPHORES[name], None)

        def body(names, *refs):
            plain_kernel(phase, names, fresh, None, *refs)

        number = (block_zero_phase, middle_phase, attention_back_phase, mlp_back_phase, last_phase).index(phase)
        held.update(call(body, ins, outs, scratch, 1 + number, phase.__name__, 48))

    def rows(array):
        return array[:TOK].reshape(TOK, heads_here, HD)

    def padded(array):
        return jnp.pad(array.reshape(TOK, -1), ((0, RP - TOK), (0, 0)))

    allowed = same_scene[lax.axis_index("seq")]
    run(
        block_zero_phase,
        ("tokens", "params", "head_params") + IN_HBM,
        ("params_full", "x0", "h0", "raw0", "q0", "k0", "v0", "att0", "x1", "br0", "m0", "act0", "slope0", "mo0", "x2", "h1", "raw1", "q1", "k1", "v1"),
        ("every", "part", "inbox", "wq", "wo", "wu", "wd"),
    )
    q1, k1, v1 = rows(held["q1"]), rows(held["k1"]), rows(held["v1"])
    attended, lse = global_forward_plain(q1, k1, v1, allowed)
    held["att1"] = padded(attended.astype(BF))
    held["grad_full"] = padded(lax.all_gather(given["grad_out"], "mp", axis=1, tiled=True))
    run(
        middle_phase,
        ("att1", "x2", "grad_full", "params_full", "w_out", "w_up", "w_down"),
        ("out_rows", "g3", "x3", "br1", "dbr1", "datt1", "d_up", "d_down", "sums"),
        ("part", "part_out", "inbox", "m1", "act1", "slope1", "dmlp", "dpre", "final_low", "wo", "wu", "wd"),
        ("sums",),
    )
    d_up1 = lax.psum_scatter(held["d_up"], "seq", scatter_dimension=0, tiled=True)
    d_down1 = lax.psum_scatter(held["d_down"], "seq", scatter_dimension=1, tiled=True)
    sums = held["sums"]
    grads = global_backward_plain(q1, k1, v1, rows(held["datt1"]), attended, lse, allowed)
    held["dq"], held["dk"], held["dv"] = (padded(array) for array in grads)
    d_out1 = lax.dot_general(
        held["att1"], held["dbr1"], (((0,), (0,)), ((), ())), preferred_element_type=F32
    ).astype(BF)
    run(
        attention_back_phase,
        ("dq", "dk", "dv", "raw1", "h1", "x2", "g3", "mo0", "params_full", "head_params", "w_qkv"),
        ("g5", "dm0", "d_qkv", "sums", "head_sums"),
        ("part", "inbox", "dproj", "wq"),
        ("sums", "head_sums"),
    )
    d_qkv1 = lax.psum_scatter(held["d_qkv"], "seq", scatter_dimension=1, tiled=True)
    d_out1 = lax.psum_scatter(d_out1, "seq", scatter_dimension=1, tiled=True)
    sums = sums + held["sums"]
    held["head_sums_in"] = held["head_sums"]
    run(
        mlp_back_phase,
        ("dm0", "act0", "slope0", "m0", "x1", "g5", "br0", "params_full", "w_up", "w_down"),
        ("g6", "dbr0", "d_up", "d_down", "sums"),
        ("part", "inbox", "dpre", "wu", "wd"),
        ("sums",),
    )
    d_up0 = lax.psum_scatter(held["d_up"], "seq", scatter_dimension=0, tiled=True)
    d_down0 = lax.psum_scatter(held["d_down"], "seq", scatter_dimension=1, tiled=True)
    held["sums_in"] = sums + held["sums"]
    run(
        last_phase,
        ("dbr0", "att0", "raw0", "q0", "k0", "v0", "h0", "x0", "g6", "params_full", "head_params", "sums_in", "head_sums_in", "w_out", "w_qkv"),
        ("grad_rows", "d_qkv", "d_out", "small"),
        ("part", "inbox", "dproj", "final", "messages", "letters", "sums", "head_sums", "wo", "wq"),
    )
    d_qkv0 = lax.psum_scatter(held["d_qkv"], "seq", scatter_dimension=1, tiled=True)
    d_out0 = lax.psum_scatter(held["d_out"], "seq", scatter_dimension=1, tiled=True)

    def both(first, second):
        return jnp.stack([first, second]).astype(F32)

    return {
        "out_rows": held["out_rows"],
        "grad_rows": held["grad_rows"].astype(F32),
        "small_out": lax.psum(held["small"], "seq"),
        "grad_w_qkv": both(d_qkv0, d_qkv1),
        "grad_w_out": both(d_out0, d_out1),
        "grad_w_up": both(d_up0, d_up1),
        "grad_w_down": both(d_down0, d_down1),
    }


def per_device(
    tokens,
    grad_out,
    frame_counts,
    slot_frames,
    block_norm_multiplier,
    block_norm_bias,
    qk_gain,
    qk_bias,
    w_qkv,
    w_out,
    w_up,
    w_down,
    layer_scale,
):
    depth = w_qkv.shape[2]
    hidden = w_up.shape[2]
    given = {
        "tokens": tokens,
        "grad_out": grad_out,
        "w_qkv": w_qkv,
        "w_out": w_out,
        "w_up": w_up,
        "w_down": w_down,
    }
    if lax.axis_size("seq") == 8:
        given.update(
            frame_counts=frame_counts,
            slot_frames=slot_frames,
            block_norm_multiplier=block_norm_multiplier,
            block_norm_bias=block_norm_bias,
            qk_gain=qk_gain,
            qk_bias=qk_bias,
            layer_scale=layer_scale,
        )
        return whole(given, depth, hidden)

    heads_here = WIDE // HD
    frame_total = slot_frames.shape[0]
    frame_ids = jnp.arange(frame_total, dtype=jnp.int32)
    scene_ends = jnp.cumsum(frame_counts)
    scene_of_frame = jnp.sum((scene_ends[None, :] <= frame_ids[:, None]).astype(jnp.int32), axis=1)
    scene_table = jnp.sum(
        jnp.where(slot_frames[:, None] == frame_ids[None, :], scene_of_frame[None, :], 0), axis=1
    )
    same_scene = scene_table[:, None] == scene_table[None, :]
    given["params"] = jnp.concatenate(
        [
            block_norm_multiplier.reshape(4, WIDE),
            block_norm_bias.reshape(4, WIDE),
            layer_scale.reshape(4, WIDE),
            jnp.zeros((4, WIDE), F32),
        ]
    )
    given["head_params"] = jnp.tile(
        jnp.concatenate([qk_gain.reshape(4, HD), qk_bias.reshape(4, HD)]), (1, heads_here)
    )
    out = by_phases(given, same_scene, depth, hidden)
    small = out["small_out"]
    head_grads = small[16:24].reshape(2, 2, 2, heads_here, HD).sum(axis=3)
    return (
        out["out_rows"][:TOK],
        out["grad_rows"][:TOK],
        small[0:4].reshape(2, 2, WIDE),
        small[4:6],
        small[6:8],
        head_grads[:, 0],
        head_grads[:, 1],
        out["grad_w_qkv"],
        out["grad_w_out"],
        out["grad_w_up"],
        out["grad_w_down"],
        small[8:12].reshape(2, 2, WIDE),
    )


def solution(mesh):
    in_specs = (
        P("seq", "mp"),
        P("seq", "mp"),
        P(),
        P(),
        P(None, None, "mp"),
        P(None, None, "mp"),
        P(),
        P(),
        P(None, None, None, "mp"),
        P(None, "mp", None),
        P(None, None, "mp"),
        P(None, "mp", None),
        P(None, None, "mp"),
    )
    out_specs = (
        P("seq", "mp"),
        P("seq", "mp"),
        P(None, None, "mp"),
        P(None, "mp"),
        P(None, "mp"),
        P(),
        P(),
        P(None, None, "seq", "mp"),
        P(None, "mp", "seq"),
        P(None, "seq", "mp"),
        P(None, "mp", "seq"),
        P(None, None, "mp"),
    )
    return jax.shard_map(
        per_device, mesh=mesh, in_specs=in_specs, out_specs=out_specs, check_vma=False
    )
```

```python
from functools import partial

import jax
import jax.numpy as jnp
from jax import lax
from jax.experimental import pallas as pl
from jax.experimental.pallas import tpu as pltpu
from jax.sharding import PartitionSpec as P

HD = 64
TOK = 261
EPS = 1e-06
NEG = -1e30

RP = 272
CH = 64
RO = 80
NZ = 4
WIDE = 256
F32 = jnp.float32
BF = jnp.bfloat16
MESH = pl.DeviceIdType.MESH


class Names:
    def __getattr__(self, name):
        return name


NAMES = Names()
HIGH = lax.Precision.HIGHEST


def dot(left, right):
    return jnp.dot(left, right, preferred_element_type=F32)


def dot_cols(left, right):
    return lax.dot_general(left, right, (((1,), (1,)), ((), ())), preferred_element_type=F32)


def dot_rows(left, right):
    return lax.dot_general(left, right, (((0,), (0,)), ((), ())), preferred_element_type=F32)


def tile(index, width=WIDE):
    return pl.ds(pl.multiple_of(index * width, width), width)


def standardize(x):
    mean = jnp.mean(x, axis=1, keepdims=True)
    centered = x - mean
    variance = jnp.mean(centered * centered, axis=1, keepdims=True)
    rstd = lax.rsqrt(variance + EPS)
    return centered * rstd, rstd


def norm_back(dnorm, x, multiplier, valid):
    xhat, rstd = standardize(x)
    gain = jnp.sum(jnp.where(valid, dnorm * xhat, 0.0), axis=0, keepdims=True)
    bias = jnp.sum(jnp.where(valid, dnorm, 0.0), axis=0, keepdims=True)
    e = dnorm * multiplier
    dv = rstd * (
        e - jnp.mean(e, axis=1, keepdims=True) - xhat * jnp.mean(e * xhat, axis=1, keepdims=True)
    )
    return dv, gain, bias


def head_means():
    row = lax.broadcasted_iota(jnp.int32, (WIDE, WIDE), 0)
    col = lax.broadcasted_iota(jnp.int32, (WIDE, WIDE), 1)
    same = lax.shift_right_logical(row, 6) == lax.shift_right_logical(col, 6)
    return jnp.where(same, 1.0 / HD, 0.0).astype(BF)


def mean_heads(x, means):
    high = x.astype(BF)
    rest = x - high.astype(F32)
    middle = rest.astype(BF)
    low = (rest - middle.astype(F32)).astype(BF)
    return dot(high, means) + (dot(middle, means) + dot(low, means))


def head_standardize(raw, means):
    centered = raw - mean_heads(raw, means)
    rstd = lax.rsqrt(mean_heads(centered * centered, means) + EPS)
    return centered * rstd, rstd


def head_back(dy, xhat, rstd, gain, means):
    e = dy * gain
    raw = rstd * (e - mean_heads(e, means) - xhat * mean_heads(e * xhat, means))
    return (
        raw,
        jnp.sum(dy * xhat, axis=0, keepdims=True),
        jnp.sum(dy, axis=0, keepdims=True),
    )


def lane_head(rows, width=WIDE):
    return lax.shift_right_logical(lax.broadcasted_iota(jnp.int32, (rows, width), 1), 6)


def key_valid():
    return lax.broadcasted_iota(jnp.int32, (RP, RP), 1) < TOK


def own_valid(z):
    row = lax.broadcasted_iota(jnp.int32, (RO, 1), 0)
    return (row < CH) | ((z == NZ - 1) & (row < TOK - (NZ - 1) * CH))


def remote(src, dst, send, recv, device):
    return pltpu.make_async_remote_copy(
        src_ref=src, dst_ref=dst, send_sem=send, recv_sem=recv, device_id=device, device_id_type=MESH
    )


def greet(devices):
    barrier = pltpu.get_barrier_semaphore()
    for device in devices:
        pl.semaphore_signal(barrier, inc=1, device_id=device, device_id_type=MESH)
    pl.semaphore_wait(barrier, len(devices))


def line(s, z):
    return [(s, lax.rem(z + d, NZ)) for d in range(1, NZ)]


def sized(last, act):
    pl.when(last)(lambda: act(RO))
    pl.when(jnp.logical_not(last))(lambda: act(CH))


def block(z, rows):
    return pl.ds(pl.multiple_of(z * CH, CH), rows)


def own_rows(z):
    return pl.ds(pl.multiple_of(z * CH, CH), RO)


def put_own(full, z, value):
    full[block(z, CH)] = value[:CH]

    @pl.when(z == NZ - 1)
    def _():
        full[pl.ds(NZ * CH, RO - CH)] = value[CH:]


class Line:
    def __init__(self, z):
        self.z = z
        self.near = lax.bitwise_xor(z, 1)
        self.is_end = (z == 0) | (z == NZ - 1)
        self.is_middle = jnp.logical_not(self.is_end)
        self.other_middle = jnp.where(z < 2, 2, 1)
        self.other_end = jnp.where(z < 2, 3, 0)


def by_rows(full):
    def view(owner, act):
        sized(owner == NZ - 1, lambda rows: act(full.at[block(owner, rows)]))

    return view


def by_columns(full):
    def view(owner, act):
        act(full.at[:, tile(owner)])

    return view


class Gather:
    def __init__(self, view, s, z, send, recv):
        self.view, self.s, self.line = view, s, Line(z)
        self.send, self.recv = send, recv

    def copy(self, ref, sent, arrived, target):
        return remote(ref, ref, self.send.at[sent], self.recv.at[arrived], (self.s, target))

    def own(self, sent, arrived, target, act):
        self.view(self.line.z, lambda ref: act(self.copy(ref, sent, arrived, target)))

    def start(self):
        line = self.line

        @pl.when(line.is_end)
        def _():
            self.own(1, 2, line.other_middle, lambda copy: copy.start())

        self.own(0, 0, line.near, lambda copy: copy.start())

        @pl.when(line.is_middle)
        def _():
            self.own(1, 1, line.other_middle, lambda copy: copy.start())
            self.own(2, 1, line.other_end, lambda copy: copy.start())

    def sent(self):
        line = self.line
        self.own(0, 0, line.near, lambda copy: copy.wait_send())
        self.own(1, 1, line.other_middle, lambda copy: copy.wait_send())

        @pl.when(line.is_middle)
        def _():
            self.own(2, 1, line.other_end, lambda copy: copy.wait_send())

    def arrive(self, number, owner):
        self.view(owner, lambda ref: self.copy(ref, 0, number, self.line.near).wait_recv())

    def take_and_pass(self):
        line = self.line
        self.arrive(2, line.other_end)
        self.view(line.other_end, lambda ref: self.copy(ref, 3, 2, line.near).start())

    def passed_on(self):
        line = self.line

        @pl.when(line.is_middle)
        def _():
            self.view(line.other_end, lambda ref: self.copy(ref, 3, 2, line.near).wait_send())

    def finish(self):
        line = self.line
        pl.when(line.is_middle)(self.take_and_pass)
        self.arrive(0, line.near)
        self.arrive(1, line.other_middle)
        self.passed_on()
        pl.when(line.is_end)(lambda: self.arrive(2, line.other_end))


class Scatter:
    def __init__(self, part, inbox, s, z, send, recv):
        self.part, self.inbox, self.s, self.line = part, inbox, s, Line(z)
        self.send, self.recv = send, recv

    def copy(self, owner, box, sent, target, act):
        def go(rows):
            act(
                remote(
                    self.part.at[block(owner, rows)],
                    self.inbox.at[box, pl.ds(0, rows)],
                    self.send.at[sent],
                    self.recv.at[box],
                    (self.s, target),
                )
            )

        sized(owner == NZ - 1, go)

    def direct(self, act):
        line = self.line

        @pl.when(line.is_end)
        def _():
            self.copy(line.other_end, 3, 1, line.near, act)
            self.copy(line.other_middle, 2, 2, line.other_middle, act)

        @pl.when(line.is_middle)
        def _():
            self.copy(line.other_middle, 1, 2, line.other_middle, act)

        self.copy(line.near, 0, 0, line.near, act)

    def start(self):
        self.direct(lambda copy: copy.start())

    def sent(self):
        self.direct(lambda copy: copy.wait_send())

    def across(self, act):
        line = self.line

        def go(rows):
            act(
                remote(
                    self.inbox.at[3, pl.ds(0, rows)],
                    self.inbox.at[1, pl.ds(0, rows)],
                    self.send.at[3],
                    self.recv.at[1],
                    (self.s, line.other_end),
                )
            )

        sized(line.other_end == NZ - 1, go)

    def arrive(self, owner, box):
        self.copy(owner, box, 0, self.line.near, lambda copy: copy.wait_recv())

    def relay(self):
        line = self.line

        @pl.when(line.is_middle)
        def _():
            self.arrive(line.other_end, 3)
            total = self.inbox[3].astype(F32) + self.part[own_rows(line.other_end)].astype(F32)
            self.inbox[3] = total.astype(BF)
            self.across(lambda copy: copy.start())

    def finish(self):
        line = self.line
        total = self.part[own_rows(line.z)].astype(F32)
        for box in (0, 1):
            self.arrive(line.z, box)
            total = total + self.inbox[box].astype(F32)

        @pl.when(line.is_middle)
        def _():
            self.arrive(line.z, 2)
            self.across(lambda copy: copy.wait_send())

        return total + jnp.where(line.is_middle, self.inbox[2].astype(F32), 0.0)


def features_start(rows_ref, full, s, z, send, recv):
    for d in range(1, NZ):
        peer = lax.rem(z + d, NZ)

        def act(rows, d=d, peer=peer):
            remote(
                rows_ref.at[pl.ds(0, rows), tile(peer)],
                full.at[block(z, rows)],
                send.at[d - 1],
                recv.at[d - 1],
                (s, peer),
            ).start()

        sized(z == NZ - 1, act)
    put_own(full, z, rows_ref[:, tile(z)])


def features_wait(rows_ref, full, s, z, send, recv):
    for d in range(1, NZ):
        source = lax.rem(z + NZ - d, NZ)
        peer = lax.rem(z + d, NZ)

        def act_in(rows, d=d, source=source):
            remote(
                rows_ref.at[pl.ds(0, rows), tile(z)],
                full.at[block(source, rows)],
                send.at[d - 1],
                recv.at[d - 1],
                (s, source),
            ).wait_recv()

        def act_out(rows, d=d, peer=peer):
            remote(
                rows_ref.at[pl.ds(0, rows), tile(peer)],
                full.at[block(z, rows)],
                send.at[d - 1],
                recv.at[d - 1],
                (s, peer),
            ).wait_send()

        sized(source == NZ - 1, act_in)
        sized(z == NZ - 1, act_out)


def rows_start(heads_ref, full, s, z, send, recv):
    for d in range(1, NZ):
        peer = lax.rem(z + d, NZ)

        def act(rows, d=d, peer=peer):
            remote(
                heads_ref.at[block(peer, rows)],
                full.at[pl.ds(0, rows), tile(z)],
                send.at[d - 1],
                recv.at[d - 1],
                (s, peer),
            ).start()

        sized(peer == NZ - 1, act)
    full[:, tile(z)] = heads_ref[own_rows(z)]


def rows_wait(heads_ref, full, s, z, send, recv):
    for d in range(1, NZ):
        source = lax.rem(z + NZ - d, NZ)
        peer = lax.rem(z + d, NZ)

        def act_in(rows, d=d, source=source):
            remote(
                heads_ref.at[block(z, rows)],
                full.at[pl.ds(0, rows), tile(source)],
                send.at[d - 1],
                recv.at[d - 1],
                (s, source),
            ).wait_recv()

        def act_out(rows, d=d, peer=peer):
            remote(
                heads_ref.at[block(peer, rows)],
                full.at[pl.ds(0, rows), tile(z)],
                send.at[d - 1],
                recv.at[d - 1],
                (s, peer),
            ).wait_send()

        sized(z == NZ - 1, act_in)
        sized(peer == NZ - 1, act_out)


class Refs:
    WEIGHTS = {NAMES.wq: NAMES.w_qkv, NAMES.wo: NAMES.w_out, NAMES.wu: NAMES.w_up, NAMES.wd: NAMES.w_down}

    def __init__(self, names, refs, fast):
        self.__dict__.update(zip(names, refs))
        self.fast = fast
        self.s, self.z = lax.axis_index("seq"), lax.axis_index("mp")
        self.a, self.core = lax.shift_right_logical(self.s, 1), lax.rem(self.s, 2)
        self.sibling = (2 * self.a + 1 - self.core, self.z)
        self.held = {}

    def weight_copy(self, name, b):
        number = list(self.WEIGHTS).index(name)
        source = getattr(self, self.WEIGHTS[name])
        return pltpu.make_async_copy(source.at[b], getattr(self, name), self.fetch_sem.at[number])

    def prefetch(self, name, b):
        self.weight_copy(name, b).start()
        self.held[name] = (b, False)

    def need(self, name, b):
        held, waited = self.held.get(name, (None, False))
        if held != b:
            self.prefetch(name, b)
            waited = False
        if not waited:
            self.weight_copy(name, b).wait()
        self.held[name] = (b, True)
        return getattr(self, name)

    def line_sems(self, number):
        return (self.s, self.z, self.z_send.at[number], self.z_recv.at[number])

    def chip(self, d):
        return lax.rem(self.a + d, 4)

    def chip_device(self, chip):
        return (2 * chip + self.core, self.z)


def project(r, b, hidden, weights, raw, queries, keys, values, rows=pl.ds(0, RP)):
    means = head_means()
    for c in range(3):
        product = dot(hidden[rows, :], weights[c])
        if c == 2:
            values[rows, :] = product.astype(BF)
            continue
        raw[c, rows, :] = product
        xhat, _ = head_standardize(product, means)
        row = 2 * b + c
        normed = xhat * r.head_params[row : row + 1] + r.head_params[4 + row : 5 + row]
        if c == 0:
            queries[rows, :] = (normed * (HD ** (-0.5))).astype(BF)
        else:
            keys[rows, :] = normed.astype(BF)


def share_rows(r, full, at):
    gather = Gather(by_rows(full), *at)
    gather.start()
    gather.sent()
    gather.finish()


def pass_rows(r, full, at, compute, sum_at=None, meanwhile=()):
    gather = Gather(by_rows(full), *at)
    line = gather.line
    scatter = Scatter(r.part, r.inbox.at[0], *sum_at) if sum_at else None
    own_half = jnp.where(line.z < 2, 0, 1)
    gather.start()

    def step(number, carry):
        half = jnp.where(number == 0, own_half, 1 - own_half)
        first, second = number == 0, number == 1

        @pl.when(first)
        def _():
            pl.when(line.is_middle)(gather.take_and_pass)
            gather.arrive(0, line.near)

        @pl.when(second)
        def _():
            gather.arrive(1, line.other_middle)
            pl.when(line.is_end)(lambda: gather.arrive(2, line.other_end))

        pl.when(half == 0)(lambda: compute(pl.ds(0, 2 * CH)))
        pl.when(half == 1)(lambda: compute(pl.ds(2 * CH, RP - 2 * CH)))
        if scatter is not None:

            def send(owner, box, sent, target):
                scatter.copy(owner, box, sent, target, lambda copy: copy.start())

            @pl.when(first)
            def _():
                send(line.near, 0, 0, line.near)

            @pl.when(second & line.is_end)
            def _():
                send(line.other_end, 3, 1, line.near)
                send(line.other_middle, 2, 2, line.other_middle)

            @pl.when(second & line.is_middle)
            def _():
                send(line.other_middle, 1, 2, line.other_middle)

        return carry

    lax.fori_loop(0, 2, step, 0)
    for work in meanwhile[:1]:
        work()
    gather.sent()
    gather.passed_on()
    if scatter is None:
        return None
    scatter.sent()
    scatter.relay()
    for work in meanwhile[1:]:
        work()
    return scatter.finish()


def sum_rows(r, at, meanwhile=(), box=0):
    scatter = Scatter(r.part, r.inbox.at[box], *at)
    scatter.start()
    for work in meanwhile[:1]:
        work()
    scatter.sent()
    scatter.relay()
    for work in meanwhile[1:]:
        work()
    return scatter.finish()


def apply_norm(x, params, b, j):
    xhat, _ = standardize(x)
    row = 2 * b + j
    return (xhat * params[row : row + 1] + params[4 + row : 5 + row]).astype(BF)


ALL_ROWS = pl.ds(0, RP)


def up_gelu(hidden, w_up, act, slope, rows=ALL_ROWS):
    def step(j, carry):
        cols = tile(j)
        pre = dot(hidden[rows, :], w_up[:, cols])
        cdf = 0.5 * (1.0 + lax.erf(pre * (0.5**0.5)))
        act[rows, cols] = (pre * cdf).astype(BF)
        slope[rows, cols] = cdf + pre * jnp.exp(-0.5 * pre * pre) * 0.3989422804014327
        return carry

    lax.fori_loop(0, w_up.shape[1] // WIDE, step, 0)


def times(left, weights, part, rows=ALL_ROWS):
    def step(j, carry):
        cols = tile(j)
        part[rows, cols] = dot(left[rows, :], weights[:, cols]).astype(BF)
        return carry

    lax.fori_loop(0, weights.shape[1] // WIDE, step, 0)


def times_turned(left, weights, part, rows=ALL_ROWS):
    def step(j, carry):
        part[rows, tile(j)] = dot_cols(left[rows, :], weights[tile(j), :]).astype(BF)
        return carry

    lax.fori_loop(0, weights.shape[0] // WIDE, step, 0)


def mlp_back(dmlp, w_down, slope, dpre, rows=ALL_ROWS):
    def step(j, carry):
        cols = tile(j)
        dact = dot_cols(dmlp[rows, :], w_down[cols, :])
        dpre[rows, cols] = (dact * slope[rows, cols]).astype(BF)
        return carry

    lax.fori_loop(0, w_down.shape[0] // WIDE, step, 0)


def attention_input_back(dproj, w_qkv, part):
    def step(j, carry):
        rows = tile(j)
        total = dot_cols(dproj[0], w_qkv[0, rows, :])
        total = total + dot_cols(dproj[1], w_qkv[1, rows, :])
        total = total + dot_cols(dproj[2], w_qkv[2, rows, :])
        part[:, rows] = total.astype(BF)
        return carry

    lax.fori_loop(0, w_qkv.shape[1] // WIDE, step, 0)


def up_grad(r, left, right, out):
    def step(j, carry):
        value = dot_rows(left[:, tile(j)], right[...]).astype(BF)
        if r.fast:
            out[0, j] = value[: WIDE // 2]
            out[1, j] = value[WIDE // 2 :]
        else:
            out[tile(j), :] = value
        return carry

    lax.fori_loop(0, left.shape[1] // WIDE, step, 0)


def down_grad(r, left, right, out):
    def step(j, carry):
        value = dot_rows(left[:, tile(j)], right[...]).astype(BF)
        if r.fast:
            for piece in range(8):
                out[piece % 2, piece // 2, tile(j), :] = value[:, 128 * piece : 128 * piece + 128]
        else:
            out[tile(j), :] = value
        return carry

    lax.fori_loop(0, left.shape[1] // WIDE, step, 0)


def qkv_grad(r, hidden, dproj, out):
    def step(j, carry):
        left = hidden[:, tile(j)]
        for c in range(3):
            value = dot_rows(left, dproj[c]).astype(BF)
            if r.fast:
                out[0, j, c] = value[: WIDE // 2]
                out[1, j, c] = value[WIDE // 2 :]
            else:
                out[c, tile(j), :] = value
        return carry

    lax.fori_loop(0, hidden.shape[1] // WIDE, step, 0)


class SeqSum:
    def __init__(self, r, name, b, number):
        self.r, self.name, self.b = r, name, b
        self.mine = getattr(r, NAMES.d_ + name)
        self.first = getattr(r, NAMES.first_ + name)
        self.second = getattr(r, NAMES.second_ + name).at[b]
        self.sems = (r.sum_send.at[number], r.sum_recv.at[number])
        self.number = number

    def across(self):
        r = self.r
        send, recv = self.sems
        return remote(self.mine.at[1 - r.core], self.first, send.at[0], recv.at[0], r.sibling)

    def toward(self, d):
        r = self.r
        send, recv = self.sems
        chip = r.chip(d)
        return remote(
            self.mine.at[r.core, chip], self.second.at[d - 1], send.at[d], recv.at[d], r.chip_device(chip)
        )

    def start(self):
        self.across().start()

    def pass_on(self):
        self.across().wait()
        core = self.r.core
        for chip in range(4):
            total = self.mine[core, chip].astype(F32) + self.first[chip].astype(F32)
            self.mine[core, chip] = total.astype(BF)
        for d in (2, 1, 3):
            self.toward(d).start()

    def store(self):
        r = self.r
        held, out = getattr(r, NAMES.held_ + self.name), getattr(r, NAMES.grad_w_ + self.name)
        return pltpu.make_async_copy(held.at[self.b], out.at[self.b], r.store_sem.at[self.number])

    def finish(self):
        for d in (1, 3, 2):
            self.toward(d).wait()
        total = self.mine[self.r.core, self.r.a].astype(F32)
        for d in range(3):
            total = total + self.second[d].astype(F32)
        getattr(self.r, NAMES.held_ + self.name)[self.b] = total
        self.store().start()


class WholeOut:
    def __init__(self, r, number):
        self.r = r
        self.full = r.wof
        self.z_sems = r.line_sems(number)
        self.sems = (r.wo_send.at[number - 20], r.wo_recv.at[number - 20])

    def fetch(self, b):
        r = self.r
        part = r.wo_part.shape[0]
        rows = r.w_out.at[b, pl.ds(pl.multiple_of(r.s * part, part), part)]
        return pltpu.make_async_copy(rows, r.wo_part, r.fetch_sem.at[4])

    def line_copy(self, d, source):
        s, z, send, recv = self.z_sems
        owner = lax.rem(z + NZ - d, NZ) if source else z
        device = (s, owner if source else lax.rem(z + d, NZ))
        return remote(self.r.wo_part, self.full.at[owner, s], send.at[d - 1], recv.at[d - 1], device)

    def start(self, b):
        r = self.r
        self.fetch(b).wait()
        self.full[r.z, r.s] = r.wo_part[...]
        for d in range(1, NZ):
            self.line_copy(d, False).start()

    def chip_copy(self, d):
        send, recv = self.sems
        mine = self.full.at[:, self.r.s]
        return remote(mine, mine, send.at[d - 1], recv.at[d - 1], self.r.chip_device(self.r.chip(d)))

    def core_copy(self, d):
        send, recv = self.sems
        held = self.full.at[:, 2 * self.r.chip(4 - d) + self.r.core]
        return remote(held, held, send.at[3 + d], recv.at[3 + d], self.r.sibling)

    def pass_on(self):
        for d in range(1, NZ):
            self.line_copy(d, True).wait_recv()
        for d in (2, 1, 3):
            self.chip_copy(d).start()
        self.core_copy(0).start()
        for d in range(1, NZ):
            self.line_copy(d, False).wait_send()

    def cross(self):
        send, recv = self.sems
        for d in (1, 3, 2):
            there = self.full.at[:, 2 * self.r.chip(4 - d) + self.r.core]
            device = self.r.chip_device(self.r.chip(4 - d))
            remote(there, there, send.at[d - 1], recv.at[d - 1], device).wait_recv()
            self.core_copy(d).start()

    def finish(self):
        send, recv = self.sems
        for d in range(4):
            there = self.full.at[:, 2 * self.r.chip(4 - d) + 1 - self.r.core]
            remote(there, there, send.at[3 + d], recv.at[3 + d], self.r.sibling).wait_recv()
        for d in range(1, 4):
            self.chip_copy(d).wait_send()
        for d in range(4):
            self.core_copy(d).wait_send()


def own_branch(r, rows, out):
    def step(j, carry):
        cols = tile(j)
        out[:, cols] = dot(rows[...], r.wof[:, :, :, cols].reshape(NZ * WIDE, WIDE))
        return carry

    lax.fori_loop(0, r.wof.shape[3] // WIDE, step, 0)


def own_attended_grad(r, value, out):
    for part in range(NZ):
        weights = r.wof[part].reshape(WIDE, r.wof.shape[3])
        out[:, WIDE * part : WIDE * part + WIDE] = dot_cols(value, weights).astype(BF)


def heads_back(r, raw, dq, dk, dv, b, dproj):
    means = head_means()
    row = 2 * b
    for c, dy in ((0, dq * (HD ** (-0.5))), (1, dk)):
        xhat, rstd = head_standardize(raw[c], means)
        gain_row = r.head_params[row + c : row + c + 1]
        draw, gain, bias = head_back(dy, xhat, rstd, gain_row, means)
        dproj[c] = draw.astype(BF)
        r.head_sums[4 * b + c : 4 * b + c + 1] = gain
        r.head_sums[4 * b + 2 + c : 4 * b + 3 + c] = bias
    dproj[2] = dv.astype(BF)


def scale_grad(r, b, j, g, branch):
    valid = own_valid(r.z)
    row = 8 + 2 * b + j
    r.sums[row : row + 1] = jnp.sum(jnp.where(valid, g * branch, 0.0), axis=0, keepdims=True)


def through_norm(r, b, j, x, dnorm, g):
    valid = own_valid(r.z)
    row = 2 * b + j
    dv, gain, bias = norm_back(dnorm, x[...], r.params_full[row : row + 1], valid)
    r.sums[row : row + 1] = gain
    r.sums[4 + 2 * j + b : 5 + 2 * j + b] = bias
    return jnp.where(valid, g + dv, 0.0)


def start_phase(r):
    for name in (NAMES.wq, NAMES.wo, NAMES.wu, NAMES.wd):
        r.prefetch(name, 0)


def put_padded(r, source, full):
    full[pl.ds(CH * NZ, RP - CH * NZ), tile(r.z)] = jnp.zeros((RP - CH * NZ, WIDE), BF)
    full[pl.ds(0, TOK), tile(r.z)] = source[...]


def block_zero_phase(r, whole_out=None):
    s, z = r.s, r.z
    tokens_at, params_at, out_at, mid_at, mlp_at, next_at = (r.line_sems(i) for i in range(6))
    r.params_full[:, tile(z)] = r.params[...]
    put_padded(r, r.tokens, r.every)
    line_params = Gather(by_columns(r.params_full), *params_at)
    line_tokens = Gather(by_columns(r.every), *tokens_at)
    line_params.start()
    line_tokens.start()
    line_tokens.sent()
    line_params.sent()
    line_params.finish()
    line_tokens.finish()
    if r.fast:
        whole_out.start(1)
    params = r.params_full

    r.h0[...] = apply_norm(r.every[...].astype(F32), params, 0, 0)
    r.x0[...] = r.every[own_rows(z)].astype(F32)
    project(r, 0, r.h0, r.need(NAMES.wq, 0), r.raw0, r.q0, r.k0, r.v0)
    r.prefetch(NAMES.wq, 1)

    heads = lane_head(RP)
    keep = key_valid()
    queries = r.q0[...].astype(F32)
    attended = jnp.zeros((RP, WIDE), F32)
    for h in range(WIDE // HD):
        qh = jnp.where(heads == h, queries, 0.0).astype(BF)
        scores = jnp.where(keep, dot_cols(qh, r.k0[...]), NEG)
        expo = jnp.exp(scores - jnp.max(scores, axis=1, keepdims=True))
        probs = (expo * (1.0 / jnp.sum(expo, axis=1, keepdims=True))).astype(BF)
        attended = jnp.where(heads == h, dot(probs, r.v0[...]), attended)
    r.att0[...] = attended.astype(BF)

    times(r.att0, r.need(NAMES.wo, 0), r.part)
    branch = sum_rows(r, out_at)
    if r.fast:
        whole_out.pass_on()
    r.br0[...] = branch
    mid = r.x0[...] + params[8:9] * branch
    r.x1[...] = mid
    put_own(r.m0, z, apply_norm(mid, params, 0, 1))
    w_up, w_down = r.need(NAMES.wu, 0), r.need(NAMES.wd, 0)

    def mlp(rows):
        up_gelu(r.m0, w_up, r.act0, r.slope0, rows)
        times(r.act0, w_down, r.part, rows)

    def fetch_next():
        if r.fast:
            r.prefetch(NAMES.wu, 1)
            r.prefetch(NAMES.wd, 1)
            whole_out.cross()

    branch = pass_rows(r, r.m0, mid_at, mlp, mlp_at, (fetch_next,))
    r.mo0[...] = branch
    result = r.x1[...] + params[9:10] * branch
    r.x2[...] = result
    put_own(r.h1, z, apply_norm(result, params, 1, 0))
    w_qkv = r.need(NAMES.wq, 1)
    pass_rows(r, r.h1, next_at, lambda rows: project(r, 1, r.h1, w_qkv, r.raw1, r.q1, r.k1, r.v1, rows))
    if r.fast:
        whole_out.finish()


def place(first):
    row = lax.broadcasted_iota(jnp.int32, (WIDE, 2 * WIDE), 0)
    col = lax.broadcasted_iota(jnp.int32, (WIDE, 2 * WIDE), 1)
    within = lax.bitwise_and(col, 127)
    head = lax.shift_right_logical(col, 7)
    if first:
        return jnp.where((within < HD) & (row == head * HD + within), 1.0, 0.0).astype(BF)
    return jnp.where((within >= HD) & (row == head * HD + within - HD), 1.0, 0.0).astype(BF)


def swap_halves():
    row = lax.broadcasted_iota(jnp.int32, (2 * HD, 2 * HD), 0)
    col = lax.broadcasted_iota(jnp.int32, (2 * HD, 2 * HD), 1)
    return jnp.where(lax.bitwise_and(row + HD, 127) == col, 1.0, 0.0).astype(BF)


def pieces(x):
    high = x.astype(BF).astype(F32)
    middle = (x - high).astype(BF).astype(F32)
    return high, middle, x - high - middle


def key_lanes(r, f):
    count = r.frame_counts.shape[0]
    lane = lax.broadcasted_iota(jnp.int32, (RP, 2 * HD), 1) - HD
    row = lax.broadcasted_iota(jnp.int32, (RP, 2 * HD), 0)
    other_scene = (lane < count) & (lane != r.scenes[f])
    padding = (lane == count) & (row >= TOK)
    numbers = (lane > count) & (lane <= count + 3)
    return jnp.where(other_scene | padding, NEG, jnp.where(numbers, -1.0, 0.0))


def query_lanes(r, f, minus=None):
    count = r.frame_counts.shape[0]
    lane = lax.broadcasted_iota(jnp.int32, (RP, 2 * HD), 1) - HD
    lanes = jnp.where((lane == r.scenes[f]) | (lane == count), 1.0, 0.0)
    if minus is not None:
        for number, piece in enumerate(pieces(minus)):
            lanes = jnp.where(lane == count + 1 + number, piece, lanes)
    return lanes


HALF_ROWS = 144


def pack_heads(x, out):
    lower, upper = dot(x, place(True)), dot(x, place(False))
    for c in range(4):
        lanes = slice(128 * c, 128 * c + 128)
        out[c] = (lower[:HALF_ROWS, lanes] + upper[RP - HALF_ROWS :, lanes]).astype(BF)


def unpack_heads(packed, out):
    lower, upper = place(True), place(False)
    top, bottom = 0.0, 0.0
    for c in range(4):
        lanes = slice(128 * c, 128 * c + 128)
        top = top + dot_cols(packed[c], lower[:, lanes])
        bottom = bottom + dot_cols(packed[c], upper[:, lanes])
    out[pl.ds(0, HALF_ROWS), :] = top.astype(out.dtype)
    out[pl.ds(HALF_ROWS, RP - HALF_ROWS), :] = bottom[2 * HALF_ROWS - RP :].astype(out.dtype)


def pack(x, swap):
    low = lane_head(HALF_ROWS, 2 * HD) == 0
    upper = dot(x[RP - HALF_ROWS :], swap)
    return jnp.where(low, x[:HALF_ROWS].astype(F32), upper).astype(BF)


def unpack(packed, swap, out, lanes=None):
    low = lane_head(HALF_ROWS, 2 * HD) == 0
    top, bottom = packed.astype(F32), dot(packed, swap)
    if lanes is not None:
        top, bottom = jnp.where(low, top, lanes), jnp.where(low, bottom, lanes)
    out[pl.ds(0, HALF_ROWS), :] = top.astype(BF)
    out[pl.ds(HALF_ROWS, RP - HALF_ROWS), :] = bottom[2 * HALF_ROWS - RP :].astype(BF)


def global_forward_phase(r):
    s, z, a, core, sibling = r.s, r.z, r.a, r.core, r.sibling
    qk, vv, ks = r.qk, r.vv, r.ks
    packed = dot(r.q1[...], place(True)) + dot(r.k1[...], place(False))
    for c in range(4):
        r.slabs[c] = packed[:, 128 * c : 128 * c + 128].astype(BF)
    pack_heads(r.v1[...], r.pairs)
    packed_values = r.packed_values

    def toward(d):
        c = r.chip(d)
        target = r.chip_device(c)
        return (
            remote(r.slabs.at[c], qk.at[s], r.f_send.at[0, d - 1], r.f_recv.at[0, d - 1], target),
            remote(r.pairs.at[c], packed_values.at[s], r.f_send.at[1, d - 1], r.f_recv.at[1, d - 1], target),
        )

    def arriving(d):
        source = 2 * r.chip(4 - d) + core
        device = (source, z)
        return (
            remote(qk.at[source], qk.at[source], r.f_send.at[0, d - 1], r.f_recv.at[0, d - 1], device),
            remote(packed_values.at[source], packed_values.at[source], r.f_send.at[1, d - 1], r.f_recv.at[1, d - 1], device),
            source,
        )

    def relay(d, frame):
        return (
            remote(qk.at[frame], qk.at[frame], r.fc_send.at[0, d], r.fc_recv.at[0, d], sibling),
            remote(packed_values.at[frame], packed_values.at[frame], r.fc_send.at[1, d], r.fc_recv.at[1, d], sibling),
        )

    for d in (2, 1, 3):
        for copy in toward(d):
            copy.start()
    put_padded(r, r.grad_out, r.grad_full)
    line_grads = Gather(by_columns(r.grad_full), *r.line_sems(6))
    line_grads.start()
    qk[s] = r.slabs[a]
    packed_values[s] = r.pairs[a]
    for copy in relay(0, s):
        copy.start()
    for d in (1, 3, 2):
        first, second, source = arriving(d)
        first.wait_recv()
        second.wait_recv()
        for copy in relay(d, source):
            copy.start()
    for d in range(4):
        frame = 2 * r.chip(4 - d) + 1 - core
        for copy in relay(d, frame):
            copy.wait_recv()
    line_grads.finish()
    swap = swap_halves()
    low_half = lane_head(RP, 2 * HD) == 0

    lane = lax.broadcasted_iota(jnp.int32, (HALF_ROWS, 2 * HD), 1)
    value_lanes = jnp.where((lane >= HD) & (lane < HD + 3), -1.0, 0.0)

    def turn(f, carry):
        turned = jnp.where(low_half, dot(qk[f], swap), key_lanes(r, f))
        ks[pl.ds(pl.multiple_of(f * RP, 16), RP), :] = turned.astype(BF)
        unpack(packed_values[f], swap, vv.at[f], value_lanes)
        return carry

    lax.fori_loop(0, 8, turn, 0)

    def back(d):
        target = r.chip(d)
        device = r.chip_device(target)
        return remote(r.outs.at[target], r.ins.at[a], r.fb_send.at[d - 1], r.fb_recv.at[d - 1], device)

    def attend(i):
        f = 2 * i + core
        qf = jnp.where(low_half, qk[f].astype(F32), query_lanes(r, f)).astype(BF)
        scores = dot_cols(qf, ks[...])
        peak = jnp.max(scores, axis=1, keepdims=True)
        expo = jnp.exp(scores - peak)
        total = jnp.sum(expo, axis=1, keepdims=True)
        product = dot(expo.astype(BF), vv[...].reshape(8 * RP, 2 * HD))
        attended = product * (1.0 / total)
        r.outs_full[i] = attended
        r.outs[i] = pack(attended.astype(BF), swap)
        r.lse[i] = jnp.broadcast_to(peak + jnp.log(total), (RP, 2 * HD))

    def attend_and_send(d, carry):
        attend(r.chip(d))
        back(d).start()
        return carry

    lax.fori_loop(1, 4, attend_and_send, 0)
    attend(a)
    r.ins[a] = r.outs[a]
    for d in (1, 3, 2):
        source = r.chip(4 - d)
        there = r.ins.at[source]
        remote(there, there, r.fb_send.at[d - 1], r.fb_recv.at[d - 1], r.chip_device(source)).wait_recv()
    unpack_heads(r.ins, r.att1)
    line_grads.sent()
    for d in (1, 2, 3):
        for copy in toward(d):
            copy.wait_send()
        back(d).wait_send()
    for copy in relay(0, s):
        copy.wait_send()
    for d in (1, 2, 3):
        for copy in relay(d, 2 * r.chip(4 - d) + core):
            copy.wait_send()


def middle_phase(r, sums_of=None):
    s, z = r.s, r.z
    params = r.params_full
    out_at, mid_at, dnorm_at, next_at = (r.line_sems(i) for i in (7, 8, 9, 11))
    valid = own_valid(z)
    if r.fast:
        rows_start(r.att1, r.att_in, *out_at)
        r.dmlp[...] = (r.grad_full[...].astype(F32) * params[11:12]).astype(BF)
        rows_wait(r.att1, r.att_in, *out_at)
        own_branch(r, r.att_in, r.br1)
        branch = r.br1[...]
    else:
        w_out = r.need(NAMES.wo, 1)
        times(r.att1, w_out, r.part)
        r.dmlp[...] = (r.grad_full[...].astype(F32) * params[11:12]).astype(BF)
        branch = sum_rows(r, out_at)
        r.br1[...] = branch
    mid = r.x2[...] + params[10:11] * branch
    r.x3[...] = mid
    put_own(r.m1, z, apply_norm(mid, params, 1, 1))
    w_up, w_down = r.need(NAMES.wu, 1), r.need(NAMES.wd, 1)

    def mlp(rows):
        up_gelu(r.m1, w_up, r.act1, r.slope1, rows)
        mlp_back(r.dmlp, w_down, r.slope1, r.dpre, rows)
        times_turned(r.dpre, w_up, r.part, rows)

    def first():
        down_grad(r, r.act1, r.dmlp, r.d_down)
        if r.fast:
            sums_of[NAMES.down].start()

    def second():
        up_grad(r, r.m1, r.dpre, r.d_up)
        if r.fast:
            sums_of[NAMES.up].start()
            r.prefetch(NAMES.wu, 0)
            sums_of[NAMES.down].pass_on()

    dnorm = pass_rows(r, r.m1, mid_at, mlp, dnorm_at, (first, second))
    g = jnp.where(valid, r.grad_full[own_rows(z)].astype(F32), 0.0)
    after = through_norm(r, 1, 1, r.x3, dnorm, g)
    r.g3[...] = after
    dbranch = (after * params[10:11]).astype(BF)
    put_own(r.dbr1, z, dbranch)
    if r.fast:
        own_attended_grad(r, dbranch, r.datt_own)
        features_start(r.datt_own, r.datt1, *r.line_sems(10))
        Gather(by_rows(r.dbr1), *next_at).start()
    scale_grad(r, 1, 0, after, r.br1[...])
    times(r.act1, w_down, r.part_out)
    if r.fast:
        r.prefetch(NAMES.wd, 0)
        features_wait(r.datt_own, r.datt1, *r.line_sems(10))
    else:
        share_rows(r, r.dbr1, next_at)
        r.datt1[...] = dot_cols(r.dbr1[...], w_out[...]).astype(BF)
        result_start(r)
        result_relay(r)
        result_end(r)


def result_start(r):
    Scatter(r.part_out, r.inbox.at[1], *r.line_sems(22)).start()


def result_relay(r):
    scatter = Scatter(r.part_out, r.inbox.at[1], *r.line_sems(22))
    scatter.sent()
    scatter.relay()


def result_end(r):
    z = r.z
    rows_at = r.line_sems(12)
    out_branch = Scatter(r.part_out, r.inbox.at[1], *r.line_sems(22)).finish()
    g = jnp.where(own_valid(z), r.grad_full[own_rows(z)].astype(F32), 0.0)
    scale_grad(r, 1, 1, g, out_branch)
    r.final_low[...] = (r.x3[...] + r.params_full[11:12] * out_branch).astype(BF)
    features_start(r.final_low, r.out_rows, *rows_at)
    if not r.fast:
        features_wait(r.final_low, r.out_rows, *rows_at)


def global_backward_phase(r, sums_of):
    s, z, a, core, sibling = r.s, r.z, r.a, r.core, r.sibling
    pack_heads(r.datt1[...], r.pairs)

    def toward(d):
        c = r.chip(d)
        return remote(r.pairs.at[c], r.dos.at[a], r.b_send.at[d - 1], r.b_recv.at[d - 1], r.chip_device(c))

    for d in (2, 1, 3):
        toward(d).start()
    r.dos[a] = r.pairs[a]
    r.dkt[...] = jnp.zeros_like(r.dkt)
    r.dvt[...] = jnp.zeros_like(r.dvt)
    for d in (1, 3, 2):
        source = r.chip(4 - d)
        there = r.dos.at[source]
        remote(there, there, r.b_send.at[d - 1], r.b_recv.at[d - 1], r.chip_device(source)).wait_recv()
    half = lane_head(RP, 2 * HD)
    low_half = half == 0
    swap = swap_halves()
    ks, vv = r.ks, r.vv

    lane = lax.broadcasted_iota(jnp.int32, (RP, 2 * HD), 1)

    def step(i, carry):
        f = 2 * i + core
        lanes = query_lanes(r, f, r.lse[i][:, 0:1])
        qf = jnp.where(low_half, r.qk[f].astype(F32), lanes).astype(BF)
        unpack(r.dos[i], swap, r.do_rows, 0.0)
        do = r.do_rows[...].astype(F32)
        delta = jnp.sum(do * r.outs_full[i], axis=1, keepdims=True)
        for number, piece in enumerate(pieces(delta)):
            do = jnp.where(lane == HD + number, piece, do)
        do = do.astype(BF)
        probs = jnp.exp(dot_cols(qf, ks[...]))
        dprobs = dot_cols(do, vv[...].reshape(8 * RP, 2 * HD))
        dscores = (probs * dprobs).astype(BF)
        r.dq_mine[i] = dot(dscores, ks[...])
        r.dkt[...] += dot_rows(qf, dscores)
        r.dvt[...] += dot_rows(do, probs.astype(BF))
        return carry

    line_dbr = Gather(by_rows(r.dbr1), *r.line_sems(11))
    line_dbr.sent()
    lax.fori_loop(0, 2, step, 0)
    line_dbr.finish()
    result_start(r)
    lax.fori_loop(2, 4, step, 0)
    r.dk_sum[...] = jnp.transpose(r.dkt[...])
    r.dv_sum[...] = jnp.transpose(r.dvt[...])

    def rows_of(frame):
        return pl.ds(pl.multiple_of(frame * RP, 16), RP)

    for i in range(4):
        theirs = rows_of(2 * i + 1 - core)
        dv = dot(r.dv_sum[theirs, :].astype(BF), swap)
        r.dkv_send[i] = jnp.where(low_half, r.dk_sum[theirs, :], dv).astype(BF)
    across = remote(r.dkv_send, r.dkv_in, r.bc_send.at[0], r.bc_recv.at[0], sibling)
    across.start()
    down_grad(r, r.att1, r.dbr1, r.d_out)
    sums_of[NAMES.out].start()
    result_relay(r)
    across.wait()
    for i in range(4):
        own = rows_of(2 * i + core)
        dk = (r.dk_sum[own, :] + r.dkv_in[i].astype(F32)).astype(BF)
        dv = r.dv_sum[own, :] + dot(r.dkv_in[i], swap)
        r.ready[i] = jnp.where(low_half, r.dq_mine[i], dot(dk, swap)).astype(BF)
        r.ready_values[i] = pack(dv.astype(BF), swap)

    def back(d):
        target = r.chip(d)
        device = r.chip_device(target)
        return (
            remote(r.ready.at[target], r.dqk_in.at[a], r.bb_send.at[0, d - 1], r.bb_recv.at[0, d - 1], device),
            remote(r.ready_values.at[target], r.dv_in.at[a], r.bb_send.at[1, d - 1], r.bb_recv.at[1, d - 1], device),
        )

    for d in (2, 1, 3):
        for copy in back(d):
            copy.start()
    r.dqk_in[a] = r.ready[a]
    r.dv_in[a] = r.ready_values[a]
    for d in (1, 3, 2):
        source = r.chip(4 - d)
        for number, box in ((0, r.dqk_in), (1, r.dv_in)):
            there = box.at[source]
            sems = (r.bb_send.at[number, d - 1], r.bb_recv.at[number, d - 1])
            remote(there, there, *sems, r.chip_device(source)).wait_recv()
    to_q, to_k = place(True), place(False)
    dq = jnp.zeros((RP, WIDE), F32)
    dk = jnp.zeros((RP, WIDE), F32)
    for c in range(4):
        cols = slice(128 * c, 128 * c + 128)
        dq = dq + dot_cols(r.dqk_in[c], to_q[:, cols])
        dk = dk + dot_cols(r.dqk_in[c], to_k[:, cols])
    r.dq[...] = dq
    r.dk[...] = dk
    unpack_heads(r.dv_in, r.dv)
    for d in (1, 2, 3):
        toward(d).wait_send()
        for copy in back(d):
            copy.wait_send()


def attention_back_phase(r, sums_of=None):
    s, z = r.s, r.z
    if r.fast:
        sums_of[NAMES.up].pass_on()
    dnorm_at, next_at = r.line_sems(13), r.line_sems(14)
    heads_back(r, r.raw1, r.dq[...], r.dk[...], r.dv[...], 1, r.dproj)
    if r.fast:
        result_end(r)
    attention_input_back(r.dproj, r.need(NAMES.wq, 1), r.part)

    def first():
        qkv_grad(r, r.h1, r.dproj, r.d_qkv)
        if r.fast:
            r.prefetch(NAMES.wq, 0)
            sums_of[NAMES.qkv].start()

    def second():
        if r.fast:
            sums_of[NAMES.out].pass_on()

    dnorm = sum_rows(r, dnorm_at, (first, second))
    after = through_norm(r, 1, 0, r.x2, dnorm, r.g3[...])
    r.g5[...] = after
    put_own(r.dm0, z, (after * r.params_full[9:10]).astype(BF))
    if r.fast:
        sums_of[NAMES.qkv].pass_on()
    else:
        share_rows(r, r.dm0, next_at)
    scale_grad(r, 0, 1, after, r.mo0[...])


def mlp_back_phase(r, sums_of=None, earlier=None):
    s, z = r.s, r.z
    dnorm_at, next_at = r.line_sems(15), r.line_sems(16)
    w_down, w_up = r.need(NAMES.wd, 0), r.need(NAMES.wu, 0)

    def back(rows):
        mlp_back(r.dm0, w_down, r.slope0, r.dpre, rows)
        times_turned(r.dpre, w_up, r.part, rows)

    def first():
        if r.fast:
            earlier[NAMES.down].finish()
        down_grad(r, r.act0, r.dm0, r.d_down)
        if r.fast:
            sums_of[NAMES.down].start()

    def second():
        if r.fast:
            earlier[NAMES.up].finish()
        up_grad(r, r.m0, r.dpre, r.d_up)
        if r.fast:
            sums_of[NAMES.up].start()
            sums_of[NAMES.down].pass_on()

    if r.fast:
        dnorm = pass_rows(r, r.dm0, r.line_sems(14), back, dnorm_at, (first, second))
    else:
        back(ALL_ROWS)
        dnorm = sum_rows(r, dnorm_at, (first, second))
    after = through_norm(r, 0, 1, r.x1, dnorm, r.g5[...])
    r.g6[...] = after
    put_own(r.dbr0, z, (after * r.params_full[8:9]).astype(BF))
    gather = Gather(by_rows(r.dbr0), *next_at)
    gather.start()
    scale_grad(r, 0, 0, after, r.br0[...])
    if r.fast:
        sums_of[NAMES.up].pass_on()
    gather.sent()
    gather.finish()


def last_phase(r, sums_of=None, earlier=None):
    s, z = r.s, r.z
    dnorm_at, rows_at, notes_at = (r.line_sems(i) for i in range(17, 20))
    valid = own_valid(z)
    datt = dot_cols(r.dbr0[...], r.need(NAMES.wo, 0)[...]).astype(BF).astype(F32)
    heads = lane_head(RP)
    keep = key_valid()
    queries = r.q0[...].astype(F32)
    dq = jnp.zeros((RP, WIDE), F32)
    dk = jnp.zeros((RP, WIDE), F32)
    dv = jnp.zeros((RP, WIDE), F32)
    for h in range(WIDE // HD):
        here = heads == h
        qh = jnp.where(here, queries, 0.0).astype(BF)
        do = jnp.where(here, datt, 0.0).astype(BF)
        scores = jnp.where(keep, dot_cols(qh, r.k0[...]), NEG)
        expo = jnp.exp(scores - jnp.max(scores, axis=1, keepdims=True))
        probs = expo * (1.0 / jnp.sum(expo, axis=1, keepdims=True))
        dprobs = dot_cols(do, r.v0[...])
        delta = jnp.sum(probs * dprobs, axis=1, keepdims=True)
        dscores = (probs * (dprobs - delta)).astype(BF)
        dq = jnp.where(here, dot(dscores, r.k0[...]), dq)
        dk = dk + dot_rows(dscores, qh)
        dv = dv + dot_rows(probs.astype(BF), do)
    heads_back(r, r.raw0, dq, dk, dv, 0, r.dproj)
    attention_input_back(r.dproj, r.need(NAMES.wq, 0), r.part)

    def first():
        if r.fast:
            earlier[NAMES.qkv].finish()
        qkv_grad(r, r.h0, r.dproj, r.d_qkv)
        if r.fast:
            sums_of[NAMES.qkv].start()

    def second():
        if r.fast:
            earlier[NAMES.out].finish()
        down_grad(r, r.att0, r.dbr0, r.d_out)
        if r.fast:
            sums_of[NAMES.out].start()
            sums_of[NAMES.qkv].pass_on()
            sums_of[NAMES.out].pass_on()
            sums_of[NAMES.down].finish()
            sums_of[NAMES.up].finish()

    dnorm = sum_rows(r, dnorm_at, (first, second))
    r.final[...] = through_norm(r, 0, 0, r.x0, dnorm, r.g6[...]).astype(BF)
    for p in range(NZ):
        r.messages[p, 0:16] = r.sums[:, WIDE * p : WIDE * p + WIDE]
        r.messages[p, 16:24] = r.head_sums[...]

    def note(d):
        send, recv = notes_at[2:]
        peer = lax.rem(z + d, NZ)
        return remote(r.messages.at[peer], r.letters.at[d - 1], send.at[d - 1], recv.at[d - 1], (s, peer))

    for d in range(1, NZ):
        note(d).start()
    features_start(r.final, r.grad_rows, *rows_at)
    for d in range(1, NZ):
        note(d).wait()
    r.small[...] = r.messages[z] + r.letters[0] + r.letters[1] + r.letters[2]
    if not r.fast:
        features_wait(r.final, r.grad_rows, *rows_at)


def small_phase(r):
    pair = remote(r.small, r.small_in.at[0], r.small_send.at[0], r.small_recv.at[0], r.sibling)
    pair.start()
    pair.wait()
    r.small_two[...] = r.small[...] + r.small_in[0]

    def toward(d):
        device = r.chip_device(r.chip(d))
        return remote(r.small_two, r.small_in.at[d], r.small_send.at[d], r.small_recv.at[d], device)

    for d in range(1, 4):
        toward(d).start()
    for d in range(1, 4):
        toward(d).wait()
    boxes = [r.small_two[...], r.small_in[1], r.small_in[2], r.small_in[3]]
    total = None
    for chip in range(4):
        distance = lax.rem(r.a + 4 - chip, 4)
        term = boxes[0]
        for d in range(1, 4):
            term = jnp.where(distance == d, boxes[d], term)
        total = term if total is None else total + term
    r.small_out[...] = total


def gather_params(r):
    for b in range(2):
        r.params[2 * b : 2 * b + 2] = r.block_norm_multiplier[b]
        r.params[4 + 2 * b : 6 + 2 * b] = r.block_norm_bias[b]
        r.params[8 + 2 * b : 10 + 2 * b] = r.layer_scale[b]
        for h in range(WIDE // HD):
            lanes = slice(HD * h, HD * h + HD)
            r.head_params[2 * b : 2 * b + 2, lanes] = r.qk_gain[b]
            r.head_params[4 + 2 * b : 6 + 2 * b, lanes] = r.qk_bias[b]
    r.params[12:16] = jnp.zeros((4, WIDE), F32)


def find_scenes(r):
    for slot in range(r.slot_frames.shape[0]):
        frame = r.slot_frames[slot]
        end, scene = 0, 0
        for number in range(r.frame_counts.shape[0]):
            end = end + r.frame_counts[number]
            scene = scene + jnp.where(end <= frame, 1, 0)
        r.scenes[slot] = scene


def whole_kernel(names, *refs):
    r = Refs(names, refs, True)
    gather_params(r)
    start_phase(r)
    greet(line(r.s, r.z) + [r.chip_device(r.chip(d)) for d in range(1, 4)] + [r.sibling])
    numbers = {NAMES.down: 0, NAMES.up: 1, NAMES.out: 2, NAMES.qkv: 3}
    later = {name: SeqSum(r, name, 1, number) for name, number in numbers.items()}
    sooner = {name: SeqSum(r, name, 0, 4 + number) for name, number in numbers.items()}
    r.sums[...] = jnp.zeros_like(r.sums)
    r.head_sums[...] = jnp.zeros_like(r.head_sums)
    find_scenes(r)
    whole_out = WholeOut(r, 20)
    whole_out.fetch(1).start()
    block_zero_phase(r, whole_out)
    global_forward_phase(r)
    middle_phase(r, later)
    global_backward_phase(r, later)
    attention_back_phase(r, later)
    features_wait(r.final_low, r.out_rows, *r.line_sems(12))
    mlp_back_phase(r, sooner, later)
    last_phase(r, sooner, later)
    small_phase(r)
    features_wait(r.final, r.grad_rows, *r.line_sems(18))
    sooner[NAMES.qkv].finish()
    sooner[NAMES.out].finish()
    for total in (*later.values(), *sooner.values()):
        total.store().wait()


def plain_kernel(phase, names, fresh, weights, *refs):
    r = Refs(names, refs, False)
    greet(line(r.s, r.z))
    for name in fresh:
        getattr(r, name)[...] = jnp.zeros_like(getattr(r, name))
    if phase is block_zero_phase:
        start_phase(r)
    if phase is last_phase:
        r.sums[...] = r.sums_in[...]
        r.head_sums[...] = r.head_sums_in[...]
    phase(r)


def results_kernel(
    out_rows,
    grad_rows,
    small,
    qkv_in,
    out_in,
    up_in,
    down_in,
    out_tokens,
    grad_tokens,
    gains,
    norm_bias,
    mlp_bias,
    head_gain,
    head_bias,
    scales,
    qkv,
    out,
    up,
    down,
    qkv_held,
    out_held,
    up_held,
    down_held,
    out_rows_held,
    grad_rows_held,
    small_held,
    sems,
):
    sources = (qkv_in, out_in, up_in, down_in, out_rows, grad_rows, small)
    held = (qkv_held, out_held, up_held, down_held, out_rows_held, grad_rows_held, small_held)
    loads = [pltpu.make_async_copy(sources[i], held[i], sems.at[0, i]) for i in range(7)]
    for copy in (loads[4], loads[5], loads[6], *loads[:4]):
        copy.start()
    stores = [
        pltpu.make_async_copy(held[i], target, sems.at[1, i]) for i, target in enumerate((qkv, out, up, down))
    ]
    for load, store in zip(loads, stores):
        load.wait()
        store.start()
    for copy in loads[4:]:
        copy.wait()
    out_rows, grad_rows, small = held[4:]
    out_tokens[...] = out_rows[pl.ds(0, TOK)]
    grad_tokens[...] = grad_rows[pl.ds(0, TOK)].astype(F32)
    for b in range(2):
        gains[b] = small[2 * b : 2 * b + 2]
        scales[b] = small[8 + 2 * b : 10 + 2 * b]
    norm_bias[...] = small[4:6]
    mlp_bias[...] = small[6:8]
    row = lax.broadcasted_iota(jnp.int32, (WIDE, HD), 0)
    col = lax.broadcasted_iota(jnp.int32, (WIDE, HD), 1)
    fold = jnp.where(lax.bitwise_and(row, HD - 1) == col, 1.0, 0.0).astype(F32)
    heads = jnp.dot(small[16:24], fold, precision=HIGH, preferred_element_type=F32)
    for b in range(2):
        head_gain[b] = heads[4 * b : 4 * b + 2]
        head_bias[b] = heads[4 * b + 2 : 4 * b + 4]
    for store in stores:
        store.wait()


def gather_frames(rows):
    return lax.all_gather(rows, "seq", axis=0)


def global_forward_plain(query_rows, key_rows, value_rows, allowed_frames):
    head_count = query_rows.shape[1]
    state = (
        jnp.full((head_count, TOK), NEG, F32),
        jnp.zeros((head_count, TOK), F32),
        jnp.zeros((head_count, TOK, HD), F32),
    )

    def advance(running, item):
        key_block, value_block, allowed = item

        def update(current):
            peak, totals, weighted = current
            scores = jnp.einsum("qhd,khd->hqk", query_rows, key_block, preferred_element_type=F32)
            new_peak = jnp.maximum(peak, jnp.max(scores, axis=-1))
            expo = jnp.exp(scores - new_peak[..., None])
            factor = jnp.exp(peak - new_peak)
            totals = totals * factor + jnp.sum(expo, axis=-1)
            weighted = weighted * factor[..., None] + jnp.einsum(
                "hqk,khd->hqd", expo.astype(BF), value_block, preferred_element_type=F32
            )
            return (new_peak, totals, weighted)

        return (lax.cond(allowed, update, lambda current: current, running), None)

    (peak, totals, weighted), _ = lax.scan(
        advance, state, (gather_frames(key_rows), gather_frames(value_rows), allowed_frames)
    )
    attended = jnp.transpose(weighted / totals[..., None], (1, 0, 2))
    return attended, peak + jnp.log(totals)


def global_backward_plain(query_rows, key_rows, value_rows, out_grad, attended, lse, allowed_frames):
    delta = jnp.transpose(jnp.sum(attended * out_grad.astype(F32), axis=-1))
    zero = jnp.zeros(query_rows.shape, F32)

    def pieces(q, do, stat, row_sum, k, v):
        scores = jnp.einsum("qhd,khd->hqk", q, k, preferred_element_type=F32)
        probs = jnp.exp(scores - stat[..., None])
        dprobs = jnp.einsum("qhd,khd->hqk", do, v, preferred_element_type=F32)
        return probs.astype(BF), (probs * (dprobs - row_sum[..., None])).astype(BF)

    def advance_query(total, item):
        k, v, allowed = item

        def update(current):
            _, dscores = pieces(query_rows, out_grad, lse, delta, k, v)
            return current + jnp.einsum("hqk,khd->qhd", dscores, k, preferred_element_type=F32)

        return (lax.cond(allowed, update, lambda current: current, total), None)

    dq, _ = lax.scan(
        advance_query, zero, (gather_frames(key_rows), gather_frames(value_rows), allowed_frames)
    )

    def advance_keys(totals, item):
        q, do, stat, row_sum, allowed = item

        def update(current):
            probs, dscores = pieces(q, do, stat, row_sum, key_rows, value_rows)
            return (
                current[0] + jnp.einsum("hqk,qhd->khd", dscores, q, preferred_element_type=F32),
                current[1] + jnp.einsum("hqk,qhd->khd", probs, do, preferred_element_type=F32),
            )

        return (lax.cond(allowed, update, lambda current: current, totals), None)

    (dk, dv), _ = lax.scan(
        advance_keys,
        (zero, zero),
        (
            gather_frames(query_rows),
            gather_frames(out_grad),
            gather_frames(lse),
            gather_frames(delta),
            allowed_frames,
        ),
    )
    return dq, dk, dv


def buffers(depth, hidden):
    rows_d = ((RP, depth), BF)
    rows_w = ((RP, WIDE), BF)
    wide_f = ((RP, WIDE), F32)
    own_f = ((RO, depth), F32)
    raw = ((2, RP, WIDE), F32)
    slab = (RP, 2 * HD)
    table = {
        NAMES.params_full: ((16, depth), F32),
        NAMES.every: rows_d,
        NAMES.wof: ((NZ, 8, WIDE // 8, depth), BF),
        NAMES.wo_part: ((WIDE // 8, depth), BF),
        NAMES.att_in: ((RO, depth), BF),
        NAMES.datt_own: ((RO, depth), BF),
        NAMES.part: rows_d,
        NAMES.part_out: rows_d,
        NAMES.inbox: ((2, 4, RO, depth), BF),
        NAMES.wq: ((3, depth, WIDE), BF),
        NAMES.wo: ((WIDE, depth), BF),
        NAMES.wu: ((depth, hidden), BF),
        NAMES.wd: ((hidden, depth), BF),
        NAMES.act0: ((RP, hidden), BF),
        NAMES.act1: ((RP, hidden), BF),
        NAMES.slope0: ((RP, hidden), F32),
        NAMES.slope1: ((RP, hidden), F32),
        NAMES.dpre: ((RP, hidden), BF),
        NAMES.final_low: ((RO, depth), BF),
        NAMES.final: ((RO, depth), BF),
        NAMES.dproj: ((3, RP, WIDE), BF),
        NAMES.sums: ((16, depth), F32),
        NAMES.head_sums: ((8, WIDE), F32),
        NAMES.messages: ((NZ, 24, WIDE), F32),
        NAMES.letters: ((NZ - 1, 24, WIDE), F32),
        NAMES.small: ((24, WIDE), F32),
        NAMES.small_two: ((24, WIDE), F32),
        NAMES.small_in: ((4, 24, WIDE), F32),
        NAMES.qk: ((8,) + slab, BF),
        NAMES.vv: ((8,) + slab, BF),
        NAMES.ks: ((8 * RP, 2 * HD), BF),
        NAMES.lse: ((4,) + slab, F32),
        NAMES.slabs: ((4,) + slab, BF),
        NAMES.pairs: ((4, HALF_ROWS, 2 * HD), BF),
        NAMES.outs: ((4, HALF_ROWS, 2 * HD), BF),
        NAMES.outs_full: ((4,) + slab, F32),
        NAMES.ins: ((4, HALF_ROWS, 2 * HD), BF),
        NAMES.dos: ((4, HALF_ROWS, 2 * HD), BF),
        NAMES.dkt: ((2 * HD, 8 * RP), F32),
        NAMES.dvt: ((2 * HD, 8 * RP), F32),
        NAMES.dq_mine: ((4,) + slab, F32),
        NAMES.dk_sum: ((8 * RP, 2 * HD), F32),
        NAMES.dv_sum: ((8 * RP, 2 * HD), F32),
        NAMES.dkv_send: ((4,) + slab, BF),
        NAMES.dkv_in: ((4,) + slab, BF),
        NAMES.ready: ((4,) + slab, BF),
        NAMES.ready_values: ((4, HALF_ROWS, 2 * HD), BF),
        NAMES.packed_values: ((8, HALF_ROWS, 2 * HD), BF),
        NAMES.do_rows: (slab, BF),
        NAMES.dqk_in: ((4,) + slab, BF),
        NAMES.dv_in: ((4, HALF_ROWS, 2 * HD), BF),
        NAMES.out_rows: rows_w,
        NAMES.grad_rows: rows_w,
    }
    for name in (NAMES.q0, NAMES.k0, NAMES.v0, NAMES.att0, NAMES.q1, NAMES.k1, NAMES.v1, NAMES.att1, NAMES.datt1):
        table[name] = rows_w
    for name in (NAMES.dq, NAMES.dk, NAMES.dv):
        table[name] = wide_f
    for name in (NAMES.h0, NAMES.m0, NAMES.h1, NAMES.m1, NAMES.grad_full, NAMES.dmlp, NAMES.dbr1, NAMES.dm0, NAMES.dbr0):
        table[name] = rows_d
    for name in (NAMES.x0, NAMES.x1, NAMES.x2, NAMES.x3, NAMES.br0, NAMES.br1, NAMES.mo0, NAMES.g3, NAMES.g5, NAMES.g6):
        table[name] = own_f
    for name in (NAMES.raw0, NAMES.raw1):
        table[name] = raw
    piece = {
        NAMES.qkv: (3, depth // 8, WIDE),
        NAMES.out: (WIDE, depth // 8),
        NAMES.up: (depth // 8, hidden),
        NAMES.down: (hidden, depth // 8),
    }
    for name, shape in piece.items():
        table[NAMES.d_ + name] = ((2, 4) + shape, BF)
        table[NAMES.first_ + name] = ((4,) + shape, BF)
        table[NAMES.second_ + name] = ((2, 3) + shape, BF)
    return table


SEMAPHORES = {
    NAMES.fetch_sem: (5,),
    NAMES.z_send: (24, 4),
    NAMES.z_recv: (24, 4),
    NAMES.wo_send: (1, 7),
    NAMES.wo_recv: (1, 7),
    NAMES.f_send: (2, 3),
    NAMES.f_recv: (2, 3),
    NAMES.fc_send: (2, 4),
    NAMES.fc_recv: (2, 4),
    NAMES.fb_send: (3,),
    NAMES.fb_recv: (3,),
    NAMES.b_send: (3,),
    NAMES.b_recv: (3,),
    NAMES.bc_send: (1,),
    NAMES.bc_recv: (1,),
    NAMES.bb_send: (2, 3),
    NAMES.bb_recv: (2, 3),
    NAMES.store_sem: (8,),
    NAMES.sum_send: (8, 4),
    NAMES.sum_recv: (8, 4),
    NAMES.small_send: (4,),
    NAMES.small_recv: (4,),
}
GRADS = (NAMES.grad_w_qkv, NAMES.grad_w_out, NAMES.grad_w_up, NAMES.grad_w_down)
IN_HBM = (NAMES.w_qkv, NAMES.w_out, NAMES.w_up, NAMES.w_down)


def call(body, given, outs, scratch, collective_id, name, vmem_mib):
    names = list(given) + list(outs) + list(scratch)
    def room(shape, kind):
        if kind is None:
            return pltpu.SemaphoreType.DMA(shape)
        return pltpu.SMEM(shape, jnp.int32) if kind == NAMES.scalars else pltpu.VMEM(shape, kind)

    def space(key):
        if key in IN_HBM or key in GRADS:
            return pl.ANY
        return pltpu.SMEM if key in (NAMES.frame_counts, NAMES.slot_frames) else pltpu.VMEM

    scratch_shapes = [room(shape, kind) for shape, kind in scratch.values()]
    results = pl.pallas_call(
        partial(body, names),
        name=name,
        out_shape=[jax.ShapeDtypeStruct(shape, kind) for shape, kind in outs.values()],
        in_specs=[pl.BlockSpec(memory_space=space(key)) for key in given],
        out_specs=[pl.BlockSpec(memory_space=space(key)) for key in outs],
        scratch_shapes=scratch_shapes,
        compiler_params=pltpu.CompilerParams(
            collective_id=collective_id, has_side_effects=True, vmem_limit_bytes=vmem_mib * 2**20
        ),
    )(*given.values())
    return dict(zip(outs, results))


def whole(given, depth, hidden):
    table = buffers(depth, hidden)
    frame_total = given[NAMES.slot_frames].shape[0]
    table[NAMES.params] = ((16, WIDE), F32)
    table[NAMES.head_params] = ((8, WIDE), F32)
    outs = {
        NAMES.out_rows: table.pop(NAMES.out_rows),
        NAMES.grad_rows: table.pop(NAMES.grad_rows),
        NAMES.small_out: ((24, WIDE), F32),
        NAMES.grad_w_qkv: ((2, 3, depth // 8, WIDE), F32),
        NAMES.grad_w_out: ((2, WIDE, depth // 8), F32),
        NAMES.grad_w_up: ((2, depth // 8, hidden), F32),
        NAMES.grad_w_down: ((2, hidden, depth // 8), F32),
    }
    scratch = {**table, **{name: (shape, None) for name, shape in SEMAPHORES.items()}}
    for name in GRADS:
        scratch[name.replace(NAMES.grad_w_, NAMES.held_)] = outs[name]
    scratch[NAMES.scenes] = ((frame_total,), NAMES.scalars)
    out = call(whole_kernel, given, outs, scratch, 0, NAMES.whole, 62)
    big = GRADS
    shapes = [
        ((TOK, WIDE), BF),
        ((TOK, WIDE), F32),
        ((2, 2, WIDE), F32),
        ((2, WIDE), F32),
        ((2, WIDE), F32),
        ((2, 2, HD), F32),
        ((2, 2, HD), F32),
        ((2, 2, WIDE), F32),
    ] + [outs[name] for name in big]
    in_vmem, in_hbm = pl.BlockSpec(memory_space=pltpu.VMEM), pl.BlockSpec(memory_space=pl.ANY)
    results = pl.pallas_call(
        results_kernel,
        name=NAMES.results,
        out_shape=[jax.ShapeDtypeStruct(shape, kind) for shape, kind in shapes],
        in_specs=[in_hbm] * 7,
        out_specs=[in_vmem] * 8 + [in_hbm] * 4,
        scratch_shapes=[pltpu.VMEM(*outs[name]) for name in big + (NAMES.out_rows, NAMES.grad_rows, NAMES.small_out)]
        + [pltpu.SemaphoreType.DMA((2, 7))],
        compiler_params=pltpu.CompilerParams(vmem_limit_bytes=60 * 2**20),
    )(out[NAMES.out_rows], out[NAMES.grad_rows], out[NAMES.small_out], *(out[name] for name in big))
    return tuple(results[:7]) + tuple(results[8:12]) + (results[7],)


def by_phases(given, same_scene, depth, hidden):
    heads_here = WIDE // HD
    table = buffers(depth, hidden)
    table[NAMES.d_qkv] = ((3, depth, WIDE), BF)
    table[NAMES.d_out] = ((WIDE, depth), BF)
    table[NAMES.d_up] = ((depth, hidden), BF)
    table[NAMES.d_down] = ((hidden, depth), BF)
    held = dict(given)

    def run(phase, ins, outs, scratch, fresh=()):
        ins = {name: held[name] for name in ins}
        outs = {name: table[name] for name in outs}
        scratch = {name: table[name] for name in scratch}
        for name in (NAMES.fetch_sem, NAMES.z_send, NAMES.z_recv):
            scratch[name] = (SEMAPHORES[name], None)

        def body(names, *refs):
            plain_kernel(phase, names, fresh, None, *refs)

        number = (block_zero_phase, middle_phase, attention_back_phase, mlp_back_phase, last_phase).index(phase)
        held.update(call(body, ins, outs, scratch, 1 + number, phase.__name__, 48))

    def rows(array):
        return array[:TOK].reshape(TOK, heads_here, HD)

    def padded(array):
        return jnp.pad(array.reshape(TOK, -1), ((0, RP - TOK), (0, 0)))

    allowed = same_scene[lax.axis_index("seq")]
    run(
        block_zero_phase,
        (NAMES.tokens, NAMES.params, NAMES.head_params) + IN_HBM,
        (NAMES.params_full, NAMES.x0, NAMES.h0, NAMES.raw0, NAMES.q0, NAMES.k0, NAMES.v0, NAMES.att0, NAMES.x1, NAMES.br0, NAMES.m0, NAMES.act0, NAMES.slope0, NAMES.mo0, NAMES.x2, NAMES.h1, NAMES.raw1, NAMES.q1, NAMES.k1, NAMES.v1),
        (NAMES.every, NAMES.part, NAMES.inbox, NAMES.wq, NAMES.wo, NAMES.wu, NAMES.wd),
    )
    q1, k1, v1 = rows(held[NAMES.q1]), rows(held[NAMES.k1]), rows(held[NAMES.v1])
    attended, lse = global_forward_plain(q1, k1, v1, allowed)
    held[NAMES.att1] = padded(attended.astype(BF))
    held[NAMES.grad_full] = padded(lax.all_gather(given[NAMES.grad_out], "mp", axis=1, tiled=True))
    run(
        middle_phase,
        (NAMES.att1, NAMES.x2, NAMES.grad_full, NAMES.params_full, NAMES.w_out, NAMES.w_up, NAMES.w_down),
        (NAMES.out_rows, NAMES.g3, NAMES.x3, NAMES.br1, NAMES.dbr1, NAMES.datt1, NAMES.d_up, NAMES.d_down, NAMES.sums),
        (NAMES.part, NAMES.part_out, NAMES.inbox, NAMES.m1, NAMES.act1, NAMES.slope1, NAMES.dmlp, NAMES.dpre, NAMES.final_low, NAMES.wo, NAMES.wu, NAMES.wd),
        (NAMES.sums,),
    )
    d_up1 = lax.psum_scatter(held[NAMES.d_up], "seq", scatter_dimension=0, tiled=True)
    d_down1 = lax.psum_scatter(held[NAMES.d_down], "seq", scatter_dimension=1, tiled=True)
    sums = held[NAMES.sums]
    grads = global_backward_plain(q1, k1, v1, rows(held[NAMES.datt1]), attended, lse, allowed)
    held[NAMES.dq], held[NAMES.dk], held[NAMES.dv] = (padded(array) for array in grads)
    d_out1 = lax.dot_general(
        held[NAMES.att1], held[NAMES.dbr1], (((0,), (0,)), ((), ())), preferred_element_type=F32
    ).astype(BF)
    run(
        attention_back_phase,
        (NAMES.dq, NAMES.dk, NAMES.dv, NAMES.raw1, NAMES.h1, NAMES.x2, NAMES.g3, NAMES.mo0, NAMES.params_full, NAMES.head_params, NAMES.w_qkv),
        (NAMES.g5, NAMES.dm0, NAMES.d_qkv, NAMES.sums, NAMES.head_sums),
        (NAMES.part, NAMES.inbox, NAMES.dproj, NAMES.wq),
        (NAMES.sums, NAMES.head_sums),
    )
    d_qkv1 = lax.psum_scatter(held[NAMES.d_qkv], "seq", scatter_dimension=1, tiled=True)
    d_out1 = lax.psum_scatter(d_out1, "seq", scatter_dimension=1, tiled=True)
    sums = sums + held[NAMES.sums]
    held[NAMES.head_sums_in] = held[NAMES.head_sums]
    run(
        mlp_back_phase,
        (NAMES.dm0, NAMES.act0, NAMES.slope0, NAMES.m0, NAMES.x1, NAMES.g5, NAMES.br0, NAMES.params_full, NAMES.w_up, NAMES.w_down),
        (NAMES.g6, NAMES.dbr0, NAMES.d_up, NAMES.d_down, NAMES.sums),
        (NAMES.part, NAMES.inbox, NAMES.dpre, NAMES.wu, NAMES.wd),
        (NAMES.sums,),
    )
    d_up0 = lax.psum_scatter(held[NAMES.d_up], "seq", scatter_dimension=0, tiled=True)
    d_down0 = lax.psum_scatter(held[NAMES.d_down], "seq", scatter_dimension=1, tiled=True)
    held[NAMES.sums_in] = sums + held[NAMES.sums]
    run(
        last_phase,
        (NAMES.dbr0, NAMES.att0, NAMES.raw0, NAMES.q0, NAMES.k0, NAMES.v0, NAMES.h0, NAMES.x0, NAMES.g6, NAMES.params_full, NAMES.head_params, NAMES.sums_in, NAMES.head_sums_in, NAMES.w_out, NAMES.w_qkv),
        (NAMES.grad_rows, NAMES.d_qkv, NAMES.d_out, NAMES.small),
        (NAMES.part, NAMES.inbox, NAMES.dproj, NAMES.final, NAMES.messages, NAMES.letters, NAMES.sums, NAMES.head_sums, NAMES.wo, NAMES.wq),
    )
    d_qkv0 = lax.psum_scatter(held[NAMES.d_qkv], "seq", scatter_dimension=1, tiled=True)
    d_out0 = lax.psum_scatter(held[NAMES.d_out], "seq", scatter_dimension=1, tiled=True)

    def both(first, second):
        return jnp.stack([first, second]).astype(F32)

    return {
        NAMES.out_rows: held[NAMES.out_rows],
        NAMES.grad_rows: held[NAMES.grad_rows].astype(F32),
        NAMES.small_out: lax.psum(held[NAMES.small], "seq"),
        NAMES.grad_w_qkv: both(d_qkv0, d_qkv1),
        NAMES.grad_w_out: both(d_out0, d_out1),
        NAMES.grad_w_up: both(d_up0, d_up1),
        NAMES.grad_w_down: both(d_down0, d_down1),
    }


def per_device(
    tokens,
    grad_out,
    frame_counts,
    slot_frames,
    block_norm_multiplier,
    block_norm_bias,
    qk_gain,
    qk_bias,
    w_qkv,
    w_out,
    w_up,
    w_down,
    layer_scale,
):
    depth = w_qkv.shape[2]
    hidden = w_up.shape[2]
    given = {
        NAMES.tokens: tokens,
        NAMES.grad_out: grad_out,
        NAMES.w_qkv: w_qkv,
        NAMES.w_out: w_out,
        NAMES.w_up: w_up,
        NAMES.w_down: w_down,
    }
    if lax.axis_size("seq") == 8:
        given.update(
            frame_counts=frame_counts,
            slot_frames=slot_frames,
            block_norm_multiplier=block_norm_multiplier,
            block_norm_bias=block_norm_bias,
            qk_gain=qk_gain,
            qk_bias=qk_bias,
            layer_scale=layer_scale,
        )
        return whole(given, depth, hidden)

    heads_here = WIDE // HD
    frame_total = slot_frames.shape[0]
    frame_ids = jnp.arange(frame_total, dtype=jnp.int32)
    scene_ends = jnp.cumsum(frame_counts)
    scene_of_frame = jnp.sum((scene_ends[None, :] <= frame_ids[:, None]).astype(jnp.int32), axis=1)
    scene_table = jnp.sum(
        jnp.where(slot_frames[:, None] == frame_ids[None, :], scene_of_frame[None, :], 0), axis=1
    )
    same_scene = scene_table[:, None] == scene_table[None, :]
    given[NAMES.params] = jnp.concatenate(
        [
            block_norm_multiplier.reshape(4, WIDE),
            block_norm_bias.reshape(4, WIDE),
            layer_scale.reshape(4, WIDE),
            jnp.zeros((4, WIDE), F32),
        ]
    )
    given[NAMES.head_params] = jnp.tile(
        jnp.concatenate([qk_gain.reshape(4, HD), qk_bias.reshape(4, HD)]), (1, heads_here)
    )
    out = by_phases(given, same_scene, depth, hidden)
    small = out[NAMES.small_out]
    head_grads = small[16:24].reshape(2, 2, 2, heads_here, HD).sum(axis=3)
    return (
        out[NAMES.out_rows][:TOK],
        out[NAMES.grad_rows][:TOK],
        small[0:4].reshape(2, 2, WIDE),
        small[4:6],
        small[6:8],
        head_grads[:, 0],
        head_grads[:, 1],
        out[NAMES.grad_w_qkv],
        out[NAMES.grad_w_out],
        out[NAMES.grad_w_up],
        out[NAMES.grad_w_down],
        small[8:12].reshape(2, 2, WIDE),
    )


def solution(mesh):
    in_specs = (
        P("seq", "mp"),
        P("seq", "mp"),
        P(),
        P(),
        P(None, None, "mp"),
        P(None, None, "mp"),
        P(),
        P(),
        P(None, None, None, "mp"),
        P(None, "mp", None),
        P(None, None, "mp"),
        P(None, "mp", None),
        P(None, None, "mp"),
    )
    out_specs = (
        P("seq", "mp"),
        P("seq", "mp"),
        P(None, None, "mp"),
        P(None, "mp"),
        P(None, "mp"),
        P(),
        P(),
        P(None, None, "seq", "mp"),
        P(None, "mp", "seq"),
        P(None, "seq", "mp"),
        P(None, "mp", "seq"),
        P(None, None, "mp"),
    )
    return jax.shard_map(
        per_device, mesh=mesh, in_specs=in_specs, out_specs=out_specs, check_vma=False
    )
```

```python
from functools import partial

import jax
import jax.numpy as jnp
from jax import lax
from jax.experimental import pallas as pl
from jax.experimental.pallas import tpu as pltpu
from jax.sharding import PartitionSpec as P

HD = 64
TOK = 261
EPS = 1e-06
NEG = -1e30

RP = 272
CH = 64
RO = 80
NZ = 4
WIDE = 256
F32 = jnp.float32
BF = jnp.bfloat16
MESH = pl.DeviceIdType.MESH


class Names:
    def __getattr__(self, name):
        return name


NAMES = Names()
HIGH = lax.Precision.HIGHEST


def dot(left, right):
    return jnp.dot(left, right, preferred_element_type=F32)


def dot_cols(left, right):
    return lax.dot_general(left, right, (((1,), (1,)), ((), ())), preferred_element_type=F32)


def dot_rows(left, right):
    return lax.dot_general(left, right, (((0,), (0,)), ((), ())), preferred_element_type=F32)


def tile(index, width=WIDE):
    return pl.ds(pl.multiple_of(index * width, width), width)


def standardize(x):
    mean = jnp.mean(x, axis=1, keepdims=True)
    centered = x - mean
    variance = jnp.mean(centered * centered, axis=1, keepdims=True)
    rstd = lax.rsqrt(variance + EPS)
    return centered * rstd, rstd


def norm_back(dnorm, x, multiplier, valid):
    xhat, rstd = standardize(x)
    gain = jnp.sum(jnp.where(valid, dnorm * xhat, 0.0), axis=0, keepdims=True)
    bias = jnp.sum(jnp.where(valid, dnorm, 0.0), axis=0, keepdims=True)
    e = dnorm * multiplier
    dv = rstd * (
        e - jnp.mean(e, axis=1, keepdims=True) - xhat * jnp.mean(e * xhat, axis=1, keepdims=True)
    )
    return dv, gain, bias


def head_means():
    row = lax.broadcasted_iota(jnp.int32, (WIDE, WIDE), 0)
    col = lax.broadcasted_iota(jnp.int32, (WIDE, WIDE), 1)
    same = lax.shift_right_logical(row, 6) == lax.shift_right_logical(col, 6)
    return jnp.where(same, 1.0 / HD, 0.0).astype(BF)


def mean_heads(x, means):
    high = x.astype(BF)
    rest = x - high.astype(F32)
    middle = rest.astype(BF)
    low = (rest - middle.astype(F32)).astype(BF)
    return dot(high, means) + (dot(middle, means) + dot(low, means))


def head_standardize(raw, means):
    centered = raw - mean_heads(raw, means)
    rstd = lax.rsqrt(mean_heads(centered * centered, means) + EPS)
    return centered * rstd, rstd


def head_back(dy, xhat, rstd, gain, means):
    e = dy * gain
    raw = rstd * (e - mean_heads(e, means) - xhat * mean_heads(e * xhat, means))
    return (
        raw,
        jnp.sum(dy * xhat, axis=0, keepdims=True),
        jnp.sum(dy, axis=0, keepdims=True),
    )


def lane_head(rows, width=WIDE):
    return lax.shift_right_logical(lax.broadcasted_iota(jnp.int32, (rows, width), 1), 6)


def key_valid():
    return lax.broadcasted_iota(jnp.int32, (RP, RP), 1) < TOK


def own_valid(z):
    row = lax.broadcasted_iota(jnp.int32, (RO, 1), 0)
    return (row < CH) | ((z == NZ - 1) & (row < TOK - (NZ - 1) * CH))


def remote(src, dst, send, recv, device):
    return pltpu.make_async_remote_copy(
        src_ref=src, dst_ref=dst, send_sem=send, recv_sem=recv, device_id=device, device_id_type=MESH
    )


def greet(devices):
    barrier = pltpu.get_barrier_semaphore()
    for device in devices:
        pl.semaphore_signal(barrier, inc=1, device_id=device, device_id_type=MESH)
    pl.semaphore_wait(barrier, len(devices))


def line(s, z):
    return [(s, lax.rem(z + d, NZ)) for d in range(1, NZ)]


def sized(last, act):
    pl.when(last)(lambda: act(RO))
    pl.when(jnp.logical_not(last))(lambda: act(CH))


def block(z, rows):
    return pl.ds(pl.multiple_of(z * CH, CH), rows)


def own_rows(z):
    return pl.ds(pl.multiple_of(z * CH, CH), RO)


def put_own(full, z, value):
    full[block(z, CH)] = value[:CH]

    @pl.when(z == NZ - 1)
    def _():
        full[pl.ds(NZ * CH, RO - CH)] = value[CH:]


class Line:
    def __init__(self, z):
        self.z = z
        self.near = lax.bitwise_xor(z, 1)
        self.is_end = (z == 0) | (z == NZ - 1)
        self.is_middle = jnp.logical_not(self.is_end)
        self.other_middle = jnp.where(z < 2, 2, 1)
        self.other_end = jnp.where(z < 2, 3, 0)


def by_rows(full):
    def view(owner, act):
        sized(owner == NZ - 1, lambda rows: act(full.at[block(owner, rows)]))

    return view


def by_columns(full):
    def view(owner, act):
        act(full.at[:, tile(owner)])

    return view


class Gather:
    def __init__(self, view, s, z, send, recv):
        self.view, self.s, self.line = view, s, Line(z)
        self.send, self.recv = send, recv

    def copy(self, ref, sent, arrived, target):
        return remote(ref, ref, self.send.at[sent], self.recv.at[arrived], (self.s, target))

    def own(self, sent, arrived, target, act):
        self.view(self.line.z, lambda ref: act(self.copy(ref, sent, arrived, target)))

    def start(self):
        line = self.line

        @pl.when(line.is_end)
        def _():
            self.own(1, 2, line.other_middle, lambda copy: copy.start())

        @pl.when(line.is_middle)
        def _():
            self.own(2, 1, line.other_end, lambda copy: copy.start())
            self.own(1, 1, line.other_middle, lambda copy: copy.start())

        self.own(0, 0, line.near, lambda copy: copy.start())

    def sent(self):
        line = self.line
        self.own(0, 0, line.near, lambda copy: copy.wait_send())
        self.own(1, 1, line.other_middle, lambda copy: copy.wait_send())

        @pl.when(line.is_middle)
        def _():
            self.own(2, 1, line.other_end, lambda copy: copy.wait_send())

    def arrive(self, number, owner):
        self.view(owner, lambda ref: self.copy(ref, 0, number, self.line.near).wait_recv())

    def take_and_pass(self):
        line = self.line
        self.arrive(2, line.other_end)
        self.view(line.other_end, lambda ref: self.copy(ref, 3, 2, line.near).start())

    def passed_on(self):
        line = self.line

        @pl.when(line.is_middle)
        def _():
            self.view(line.other_end, lambda ref: self.copy(ref, 3, 2, line.near).wait_send())

    def finish(self):
        line = self.line
        pl.when(line.is_middle)(self.take_and_pass)
        self.arrive(0, line.near)
        self.arrive(1, line.other_middle)
        self.passed_on()
        pl.when(line.is_end)(lambda: self.arrive(2, line.other_end))


class Scatter:
    def __init__(self, part, inbox, s, z, send, recv):
        self.part, self.inbox, self.s, self.line = part, inbox, s, Line(z)
        self.send, self.recv = send, recv

    def copy(self, owner, box, sent, target, act):
        def go(rows):
            act(
                remote(
                    self.part.at[block(owner, rows)],
                    self.inbox.at[box, pl.ds(0, rows)],
                    self.send.at[sent],
                    self.recv.at[box],
                    (self.s, target),
                )
            )

        sized(owner == NZ - 1, go)

    def direct(self, act):
        line = self.line

        @pl.when(line.is_end)
        def _():
            self.copy(line.other_end, 3, 1, line.near, act)
            self.copy(line.other_middle, 2, 2, line.other_middle, act)

        @pl.when(line.is_middle)
        def _():
            self.copy(line.other_middle, 1, 2, line.other_middle, act)

        self.copy(line.near, 0, 0, line.near, act)

    def start(self):
        self.direct(lambda copy: copy.start())

    def sent(self):
        self.direct(lambda copy: copy.wait_send())

    def across(self, act):
        line = self.line

        def go(rows):
            act(
                remote(
                    self.inbox.at[3, pl.ds(0, rows)],
                    self.inbox.at[1, pl.ds(0, rows)],
                    self.send.at[3],
                    self.recv.at[1],
                    (self.s, line.other_end),
                )
            )

        sized(line.other_end == NZ - 1, go)

    def arrive(self, owner, box):
        self.copy(owner, box, 0, self.line.near, lambda copy: copy.wait_recv())

    def relay(self):
        line = self.line

        @pl.when(line.is_middle)
        def _():
            self.arrive(line.other_end, 3)
            total = self.inbox[3].astype(F32) + self.part[own_rows(line.other_end)].astype(F32)
            self.inbox[3] = total.astype(BF)
            self.across(lambda copy: copy.start())

    def finish(self):
        line = self.line
        total = self.part[own_rows(line.z)].astype(F32)
        for box in (0, 1):
            self.arrive(line.z, box)
            total = total + self.inbox[box].astype(F32)

        @pl.when(line.is_middle)
        def _():
            self.arrive(line.z, 2)
            self.across(lambda copy: copy.wait_send())

        return total + jnp.where(line.is_middle, self.inbox[2].astype(F32), 0.0)


def features_start(rows_ref, full, s, z, send, recv):
    for d in range(1, NZ):
        peer = lax.rem(z + d, NZ)

        def act(rows, d=d, peer=peer):
            remote(
                rows_ref.at[pl.ds(0, rows), tile(peer)],
                full.at[block(z, rows)],
                send.at[d - 1],
                recv.at[d - 1],
                (s, peer),
            ).start()

        sized(z == NZ - 1, act)
    put_own(full, z, rows_ref[:, tile(z)])


def features_wait(rows_ref, full, s, z, send, recv):
    for d in range(1, NZ):
        source = lax.rem(z + NZ - d, NZ)
        peer = lax.rem(z + d, NZ)

        def act_in(rows, d=d, source=source):
            remote(
                rows_ref.at[pl.ds(0, rows), tile(z)],
                full.at[block(source, rows)],
                send.at[d - 1],
                recv.at[d - 1],
                (s, source),
            ).wait_recv()

        def act_out(rows, d=d, peer=peer):
            remote(
                rows_ref.at[pl.ds(0, rows), tile(peer)],
                full.at[block(z, rows)],
                send.at[d - 1],
                recv.at[d - 1],
                (s, peer),
            ).wait_send()

        sized(source == NZ - 1, act_in)
        sized(z == NZ - 1, act_out)


def rows_start(heads_ref, full, s, z, send, recv):
    for d in range(1, NZ):
        peer = lax.rem(z + d, NZ)

        def act(rows, d=d, peer=peer):
            remote(
                heads_ref.at[block(peer, rows)],
                full.at[pl.ds(0, rows), tile(z)],
                send.at[d - 1],
                recv.at[d - 1],
                (s, peer),
            ).start()

        sized(peer == NZ - 1, act)
    full[:, tile(z)] = heads_ref[own_rows(z)]


def rows_wait(heads_ref, full, s, z, send, recv):
    for d in range(1, NZ):
        source = lax.rem(z + NZ - d, NZ)
        peer = lax.rem(z + d, NZ)

        def act_in(rows, d=d, source=source):
            remote(
                heads_ref.at[block(z, rows)],
                full.at[pl.ds(0, rows), tile(source)],
                send.at[d - 1],
                recv.at[d - 1],
                (s, source),
            ).wait_recv()

        def act_out(rows, d=d, peer=peer):
            remote(
                heads_ref.at[block(peer, rows)],
                full.at[pl.ds(0, rows), tile(z)],
                send.at[d - 1],
                recv.at[d - 1],
                (s, peer),
            ).wait_send()

        sized(z == NZ - 1, act_in)
        sized(peer == NZ - 1, act_out)


class Refs:
    WEIGHTS = {NAMES.wq: NAMES.w_qkv, NAMES.wo: NAMES.w_out, NAMES.wu: NAMES.w_up, NAMES.wd: NAMES.w_down}

    def __init__(self, names, refs, fast):
        self.__dict__.update(zip(names, refs))
        self.fast = fast
        self.s, self.z = lax.axis_index("seq"), lax.axis_index("mp")
        self.a, self.core = lax.shift_right_logical(self.s, 1), lax.rem(self.s, 2)
        self.sibling = (2 * self.a + 1 - self.core, self.z)
        self.held = {}

    def weight_copy(self, name, b):
        number = list(self.WEIGHTS).index(name)
        source = getattr(self, self.WEIGHTS[name])
        return pltpu.make_async_copy(source.at[b], getattr(self, name), self.fetch_sem.at[number])

    def prefetch(self, name, b):
        self.weight_copy(name, b).start()
        self.held[name] = (b, False)

    def need(self, name, b):
        held, waited = self.held.get(name, (None, False))
        if held != b:
            self.prefetch(name, b)
            waited = False
        if not waited:
            self.weight_copy(name, b).wait()
        self.held[name] = (b, True)
        return getattr(self, name)

    def line_sems(self, number):
        return (self.s, self.z, self.z_send.at[number], self.z_recv.at[number])

    def chip(self, d):
        return lax.rem(self.a + d, 4)

    def chip_device(self, chip):
        return (2 * chip + self.core, self.z)


def project(r, b, hidden, weights, raw, queries, keys, values, rows=pl.ds(0, RP)):
    means = head_means()
    for c in range(3):
        product = dot(hidden[rows, :], weights[c])
        if c == 2:
            values[rows, :] = product.astype(BF)
            continue
        raw[c, rows, :] = product
        xhat, _ = head_standardize(product, means)
        row = 2 * b + c
        normed = xhat * r.head_params[row : row + 1] + r.head_params[4 + row : 5 + row]
        if c == 0:
            queries[rows, :] = (normed * (HD ** (-0.5))).astype(BF)
        else:
            keys[rows, :] = normed.astype(BF)


def share_rows(r, full, at):
    gather = Gather(by_rows(full), *at)
    gather.start()
    gather.sent()
    gather.finish()


def pass_rows(r, full, at, compute, sum_at=None, meanwhile=()):
    gather = Gather(by_rows(full), *at)
    line = gather.line
    scatter = Scatter(r.part, r.inbox.at[0], *sum_at) if sum_at else None
    own_half = jnp.where(line.z < 2, 0, 1)
    gather.start()

    def step(number, carry):
        half = jnp.where(number == 0, own_half, 1 - own_half)
        first, second = number == 0, number == 1

        @pl.when(first)
        def _():
            pl.when(line.is_middle)(gather.take_and_pass)
            gather.arrive(0, line.near)

        @pl.when(second)
        def _():
            gather.arrive(1, line.other_middle)
            pl.when(line.is_end)(lambda: gather.arrive(2, line.other_end))

        pl.when(half == 0)(lambda: compute(pl.ds(0, 2 * CH)))
        pl.when(half == 1)(lambda: compute(pl.ds(2 * CH, RP - 2 * CH)))
        if scatter is not None:

            def send(owner, box, sent, target):
                scatter.copy(owner, box, sent, target, lambda copy: copy.start())

            @pl.when(first)
            def _():
                send(line.near, 0, 0, line.near)

            @pl.when(second & line.is_end)
            def _():
                send(line.other_end, 3, 1, line.near)
                send(line.other_middle, 2, 2, line.other_middle)

            @pl.when(second & line.is_middle)
            def _():
                send(line.other_middle, 1, 2, line.other_middle)

        return carry

    lax.fori_loop(0, 2, step, 0)
    for work in meanwhile[:1]:
        work()
    gather.sent()
    gather.passed_on()
    if scatter is None:
        return None
    scatter.sent()
    scatter.relay()
    for work in meanwhile[1:]:
        work()
    return scatter.finish()


def sum_rows(r, at, meanwhile=(), box=0):
    scatter = Scatter(r.part, r.inbox.at[box], *at)
    scatter.start()
    for work in meanwhile[:1]:
        work()
    scatter.sent()
    scatter.relay()
    for work in meanwhile[1:]:
        work()
    return scatter.finish()


def apply_norm(x, params, b, j):
    xhat, _ = standardize(x)
    row = 2 * b + j
    return (xhat * params[row : row + 1] + params[4 + row : 5 + row]).astype(BF)


ALL_ROWS = pl.ds(0, RP)


def up_gelu(hidden, w_up, act, slope, rows=ALL_ROWS):
    def step(j, carry):
        cols = tile(j)
        pre = dot(hidden[rows, :], w_up[:, cols])
        cdf = 0.5 * (1.0 + lax.erf(pre * (0.5**0.5)))
        act[rows, cols] = (pre * cdf).astype(BF)
        slope[rows, cols] = cdf + pre * jnp.exp(-0.5 * pre * pre) * 0.3989422804014327
        return carry

    lax.fori_loop(0, w_up.shape[1] // WIDE, step, 0)


def times(left, weights, part, rows=ALL_ROWS):
    def step(j, carry):
        cols = tile(j)
        part[rows, cols] = dot(left[rows, :], weights[:, cols]).astype(BF)
        return carry

    lax.fori_loop(0, weights.shape[1] // WIDE, step, 0)


def times_turned(left, weights, part, rows=ALL_ROWS):
    def step(j, carry):
        part[rows, tile(j)] = dot_cols(left[rows, :], weights[tile(j), :]).astype(BF)
        return carry

    lax.fori_loop(0, weights.shape[0] // WIDE, step, 0)


def mlp_back(dmlp, w_down, slope, dpre, rows=ALL_ROWS):
    def step(j, carry):
        cols = tile(j)
        dact = dot_cols(dmlp[rows, :], w_down[cols, :])
        dpre[rows, cols] = (dact * slope[rows, cols]).astype(BF)
        return carry

    lax.fori_loop(0, w_down.shape[0] // WIDE, step, 0)


def attention_input_back(dproj, w_qkv, part):
    def step(j, carry):
        rows = tile(j)
        total = dot_cols(dproj[0], w_qkv[0, rows, :])
        total = total + dot_cols(dproj[1], w_qkv[1, rows, :])
        total = total + dot_cols(dproj[2], w_qkv[2, rows, :])
        part[:, rows] = total.astype(BF)
        return carry

    lax.fori_loop(0, w_qkv.shape[1] // WIDE, step, 0)


def up_grad(r, left, right, out):
    def step(j, carry):
        value = dot_rows(left[:, tile(j)], right[...]).astype(BF)
        if r.fast:
            out[0, j] = value[: WIDE // 2]
            out[1, j] = value[WIDE // 2 :]
        else:
            out[tile(j), :] = value
        return carry

    lax.fori_loop(0, left.shape[1] // WIDE, step, 0)


def down_grad(r, left, right, out):
    def step(j, carry):
        value = dot_rows(left[:, tile(j)], right[...]).astype(BF)
        if r.fast:
            for piece in range(8):
                out[piece % 2, piece // 2, tile(j), :] = value[:, 128 * piece : 128 * piece + 128]
        else:
            out[tile(j), :] = value
        return carry

    lax.fori_loop(0, left.shape[1] // WIDE, step, 0)


def qkv_grad(r, hidden, dproj, out):
    def step(j, carry):
        left = hidden[:, tile(j)]
        for c in range(3):
            value = dot_rows(left, dproj[c]).astype(BF)
            if r.fast:
                out[0, j, c] = value[: WIDE // 2]
                out[1, j, c] = value[WIDE // 2 :]
            else:
                out[c, tile(j), :] = value
        return carry

    lax.fori_loop(0, hidden.shape[1] // WIDE, step, 0)


class SeqSum:
    def __init__(self, r, name, b, number):
        self.r, self.name, self.b = r, name, b
        self.mine = getattr(r, NAMES.d_ + name)
        self.first = getattr(r, NAMES.first_ + name)
        self.second = getattr(r, NAMES.second_ + name).at[b]
        self.sems = (r.sum_send.at[number], r.sum_recv.at[number])
        self.number = number

    def across(self):
        r = self.r
        send, recv = self.sems
        return remote(self.mine.at[1 - r.core], self.first, send.at[0], recv.at[0], r.sibling)

    def toward(self, d):
        r = self.r
        send, recv = self.sems
        chip = r.chip(d)
        return remote(
            self.mine.at[r.core, chip], self.second.at[d - 1], send.at[d], recv.at[d], r.chip_device(chip)
        )

    def start(self):
        self.across().start()

    def pass_on(self):
        self.across().wait()
        core = self.r.core
        for chip in range(4):
            total = self.mine[core, chip].astype(F32) + self.first[chip].astype(F32)
            self.mine[core, chip] = total.astype(BF)
        for d in (2, 1, 3):
            self.toward(d).start()

    def store(self):
        r = self.r
        held, out = getattr(r, NAMES.held_ + self.name), getattr(r, NAMES.grad_w_ + self.name)
        return pltpu.make_async_copy(held.at[self.b], out.at[self.b], r.store_sem.at[self.number])

    def finish(self):
        for d in (1, 3, 2):
            self.toward(d).wait()
        total = self.mine[self.r.core, self.r.a].astype(F32)
        for d in range(3):
            total = total + self.second[d].astype(F32)
        getattr(self.r, NAMES.held_ + self.name)[self.b] = total
        self.store().start()


class WholeOut:
    def __init__(self, r, number):
        self.r = r
        self.full = r.wof
        self.z_sems = r.line_sems(number)
        self.sems = (r.wo_send.at[number - 20], r.wo_recv.at[number - 20])

    def fetch(self, b):
        r = self.r
        part = r.wo_part.shape[0]
        rows = r.w_out.at[b, pl.ds(pl.multiple_of(r.s * part, part), part)]
        return pltpu.make_async_copy(rows, r.wo_part, r.fetch_sem.at[4])

    def line_copy(self, d, source):
        s, z, send, recv = self.z_sems
        owner = lax.rem(z + NZ - d, NZ) if source else z
        device = (s, owner if source else lax.rem(z + d, NZ))
        return remote(self.r.wo_part, self.full.at[owner, s], send.at[d - 1], recv.at[d - 1], device)

    def start(self, b):
        r = self.r
        self.fetch(b).wait()
        self.full[r.z, r.s] = r.wo_part[...]
        for d in range(1, NZ):
            self.line_copy(d, False).start()

    def chip_copy(self, d):
        send, recv = self.sems
        mine = self.full.at[:, self.r.s]
        return remote(mine, mine, send.at[d - 1], recv.at[d - 1], self.r.chip_device(self.r.chip(d)))

    def core_copy(self, d):
        send, recv = self.sems
        held = self.full.at[:, 2 * self.r.chip(4 - d) + self.r.core]
        return remote(held, held, send.at[3 + d], recv.at[3 + d], self.r.sibling)

    def pass_on(self):
        for d in range(1, NZ):
            self.line_copy(d, True).wait_recv()
        for d in (2, 1, 3):
            self.chip_copy(d).start()
        self.core_copy(0).start()
        for d in range(1, NZ):
            self.line_copy(d, False).wait_send()

    def cross(self):
        send, recv = self.sems
        for d in (1, 3, 2):
            there = self.full.at[:, 2 * self.r.chip(4 - d) + self.r.core]
            device = self.r.chip_device(self.r.chip(4 - d))
            remote(there, there, send.at[d - 1], recv.at[d - 1], device).wait_recv()
            self.core_copy(d).start()

    def finish(self):
        send, recv = self.sems
        for d in range(4):
            there = self.full.at[:, 2 * self.r.chip(4 - d) + 1 - self.r.core]
            remote(there, there, send.at[3 + d], recv.at[3 + d], self.r.sibling).wait_recv()
        for d in range(1, 4):
            self.chip_copy(d).wait_send()
        for d in range(4):
            self.core_copy(d).wait_send()


def own_branch(r, rows, out):
    def step(j, carry):
        cols = tile(j)
        out[:, cols] = dot(rows[...], r.wof[:, :, :, cols].reshape(NZ * WIDE, WIDE))
        return carry

    lax.fori_loop(0, r.wof.shape[3] // WIDE, step, 0)


def own_attended_grad(r, value, out):
    for part in range(NZ):
        weights = r.wof[part].reshape(WIDE, r.wof.shape[3])
        out[:, WIDE * part : WIDE * part + WIDE] = dot_cols(value, weights).astype(BF)


def heads_back(r, raw, dq, dk, dv, b, dproj):
    means = head_means()
    row = 2 * b
    for c, dy in ((0, dq * (HD ** (-0.5))), (1, dk)):
        xhat, rstd = head_standardize(raw[c], means)
        gain_row = r.head_params[row + c : row + c + 1]
        draw, gain, bias = head_back(dy, xhat, rstd, gain_row, means)
        dproj[c] = draw.astype(BF)
        r.head_sums[4 * b + c : 4 * b + c + 1] = gain
        r.head_sums[4 * b + 2 + c : 4 * b + 3 + c] = bias
    dproj[2] = dv.astype(BF)


def scale_grad(r, b, j, g, branch):
    valid = own_valid(r.z)
    row = 8 + 2 * b + j
    r.sums[row : row + 1] = jnp.sum(jnp.where(valid, g * branch, 0.0), axis=0, keepdims=True)


def through_norm(r, b, j, x, dnorm, g):
    valid = own_valid(r.z)
    row = 2 * b + j
    dv, gain, bias = norm_back(dnorm, x[...], r.params_full[row : row + 1], valid)
    r.sums[row : row + 1] = gain
    r.sums[4 + 2 * j + b : 5 + 2 * j + b] = bias
    return jnp.where(valid, g + dv, 0.0)


def start_phase(r):
    for name in (NAMES.wq, NAMES.wo, NAMES.wu, NAMES.wd):
        r.prefetch(name, 0)


def put_padded(r, source, full):
    full[pl.ds(CH * NZ, RP - CH * NZ), tile(r.z)] = jnp.zeros((RP - CH * NZ, WIDE), BF)
    full[pl.ds(0, TOK), tile(r.z)] = source[...]


def block_zero_phase(r, whole_out=None):
    s, z = r.s, r.z
    tokens_at, params_at, out_at, mid_at, mlp_at, next_at = (r.line_sems(i) for i in range(6))
    r.params_full[:, tile(z)] = r.params[...]
    put_padded(r, r.tokens, r.every)
    line_params = Gather(by_columns(r.params_full), *params_at)
    line_tokens = Gather(by_columns(r.every), *tokens_at)
    line_params.start()
    line_tokens.start()
    line_tokens.sent()
    line_params.sent()
    line_params.finish()
    line_tokens.finish()
    if r.fast:
        whole_out.start(1)
    params = r.params_full

    r.h0[...] = apply_norm(r.every[...].astype(F32), params, 0, 0)
    r.x0[...] = r.every[own_rows(z)].astype(F32)
    project(r, 0, r.h0, r.need(NAMES.wq, 0), r.raw0, r.q0, r.k0, r.v0)
    r.prefetch(NAMES.wq, 1)

    heads = lane_head(RP)
    keep = key_valid()
    queries = r.q0[...].astype(F32)
    attended = jnp.zeros((RP, WIDE), F32)
    for h in range(WIDE // HD):
        qh = jnp.where(heads == h, queries, 0.0).astype(BF)
        scores = jnp.where(keep, dot_cols(qh, r.k0[...]), NEG)
        expo = jnp.exp(scores - jnp.max(scores, axis=1, keepdims=True))
        probs = (expo * (1.0 / jnp.sum(expo, axis=1, keepdims=True))).astype(BF)
        attended = jnp.where(heads == h, dot(probs, r.v0[...]), attended)
    r.att0[...] = attended.astype(BF)

    times(r.att0, r.need(NAMES.wo, 0), r.part)
    branch = sum_rows(r, out_at)
    if r.fast:
        whole_out.pass_on()
    r.br0[...] = branch
    mid = r.x0[...] + params[8:9] * branch
    r.x1[...] = mid
    put_own(r.m0, z, apply_norm(mid, params, 0, 1))
    w_up, w_down = r.need(NAMES.wu, 0), r.need(NAMES.wd, 0)

    def mlp(rows):
        up_gelu(r.m0, w_up, r.act0, r.slope0, rows)
        times(r.act0, w_down, r.part, rows)

    def fetch_next():
        if r.fast:
            r.prefetch(NAMES.wu, 1)
            r.prefetch(NAMES.wd, 1)
            whole_out.cross()

    branch = pass_rows(r, r.m0, mid_at, mlp, mlp_at, (fetch_next,))
    r.mo0[...] = branch
    result = r.x1[...] + params[9:10] * branch
    r.x2[...] = result
    put_own(r.h1, z, apply_norm(result, params, 1, 0))
    w_qkv = r.need(NAMES.wq, 1)
    pass_rows(r, r.h1, next_at, lambda rows: project(r, 1, r.h1, w_qkv, r.raw1, r.q1, r.k1, r.v1, rows))
    if r.fast:
        whole_out.finish()


def place(first):
    row = lax.broadcasted_iota(jnp.int32, (WIDE, 2 * WIDE), 0)
    col = lax.broadcasted_iota(jnp.int32, (WIDE, 2 * WIDE), 1)
    within = lax.bitwise_and(col, 127)
    head = lax.shift_right_logical(col, 7)
    if first:
        return jnp.where((within < HD) & (row == head * HD + within), 1.0, 0.0).astype(BF)
    return jnp.where((within >= HD) & (row == head * HD + within - HD), 1.0, 0.0).astype(BF)


def swap_halves():
    row = lax.broadcasted_iota(jnp.int32, (2 * HD, 2 * HD), 0)
    col = lax.broadcasted_iota(jnp.int32, (2 * HD, 2 * HD), 1)
    return jnp.where(lax.bitwise_and(row + HD, 127) == col, 1.0, 0.0).astype(BF)


def pieces(x):
    high = x.astype(BF).astype(F32)
    middle = (x - high).astype(BF).astype(F32)
    return high, middle, x - high - middle


def key_lanes(r, f):
    count = r.frame_counts.shape[0]
    lane = lax.broadcasted_iota(jnp.int32, (RP, 2 * HD), 1) - HD
    row = lax.broadcasted_iota(jnp.int32, (RP, 2 * HD), 0)
    other_scene = (lane < count) & (lane != r.scenes[f])
    padding = (lane == count) & (row >= TOK)
    numbers = (lane > count) & (lane <= count + 3)
    return jnp.where(other_scene | padding, NEG, jnp.where(numbers, -1.0, 0.0))


def query_lanes(r, f, minus=None):
    count = r.frame_counts.shape[0]
    lane = lax.broadcasted_iota(jnp.int32, (RP, 2 * HD), 1) - HD
    lanes = jnp.where((lane == r.scenes[f]) | (lane == count), 1.0, 0.0)
    if minus is not None:
        for number, piece in enumerate(pieces(minus)):
            lanes = jnp.where(lane == count + 1 + number, piece, lanes)
    return lanes


HALF_ROWS = 144


def pack_heads(x, out):
    lower, upper = dot(x, place(True)), dot(x, place(False))
    for c in range(4):
        lanes = slice(128 * c, 128 * c + 128)
        out[c] = (lower[:HALF_ROWS, lanes] + upper[RP - HALF_ROWS :, lanes]).astype(BF)


def unpack_heads(packed, out):
    lower, upper = place(True), place(False)
    top, bottom = 0.0, 0.0
    for c in range(4):
        lanes = slice(128 * c, 128 * c + 128)
        top = top + dot_cols(packed[c], lower[:, lanes])
        bottom = bottom + dot_cols(packed[c], upper[:, lanes])
    out[pl.ds(0, HALF_ROWS), :] = top.astype(out.dtype)
    out[pl.ds(HALF_ROWS, RP - HALF_ROWS), :] = bottom[2 * HALF_ROWS - RP :].astype(out.dtype)


def pack(x, swap):
    low = lane_head(HALF_ROWS, 2 * HD) == 0
    upper = dot(x[RP - HALF_ROWS :], swap)
    return jnp.where(low, x[:HALF_ROWS].astype(F32), upper).astype(BF)


def unpack(packed, swap, out, lanes=None):
    low = lane_head(HALF_ROWS, 2 * HD) == 0
    top, bottom = packed.astype(F32), dot(packed, swap)
    if lanes is not None:
        top, bottom = jnp.where(low, top, lanes), jnp.where(low, bottom, lanes)
    out[pl.ds(0, HALF_ROWS), :] = top.astype(BF)
    out[pl.ds(HALF_ROWS, RP - HALF_ROWS), :] = bottom[2 * HALF_ROWS - RP :].astype(BF)


def global_forward_phase(r):
    s, z, a, core, sibling = r.s, r.z, r.a, r.core, r.sibling
    qk, vv, ks = r.qk, r.vv, r.ks
    packed = dot(r.q1[...], place(True)) + dot(r.k1[...], place(False))
    for c in range(4):
        r.slabs[c] = packed[:, 128 * c : 128 * c + 128].astype(BF)
    pack_heads(r.v1[...], r.pairs)
    packed_values = r.packed_values

    def toward(d):
        c = r.chip(d)
        target = r.chip_device(c)
        return (
            remote(r.slabs.at[c], qk.at[s], r.f_send.at[0, d - 1], r.f_recv.at[0, d - 1], target),
            remote(r.pairs.at[c], packed_values.at[s], r.f_send.at[1, d - 1], r.f_recv.at[1, d - 1], target),
        )

    def arriving(d):
        source = 2 * r.chip(4 - d) + core
        device = (source, z)
        return (
            remote(qk.at[source], qk.at[source], r.f_send.at[0, d - 1], r.f_recv.at[0, d - 1], device),
            remote(packed_values.at[source], packed_values.at[source], r.f_send.at[1, d - 1], r.f_recv.at[1, d - 1], device),
            source,
        )

    def relay(d, frame):
        return (
            remote(qk.at[frame], qk.at[frame], r.fc_send.at[0, d], r.fc_recv.at[0, d], sibling),
            remote(packed_values.at[frame], packed_values.at[frame], r.fc_send.at[1, d], r.fc_recv.at[1, d], sibling),
        )

    for d in (2, 1, 3):
        for copy in toward(d):
            copy.start()
    put_padded(r, r.grad_out, r.grad_full)
    line_grads = Gather(by_columns(r.grad_full), *r.line_sems(6))
    line_grads.start()
    qk[s] = r.slabs[a]
    packed_values[s] = r.pairs[a]
    for copy in relay(0, s):
        copy.start()
    for d in (1, 3, 2):
        first, second, source = arriving(d)
        first.wait_recv()
        second.wait_recv()
        for copy in relay(d, source):
            copy.start()
    for d in range(4):
        frame = 2 * r.chip(4 - d) + 1 - core
        for copy in relay(d, frame):
            copy.wait_recv()
    line_grads.finish()
    swap = swap_halves()
    low_half = lane_head(RP, 2 * HD) == 0

    lane = lax.broadcasted_iota(jnp.int32, (HALF_ROWS, 2 * HD), 1)
    value_lanes = jnp.where((lane >= HD) & (lane < HD + 3), -1.0, 0.0)

    def turn(f, carry):
        turned = jnp.where(low_half, dot(qk[f], swap), key_lanes(r, f))
        ks[pl.ds(pl.multiple_of(f * RP, 16), RP), :] = turned.astype(BF)
        unpack(packed_values[f], swap, vv.at[f], value_lanes)
        return carry

    lax.fori_loop(0, 8, turn, 0)

    def back(d):
        target = r.chip(d)
        device = r.chip_device(target)
        return remote(r.outs.at[target], r.ins.at[a], r.fb_send.at[d - 1], r.fb_recv.at[d - 1], device)

    def attend(i):
        f = 2 * i + core
        qf = jnp.where(low_half, qk[f].astype(F32), query_lanes(r, f)).astype(BF)
        scores = dot_cols(qf, ks[...])
        peak = jnp.max(scores, axis=1, keepdims=True)
        expo = jnp.exp(scores - peak)
        total = jnp.sum(expo, axis=1, keepdims=True)
        product = dot(expo.astype(BF), vv[...].reshape(8 * RP, 2 * HD))
        attended = product * (1.0 / total)
        r.outs_full[i] = attended
        r.outs[i] = pack(attended.astype(BF), swap)
        r.lse[i] = jnp.broadcast_to(peak + jnp.log(total), (RP, 2 * HD))

    def attend_and_send(d, carry):
        attend(r.chip(d))
        back(d).start()
        return carry

    lax.fori_loop(1, 4, attend_and_send, 0)
    attend(a)
    r.ins[a] = r.outs[a]
    for d in (1, 3, 2):
        source = r.chip(4 - d)
        there = r.ins.at[source]
        remote(there, there, r.fb_send.at[d - 1], r.fb_recv.at[d - 1], r.chip_device(source)).wait_recv()
    unpack_heads(r.ins, r.att1)
    line_grads.sent()
    for d in (1, 2, 3):
        for copy in toward(d):
            copy.wait_send()
        back(d).wait_send()
    for copy in relay(0, s):
        copy.wait_send()
    for d in (1, 2, 3):
        for copy in relay(d, 2 * r.chip(4 - d) + core):
            copy.wait_send()


def middle_phase(r, sums_of=None):
    s, z = r.s, r.z
    params = r.params_full
    out_at, mid_at, dnorm_at, next_at = (r.line_sems(i) for i in (7, 8, 9, 11))
    valid = own_valid(z)
    if r.fast:
        rows_start(r.att1, r.att_in, *out_at)
        r.dmlp[...] = (r.grad_full[...].astype(F32) * params[11:12]).astype(BF)
        rows_wait(r.att1, r.att_in, *out_at)
        own_branch(r, r.att_in, r.br1)
        branch = r.br1[...]
    else:
        w_out = r.need(NAMES.wo, 1)
        times(r.att1, w_out, r.part)
        r.dmlp[...] = (r.grad_full[...].astype(F32) * params[11:12]).astype(BF)
        branch = sum_rows(r, out_at)
        r.br1[...] = branch
    mid = r.x2[...] + params[10:11] * branch
    r.x3[...] = mid
    put_own(r.m1, z, apply_norm(mid, params, 1, 1))
    w_up, w_down = r.need(NAMES.wu, 1), r.need(NAMES.wd, 1)

    def mlp(rows):
        up_gelu(r.m1, w_up, r.act1, r.slope1, rows)
        mlp_back(r.dmlp, w_down, r.slope1, r.dpre, rows)
        times_turned(r.dpre, w_up, r.part, rows)

    def first():
        down_grad(r, r.act1, r.dmlp, r.d_down)
        if r.fast:
            sums_of[NAMES.down].start()

    def second():
        up_grad(r, r.m1, r.dpre, r.d_up)
        if r.fast:
            sums_of[NAMES.up].start()
            r.prefetch(NAMES.wu, 0)
            sums_of[NAMES.down].pass_on()

    dnorm = pass_rows(r, r.m1, mid_at, mlp, dnorm_at, (first, second))
    g = jnp.where(valid, r.grad_full[own_rows(z)].astype(F32), 0.0)
    after = through_norm(r, 1, 1, r.x3, dnorm, g)
    r.g3[...] = after
    dbranch = (after * params[10:11]).astype(BF)
    put_own(r.dbr1, z, dbranch)
    if r.fast:
        own_attended_grad(r, dbranch, r.datt_own)
        features_start(r.datt_own, r.datt1, *r.line_sems(10))
        Gather(by_rows(r.dbr1), *next_at).start()
    scale_grad(r, 1, 0, after, r.br1[...])
    times(r.act1, w_down, r.part_out)
    if r.fast:
        r.prefetch(NAMES.wd, 0)
        features_wait(r.datt_own, r.datt1, *r.line_sems(10))
    else:
        share_rows(r, r.dbr1, next_at)
        r.datt1[...] = dot_cols(r.dbr1[...], w_out[...]).astype(BF)
        result_start(r)
        result_relay(r)
        result_end(r)


def result_start(r):
    Scatter(r.part_out, r.inbox.at[1], *r.line_sems(22)).start()


def result_relay(r):
    scatter = Scatter(r.part_out, r.inbox.at[1], *r.line_sems(22))
    scatter.sent()
    scatter.relay()


def result_end(r):
    z = r.z
    rows_at = r.line_sems(12)
    out_branch = Scatter(r.part_out, r.inbox.at[1], *r.line_sems(22)).finish()
    g = jnp.where(own_valid(z), r.grad_full[own_rows(z)].astype(F32), 0.0)
    scale_grad(r, 1, 1, g, out_branch)
    r.final_low[...] = (r.x3[...] + r.params_full[11:12] * out_branch).astype(BF)
    features_start(r.final_low, r.out_rows, *rows_at)
    if not r.fast:
        features_wait(r.final_low, r.out_rows, *rows_at)


def global_backward_phase(r, sums_of):
    s, z, a, core, sibling = r.s, r.z, r.a, r.core, r.sibling
    pack_heads(r.datt1[...], r.pairs)

    def toward(d):
        c = r.chip(d)
        return remote(r.pairs.at[c], r.dos.at[a], r.b_send.at[d - 1], r.b_recv.at[d - 1], r.chip_device(c))

    for d in (2, 1, 3):
        toward(d).start()
    r.dos[a] = r.pairs[a]
    r.dkt[...] = jnp.zeros_like(r.dkt)
    r.dvt[...] = jnp.zeros_like(r.dvt)
    for d in (1, 3, 2):
        source = r.chip(4 - d)
        there = r.dos.at[source]
        remote(there, there, r.b_send.at[d - 1], r.b_recv.at[d - 1], r.chip_device(source)).wait_recv()
    half = lane_head(RP, 2 * HD)
    low_half = half == 0
    swap = swap_halves()
    ks, vv = r.ks, r.vv

    lane = lax.broadcasted_iota(jnp.int32, (RP, 2 * HD), 1)

    def step(i, carry):
        f = 2 * i + core
        lanes = query_lanes(r, f, r.lse[i][:, 0:1])
        qf = jnp.where(low_half, r.qk[f].astype(F32), lanes).astype(BF)
        unpack(r.dos[i], swap, r.do_rows, 0.0)
        do = r.do_rows[...].astype(F32)
        delta = jnp.sum(do * r.outs_full[i], axis=1, keepdims=True)
        for number, piece in enumerate(pieces(delta)):
            do = jnp.where(lane == HD + number, piece, do)
        do = do.astype(BF)
        probs = jnp.exp(dot_cols(qf, ks[...]))
        dprobs = dot_cols(do, vv[...].reshape(8 * RP, 2 * HD))
        dscores = (probs * dprobs).astype(BF)
        r.dq_mine[i] = dot(dscores, ks[...])
        r.dkt[...] += dot_rows(qf, dscores)
        r.dvt[...] += dot_rows(do, probs.astype(BF))
        return carry

    line_dbr = Gather(by_rows(r.dbr1), *r.line_sems(11))
    line_dbr.sent()
    lax.fori_loop(0, 2, step, 0)
    line_dbr.finish()
    result_start(r)
    lax.fori_loop(2, 4, step, 0)
    r.dk_sum[...] = jnp.transpose(r.dkt[...])
    r.dv_sum[...] = jnp.transpose(r.dvt[...])

    def rows_of(frame):
        return pl.ds(pl.multiple_of(frame * RP, 16), RP)

    for i in range(4):
        theirs = rows_of(2 * i + 1 - core)
        dv = dot(r.dv_sum[theirs, :].astype(BF), swap)
        r.dkv_send[i] = jnp.where(low_half, r.dk_sum[theirs, :], dv).astype(BF)
    across = remote(r.dkv_send, r.dkv_in, r.bc_send.at[0], r.bc_recv.at[0], sibling)
    across.start()
    down_grad(r, r.att1, r.dbr1, r.d_out)
    sums_of[NAMES.out].start()
    result_relay(r)
    across.wait()
    for i in range(4):
        own = rows_of(2 * i + core)
        dk = (r.dk_sum[own, :] + r.dkv_in[i].astype(F32)).astype(BF)
        dv = r.dv_sum[own, :] + dot(r.dkv_in[i], swap)
        r.ready[i] = jnp.where(low_half, r.dq_mine[i], dot(dk, swap)).astype(BF)
        r.ready_values[i] = pack(dv.astype(BF), swap)

    def back(d):
        target = r.chip(d)
        device = r.chip_device(target)
        return (
            remote(r.ready.at[target], r.dqk_in.at[a], r.bb_send.at[0, d - 1], r.bb_recv.at[0, d - 1], device),
            remote(r.ready_values.at[target], r.dv_in.at[a], r.bb_send.at[1, d - 1], r.bb_recv.at[1, d - 1], device),
        )

    for d in (2, 1, 3):
        for copy in back(d):
            copy.start()
    r.dqk_in[a] = r.ready[a]
    r.dv_in[a] = r.ready_values[a]
    for d in (1, 3, 2):
        source = r.chip(4 - d)
        for number, box in ((0, r.dqk_in), (1, r.dv_in)):
            there = box.at[source]
            sems = (r.bb_send.at[number, d - 1], r.bb_recv.at[number, d - 1])
            remote(there, there, *sems, r.chip_device(source)).wait_recv()
    to_q, to_k = place(True), place(False)
    dq = jnp.zeros((RP, WIDE), F32)
    dk = jnp.zeros((RP, WIDE), F32)
    for c in range(4):
        cols = slice(128 * c, 128 * c + 128)
        dq = dq + dot_cols(r.dqk_in[c], to_q[:, cols])
        dk = dk + dot_cols(r.dqk_in[c], to_k[:, cols])
    r.dq[...] = dq
    r.dk[...] = dk
    unpack_heads(r.dv_in, r.dv)
    for d in (1, 2, 3):
        toward(d).wait_send()
        for copy in back(d):
            copy.wait_send()


def attention_back_phase(r, sums_of=None):
    s, z = r.s, r.z
    if r.fast:
        sums_of[NAMES.up].pass_on()
    dnorm_at, next_at = r.line_sems(13), r.line_sems(14)
    heads_back(r, r.raw1, r.dq[...], r.dk[...], r.dv[...], 1, r.dproj)
    if r.fast:
        result_end(r)
    attention_input_back(r.dproj, r.need(NAMES.wq, 1), r.part)

    def first():
        qkv_grad(r, r.h1, r.dproj, r.d_qkv)
        if r.fast:
            r.prefetch(NAMES.wq, 0)
            sums_of[NAMES.qkv].start()

    def second():
        if r.fast:
            sums_of[NAMES.out].pass_on()

    dnorm = sum_rows(r, dnorm_at, (first, second))
    after = through_norm(r, 1, 0, r.x2, dnorm, r.g3[...])
    r.g5[...] = after
    put_own(r.dm0, z, (after * r.params_full[9:10]).astype(BF))
    if r.fast:
        sums_of[NAMES.qkv].pass_on()
    else:
        share_rows(r, r.dm0, next_at)
    scale_grad(r, 0, 1, after, r.mo0[...])


def mlp_back_phase(r, sums_of=None, earlier=None):
    s, z = r.s, r.z
    dnorm_at, next_at = r.line_sems(15), r.line_sems(16)
    w_down, w_up = r.need(NAMES.wd, 0), r.need(NAMES.wu, 0)

    def back(rows):
        mlp_back(r.dm0, w_down, r.slope0, r.dpre, rows)
        times_turned(r.dpre, w_up, r.part, rows)

    def first():
        if r.fast:
            earlier[NAMES.down].finish()
        down_grad(r, r.act0, r.dm0, r.d_down)
        if r.fast:
            sums_of[NAMES.down].start()

    def second():
        if r.fast:
            earlier[NAMES.up].finish()
        up_grad(r, r.m0, r.dpre, r.d_up)
        if r.fast:
            sums_of[NAMES.up].start()
            sums_of[NAMES.down].pass_on()

    if r.fast:
        dnorm = pass_rows(r, r.dm0, r.line_sems(14), back, dnorm_at, (first, second))
    else:
        back(ALL_ROWS)
        dnorm = sum_rows(r, dnorm_at, (first, second))
    after = through_norm(r, 0, 1, r.x1, dnorm, r.g5[...])
    r.g6[...] = after
    put_own(r.dbr0, z, (after * r.params_full[8:9]).astype(BF))
    gather = Gather(by_rows(r.dbr0), *next_at)
    gather.start()
    scale_grad(r, 0, 0, after, r.br0[...])
    if r.fast:
        sums_of[NAMES.up].pass_on()
    gather.sent()
    gather.finish()


def last_phase(r, sums_of=None, earlier=None):
    s, z = r.s, r.z
    dnorm_at, rows_at, notes_at = (r.line_sems(i) for i in range(17, 20))
    valid = own_valid(z)
    datt = dot_cols(r.dbr0[...], r.need(NAMES.wo, 0)[...]).astype(BF).astype(F32)
    heads = lane_head(RP)
    keep = key_valid()
    queries = r.q0[...].astype(F32)
    dq = jnp.zeros((RP, WIDE), F32)
    dk = jnp.zeros((RP, WIDE), F32)
    dv = jnp.zeros((RP, WIDE), F32)
    for h in range(WIDE // HD):
        here = heads == h
        qh = jnp.where(here, queries, 0.0).astype(BF)
        do = jnp.where(here, datt, 0.0).astype(BF)
        scores = jnp.where(keep, dot_cols(qh, r.k0[...]), NEG)
        expo = jnp.exp(scores - jnp.max(scores, axis=1, keepdims=True))
        probs = expo * (1.0 / jnp.sum(expo, axis=1, keepdims=True))
        dprobs = dot_cols(do, r.v0[...])
        delta = jnp.sum(probs * dprobs, axis=1, keepdims=True)
        dscores = (probs * (dprobs - delta)).astype(BF)
        dq = jnp.where(here, dot(dscores, r.k0[...]), dq)
        dk = dk + dot_rows(dscores, qh)
        dv = dv + dot_rows(probs.astype(BF), do)
    heads_back(r, r.raw0, dq, dk, dv, 0, r.dproj)
    attention_input_back(r.dproj, r.need(NAMES.wq, 0), r.part)

    def first():
        if r.fast:
            earlier[NAMES.qkv].finish()
        qkv_grad(r, r.h0, r.dproj, r.d_qkv)
        if r.fast:
            sums_of[NAMES.qkv].start()

    def second():
        if r.fast:
            earlier[NAMES.out].finish()
        down_grad(r, r.att0, r.dbr0, r.d_out)
        if r.fast:
            sums_of[NAMES.out].start()
            sums_of[NAMES.qkv].pass_on()
            sums_of[NAMES.out].pass_on()
            sums_of[NAMES.down].finish()
            sums_of[NAMES.up].finish()

    dnorm = sum_rows(r, dnorm_at, (first, second))
    r.final[...] = through_norm(r, 0, 0, r.x0, dnorm, r.g6[...]).astype(BF)
    for p in range(NZ):
        r.messages[p, 0:16] = r.sums[:, WIDE * p : WIDE * p + WIDE]
        r.messages[p, 16:24] = r.head_sums[...]

    def note(d):
        send, recv = notes_at[2:]
        peer = lax.rem(z + d, NZ)
        return remote(r.messages.at[peer], r.letters.at[d - 1], send.at[d - 1], recv.at[d - 1], (s, peer))

    for d in range(1, NZ):
        note(d).start()
    features_start(r.final, r.grad_rows, *rows_at)
    for d in range(1, NZ):
        note(d).wait()
    r.small[...] = r.messages[z] + r.letters[0] + r.letters[1] + r.letters[2]
    if not r.fast:
        features_wait(r.final, r.grad_rows, *rows_at)


def small_phase(r):
    pair = remote(r.small, r.small_in.at[0], r.small_send.at[0], r.small_recv.at[0], r.sibling)
    pair.start()
    pair.wait()
    r.small_two[...] = r.small[...] + r.small_in[0]

    def toward(d):
        device = r.chip_device(r.chip(d))
        return remote(r.small_two, r.small_in.at[d], r.small_send.at[d], r.small_recv.at[d], device)

    for d in range(1, 4):
        toward(d).start()
    for d in range(1, 4):
        toward(d).wait()
    boxes = [r.small_two[...], r.small_in[1], r.small_in[2], r.small_in[3]]
    total = None
    for chip in range(4):
        distance = lax.rem(r.a + 4 - chip, 4)
        term = boxes[0]
        for d in range(1, 4):
            term = jnp.where(distance == d, boxes[d], term)
        total = term if total is None else total + term
    r.small_out[...] = total


def gather_params(r):
    for b in range(2):
        r.params[2 * b : 2 * b + 2] = r.block_norm_multiplier[b]
        r.params[4 + 2 * b : 6 + 2 * b] = r.block_norm_bias[b]
        r.params[8 + 2 * b : 10 + 2 * b] = r.layer_scale[b]
        for h in range(WIDE // HD):
            lanes = slice(HD * h, HD * h + HD)
            r.head_params[2 * b : 2 * b + 2, lanes] = r.qk_gain[b]
            r.head_params[4 + 2 * b : 6 + 2 * b, lanes] = r.qk_bias[b]
    r.params[12:16] = jnp.zeros((4, WIDE), F32)


def find_scenes(r):
    for slot in range(r.slot_frames.shape[0]):
        frame = r.slot_frames[slot]
        end, scene = 0, 0
        for number in range(r.frame_counts.shape[0]):
            end = end + r.frame_counts[number]
            scene = scene + jnp.where(end <= frame, 1, 0)
        r.scenes[slot] = scene


def whole_kernel(names, *refs):
    r = Refs(names, refs, True)
    gather_params(r)
    start_phase(r)
    greet(line(r.s, r.z) + [r.chip_device(r.chip(d)) for d in range(1, 4)] + [r.sibling])
    numbers = {NAMES.down: 0, NAMES.up: 1, NAMES.out: 2, NAMES.qkv: 3}
    later = {name: SeqSum(r, name, 1, number) for name, number in numbers.items()}
    sooner = {name: SeqSum(r, name, 0, 4 + number) for name, number in numbers.items()}
    r.sums[...] = jnp.zeros_like(r.sums)
    r.head_sums[...] = jnp.zeros_like(r.head_sums)
    find_scenes(r)
    whole_out = WholeOut(r, 20)
    whole_out.fetch(1).start()
    block_zero_phase(r, whole_out)
    global_forward_phase(r)
    middle_phase(r, later)
    global_backward_phase(r, later)
    attention_back_phase(r, later)
    features_wait(r.final_low, r.out_rows, *r.line_sems(12))
    mlp_back_phase(r, sooner, later)
    last_phase(r, sooner, later)
    small_phase(r)
    features_wait(r.final, r.grad_rows, *r.line_sems(18))
    sooner[NAMES.qkv].finish()
    sooner[NAMES.out].finish()
    for total in (*later.values(), *sooner.values()):
        total.store().wait()


def plain_kernel(phase, names, fresh, weights, *refs):
    r = Refs(names, refs, False)
    greet(line(r.s, r.z))
    for name in fresh:
        getattr(r, name)[...] = jnp.zeros_like(getattr(r, name))
    if phase is block_zero_phase:
        start_phase(r)
    if phase is last_phase:
        r.sums[...] = r.sums_in[...]
        r.head_sums[...] = r.head_sums_in[...]
    phase(r)


def results_kernel(
    out_rows,
    grad_rows,
    small,
    qkv_in,
    out_in,
    up_in,
    down_in,
    out_tokens,
    grad_tokens,
    gains,
    norm_bias,
    mlp_bias,
    head_gain,
    head_bias,
    scales,
    qkv,
    out,
    up,
    down,
    qkv_held,
    out_held,
    up_held,
    down_held,
    out_rows_held,
    grad_rows_held,
    small_held,
    sems,
):
    sources = (qkv_in, out_in, up_in, down_in, out_rows, grad_rows, small)
    held = (qkv_held, out_held, up_held, down_held, out_rows_held, grad_rows_held, small_held)
    loads = [pltpu.make_async_copy(sources[i], held[i], sems.at[0, i]) for i in range(7)]
    for copy in (loads[4], loads[5], loads[6], *loads[:4]):
        copy.start()
    stores = [
        pltpu.make_async_copy(held[i], target, sems.at[1, i]) for i, target in enumerate((qkv, out, up, down))
    ]
    for load, store in zip(loads, stores):
        load.wait()
        store.start()
    for copy in loads[4:]:
        copy.wait()
    out_rows, grad_rows, small = held[4:]
    out_tokens[...] = out_rows[pl.ds(0, TOK)]
    grad_tokens[...] = grad_rows[pl.ds(0, TOK)].astype(F32)
    for b in range(2):
        gains[b] = small[2 * b : 2 * b + 2]
        scales[b] = small[8 + 2 * b : 10 + 2 * b]
    norm_bias[...] = small[4:6]
    mlp_bias[...] = small[6:8]
    row = lax.broadcasted_iota(jnp.int32, (WIDE, HD), 0)
    col = lax.broadcasted_iota(jnp.int32, (WIDE, HD), 1)
    fold = jnp.where(lax.bitwise_and(row, HD - 1) == col, 1.0, 0.0).astype(F32)
    heads = jnp.dot(small[16:24], fold, precision=HIGH, preferred_element_type=F32)
    for b in range(2):
        head_gain[b] = heads[4 * b : 4 * b + 2]
        head_bias[b] = heads[4 * b + 2 : 4 * b + 4]
    for store in stores:
        store.wait()


def gather_frames(rows):
    return lax.all_gather(rows, "seq", axis=0)


def global_forward_plain(query_rows, key_rows, value_rows, allowed_frames):
    head_count = query_rows.shape[1]
    state = (
        jnp.full((head_count, TOK), NEG, F32),
        jnp.zeros((head_count, TOK), F32),
        jnp.zeros((head_count, TOK, HD), F32),
    )

    def advance(running, item):
        key_block, value_block, allowed = item

        def update(current):
            peak, totals, weighted = current
            scores = jnp.einsum("qhd,khd->hqk", query_rows, key_block, preferred_element_type=F32)
            new_peak = jnp.maximum(peak, jnp.max(scores, axis=-1))
            expo = jnp.exp(scores - new_peak[..., None])
            factor = jnp.exp(peak - new_peak)
            totals = totals * factor + jnp.sum(expo, axis=-1)
            weighted = weighted * factor[..., None] + jnp.einsum(
                "hqk,khd->hqd", expo.astype(BF), value_block, preferred_element_type=F32
            )
            return (new_peak, totals, weighted)

        return (lax.cond(allowed, update, lambda current: current, running), None)

    (peak, totals, weighted), _ = lax.scan(
        advance, state, (gather_frames(key_rows), gather_frames(value_rows), allowed_frames)
    )
    attended = jnp.transpose(weighted / totals[..., None], (1, 0, 2))
    return attended, peak + jnp.log(totals)


def global_backward_plain(query_rows, key_rows, value_rows, out_grad, attended, lse, allowed_frames):
    delta = jnp.transpose(jnp.sum(attended * out_grad.astype(F32), axis=-1))
    zero = jnp.zeros(query_rows.shape, F32)

    def pieces(q, do, stat, row_sum, k, v):
        scores = jnp.einsum("qhd,khd->hqk", q, k, preferred_element_type=F32)
        probs = jnp.exp(scores - stat[..., None])
        dprobs = jnp.einsum("qhd,khd->hqk", do, v, preferred_element_type=F32)
        return probs.astype(BF), (probs * (dprobs - row_sum[..., None])).astype(BF)

    def advance_query(total, item):
        k, v, allowed = item

        def update(current):
            _, dscores = pieces(query_rows, out_grad, lse, delta, k, v)
            return current + jnp.einsum("hqk,khd->qhd", dscores, k, preferred_element_type=F32)

        return (lax.cond(allowed, update, lambda current: current, total), None)

    dq, _ = lax.scan(
        advance_query, zero, (gather_frames(key_rows), gather_frames(value_rows), allowed_frames)
    )

    def advance_keys(totals, item):
        q, do, stat, row_sum, allowed = item

        def update(current):
            probs, dscores = pieces(q, do, stat, row_sum, key_rows, value_rows)
            return (
                current[0] + jnp.einsum("hqk,qhd->khd", dscores, q, preferred_element_type=F32),
                current[1] + jnp.einsum("hqk,qhd->khd", probs, do, preferred_element_type=F32),
            )

        return (lax.cond(allowed, update, lambda current: current, totals), None)

    (dk, dv), _ = lax.scan(
        advance_keys,
        (zero, zero),
        (
            gather_frames(query_rows),
            gather_frames(out_grad),
            gather_frames(lse),
            gather_frames(delta),
            allowed_frames,
        ),
    )
    return dq, dk, dv


def buffers(depth, hidden):
    rows_d = ((RP, depth), BF)
    rows_w = ((RP, WIDE), BF)
    wide_f = ((RP, WIDE), F32)
    own_f = ((RO, depth), F32)
    raw = ((2, RP, WIDE), F32)
    slab = (RP, 2 * HD)
    table = {
        NAMES.params_full: ((16, depth), F32),
        NAMES.every: rows_d,
        NAMES.wof: ((NZ, 8, WIDE // 8, depth), BF),
        NAMES.wo_part: ((WIDE // 8, depth), BF),
        NAMES.att_in: ((RO, depth), BF),
        NAMES.datt_own: ((RO, depth), BF),
        NAMES.part: rows_d,
        NAMES.part_out: rows_d,
        NAMES.inbox: ((2, 4, RO, depth), BF),
        NAMES.wq: ((3, depth, WIDE), BF),
        NAMES.wo: ((WIDE, depth), BF),
        NAMES.wu: ((depth, hidden), BF),
        NAMES.wd: ((hidden, depth), BF),
        NAMES.act0: ((RP, hidden), BF),
        NAMES.act1: ((RP, hidden), BF),
        NAMES.slope0: ((RP, hidden), F32),
        NAMES.slope1: ((RP, hidden), F32),
        NAMES.dpre: ((RP, hidden), BF),
        NAMES.final_low: ((RO, depth), BF),
        NAMES.final: ((RO, depth), BF),
        NAMES.dproj: ((3, RP, WIDE), BF),
        NAMES.sums: ((16, depth), F32),
        NAMES.head_sums: ((8, WIDE), F32),
        NAMES.messages: ((NZ, 24, WIDE), F32),
        NAMES.letters: ((NZ - 1, 24, WIDE), F32),
        NAMES.small: ((24, WIDE), F32),
        NAMES.small_two: ((24, WIDE), F32),
        NAMES.small_in: ((4, 24, WIDE), F32),
        NAMES.qk: ((8,) + slab, BF),
        NAMES.vv: ((8,) + slab, BF),
        NAMES.ks: ((8 * RP, 2 * HD), BF),
        NAMES.lse: ((4,) + slab, F32),
        NAMES.slabs: ((4,) + slab, BF),
        NAMES.pairs: ((4, HALF_ROWS, 2 * HD), BF),
        NAMES.outs: ((4, HALF_ROWS, 2 * HD), BF),
        NAMES.outs_full: ((4,) + slab, F32),
        NAMES.ins: ((4, HALF_ROWS, 2 * HD), BF),
        NAMES.dos: ((4, HALF_ROWS, 2 * HD), BF),
        NAMES.dkt: ((2 * HD, 8 * RP), F32),
        NAMES.dvt: ((2 * HD, 8 * RP), F32),
        NAMES.dq_mine: ((4,) + slab, F32),
        NAMES.dk_sum: ((8 * RP, 2 * HD), F32),
        NAMES.dv_sum: ((8 * RP, 2 * HD), F32),
        NAMES.dkv_send: ((4,) + slab, BF),
        NAMES.dkv_in: ((4,) + slab, BF),
        NAMES.ready: ((4,) + slab, BF),
        NAMES.ready_values: ((4, HALF_ROWS, 2 * HD), BF),
        NAMES.packed_values: ((8, HALF_ROWS, 2 * HD), BF),
        NAMES.do_rows: (slab, BF),
        NAMES.dqk_in: ((4,) + slab, BF),
        NAMES.dv_in: ((4, HALF_ROWS, 2 * HD), BF),
        NAMES.out_rows: rows_w,
        NAMES.grad_rows: rows_w,
    }
    for name in (NAMES.q0, NAMES.k0, NAMES.v0, NAMES.att0, NAMES.q1, NAMES.k1, NAMES.v1, NAMES.att1, NAMES.datt1):
        table[name] = rows_w
    for name in (NAMES.dq, NAMES.dk, NAMES.dv):
        table[name] = wide_f
    for name in (NAMES.h0, NAMES.m0, NAMES.h1, NAMES.m1, NAMES.grad_full, NAMES.dmlp, NAMES.dbr1, NAMES.dm0, NAMES.dbr0):
        table[name] = rows_d
    for name in (NAMES.x0, NAMES.x1, NAMES.x2, NAMES.x3, NAMES.br0, NAMES.br1, NAMES.mo0, NAMES.g3, NAMES.g5, NAMES.g6):
        table[name] = own_f
    for name in (NAMES.raw0, NAMES.raw1):
        table[name] = raw
    piece = {
        NAMES.qkv: (3, depth // 8, WIDE),
        NAMES.out: (WIDE, depth // 8),
        NAMES.up: (depth // 8, hidden),
        NAMES.down: (hidden, depth // 8),
    }
    for name, shape in piece.items():
        table[NAMES.d_ + name] = ((2, 4) + shape, BF)
        table[NAMES.first_ + name] = ((4,) + shape, BF)
        table[NAMES.second_ + name] = ((2, 3) + shape, BF)
    return table


SEMAPHORES = {
    NAMES.fetch_sem: (5,),
    NAMES.z_send: (24, 4),
    NAMES.z_recv: (24, 4),
    NAMES.wo_send: (1, 7),
    NAMES.wo_recv: (1, 7),
    NAMES.f_send: (2, 3),
    NAMES.f_recv: (2, 3),
    NAMES.fc_send: (2, 4),
    NAMES.fc_recv: (2, 4),
    NAMES.fb_send: (3,),
    NAMES.fb_recv: (3,),
    NAMES.b_send: (3,),
    NAMES.b_recv: (3,),
    NAMES.bc_send: (1,),
    NAMES.bc_recv: (1,),
    NAMES.bb_send: (2, 3),
    NAMES.bb_recv: (2, 3),
    NAMES.store_sem: (8,),
    NAMES.sum_send: (8, 4),
    NAMES.sum_recv: (8, 4),
    NAMES.small_send: (4,),
    NAMES.small_recv: (4,),
}
GRADS = (NAMES.grad_w_qkv, NAMES.grad_w_out, NAMES.grad_w_up, NAMES.grad_w_down)
IN_HBM = (NAMES.w_qkv, NAMES.w_out, NAMES.w_up, NAMES.w_down)


def call(body, given, outs, scratch, collective_id, name, vmem_mib):
    names = list(given) + list(outs) + list(scratch)
    def room(shape, kind):
        if kind is None:
            return pltpu.SemaphoreType.DMA(shape)
        return pltpu.SMEM(shape, jnp.int32) if kind == NAMES.scalars else pltpu.VMEM(shape, kind)

    def space(key):
        if key in IN_HBM or key in GRADS:
            return pl.ANY
        return pltpu.SMEM if key in (NAMES.frame_counts, NAMES.slot_frames) else pltpu.VMEM

    scratch_shapes = [room(shape, kind) for shape, kind in scratch.values()]
    results = pl.pallas_call(
        partial(body, names),
        name=name,
        out_shape=[jax.ShapeDtypeStruct(shape, kind) for shape, kind in outs.values()],
        in_specs=[pl.BlockSpec(memory_space=space(key)) for key in given],
        out_specs=[pl.BlockSpec(memory_space=space(key)) for key in outs],
        scratch_shapes=scratch_shapes,
        compiler_params=pltpu.CompilerParams(
            collective_id=collective_id, has_side_effects=True, vmem_limit_bytes=vmem_mib * 2**20
        ),
    )(*given.values())
    return dict(zip(outs, results))


def whole(given, depth, hidden):
    table = buffers(depth, hidden)
    frame_total = given[NAMES.slot_frames].shape[0]
    table[NAMES.params] = ((16, WIDE), F32)
    table[NAMES.head_params] = ((8, WIDE), F32)
    outs = {
        NAMES.out_rows: table.pop(NAMES.out_rows),
        NAMES.grad_rows: table.pop(NAMES.grad_rows),
        NAMES.small_out: ((24, WIDE), F32),
        NAMES.grad_w_qkv: ((2, 3, depth // 8, WIDE), F32),
        NAMES.grad_w_out: ((2, WIDE, depth // 8), F32),
        NAMES.grad_w_up: ((2, depth // 8, hidden), F32),
        NAMES.grad_w_down: ((2, hidden, depth // 8), F32),
    }
    scratch = {**table, **{name: (shape, None) for name, shape in SEMAPHORES.items()}}
    for name in GRADS:
        scratch[name.replace(NAMES.grad_w_, NAMES.held_)] = outs[name]
    scratch[NAMES.scenes] = ((frame_total,), NAMES.scalars)
    out = call(whole_kernel, given, outs, scratch, 0, NAMES.whole, 62)
    big = GRADS
    shapes = [
        ((TOK, WIDE), BF),
        ((TOK, WIDE), F32),
        ((2, 2, WIDE), F32),
        ((2, WIDE), F32),
        ((2, WIDE), F32),
        ((2, 2, HD), F32),
        ((2, 2, HD), F32),
        ((2, 2, WIDE), F32),
    ] + [outs[name] for name in big]
    in_vmem, in_hbm = pl.BlockSpec(memory_space=pltpu.VMEM), pl.BlockSpec(memory_space=pl.ANY)
    results = pl.pallas_call(
        results_kernel,
        name=NAMES.results,
        out_shape=[jax.ShapeDtypeStruct(shape, kind) for shape, kind in shapes],
        in_specs=[in_hbm] * 7,
        out_specs=[in_vmem] * 8 + [in_hbm] * 4,
        scratch_shapes=[pltpu.VMEM(*outs[name]) for name in big + (NAMES.out_rows, NAMES.grad_rows, NAMES.small_out)]
        + [pltpu.SemaphoreType.DMA((2, 7))],
        compiler_params=pltpu.CompilerParams(vmem_limit_bytes=60 * 2**20),
    )(out[NAMES.out_rows], out[NAMES.grad_rows], out[NAMES.small_out], *(out[name] for name in big))
    return tuple(results[:7]) + tuple(results[8:12]) + (results[7],)


def by_phases(given, same_scene, depth, hidden):
    heads_here = WIDE // HD
    table = buffers(depth, hidden)
    table[NAMES.d_qkv] = ((3, depth, WIDE), BF)
    table[NAMES.d_out] = ((WIDE, depth), BF)
    table[NAMES.d_up] = ((depth, hidden), BF)
    table[NAMES.d_down] = ((hidden, depth), BF)
    held = dict(given)

    def run(phase, ins, outs, scratch, fresh=()):
        ins = {name: held[name] for name in ins}
        outs = {name: table[name] for name in outs}
        scratch = {name: table[name] for name in scratch}
        for name in (NAMES.fetch_sem, NAMES.z_send, NAMES.z_recv):
            scratch[name] = (SEMAPHORES[name], None)

        def body(names, *refs):
            plain_kernel(phase, names, fresh, None, *refs)

        number = (block_zero_phase, middle_phase, attention_back_phase, mlp_back_phase, last_phase).index(phase)
        held.update(call(body, ins, outs, scratch, 1 + number, phase.__name__, 48))

    def rows(array):
        return array[:TOK].reshape(TOK, heads_here, HD)

    def padded(array):
        return jnp.pad(array.reshape(TOK, -1), ((0, RP - TOK), (0, 0)))

    allowed = same_scene[lax.axis_index("seq")]
    run(
        block_zero_phase,
        (NAMES.tokens, NAMES.params, NAMES.head_params) + IN_HBM,
        (NAMES.params_full, NAMES.x0, NAMES.h0, NAMES.raw0, NAMES.q0, NAMES.k0, NAMES.v0, NAMES.att0, NAMES.x1, NAMES.br0, NAMES.m0, NAMES.act0, NAMES.slope0, NAMES.mo0, NAMES.x2, NAMES.h1, NAMES.raw1, NAMES.q1, NAMES.k1, NAMES.v1),
        (NAMES.every, NAMES.part, NAMES.inbox, NAMES.wq, NAMES.wo, NAMES.wu, NAMES.wd),
    )
    q1, k1, v1 = rows(held[NAMES.q1]), rows(held[NAMES.k1]), rows(held[NAMES.v1])
    attended, lse = global_forward_plain(q1, k1, v1, allowed)
    held[NAMES.att1] = padded(attended.astype(BF))
    held[NAMES.grad_full] = padded(lax.all_gather(given[NAMES.grad_out], "mp", axis=1, tiled=True))
    run(
        middle_phase,
        (NAMES.att1, NAMES.x2, NAMES.grad_full, NAMES.params_full, NAMES.w_out, NAMES.w_up, NAMES.w_down),
        (NAMES.out_rows, NAMES.g3, NAMES.x3, NAMES.br1, NAMES.dbr1, NAMES.datt1, NAMES.d_up, NAMES.d_down, NAMES.sums),
        (NAMES.part, NAMES.part_out, NAMES.inbox, NAMES.m1, NAMES.act1, NAMES.slope1, NAMES.dmlp, NAMES.dpre, NAMES.final_low, NAMES.wo, NAMES.wu, NAMES.wd),
        (NAMES.sums,),
    )
    d_up1 = lax.psum_scatter(held[NAMES.d_up], "seq", scatter_dimension=0, tiled=True)
    d_down1 = lax.psum_scatter(held[NAMES.d_down], "seq", scatter_dimension=1, tiled=True)
    sums = held[NAMES.sums]
    grads = global_backward_plain(q1, k1, v1, rows(held[NAMES.datt1]), attended, lse, allowed)
    held[NAMES.dq], held[NAMES.dk], held[NAMES.dv] = (padded(array) for array in grads)
    d_out1 = lax.dot_general(
        held[NAMES.att1], held[NAMES.dbr1], (((0,), (0,)), ((), ())), preferred_element_type=F32
    ).astype(BF)
    run(
        attention_back_phase,
        (NAMES.dq, NAMES.dk, NAMES.dv, NAMES.raw1, NAMES.h1, NAMES.x2, NAMES.g3, NAMES.mo0, NAMES.params_full, NAMES.head_params, NAMES.w_qkv),
        (NAMES.g5, NAMES.dm0, NAMES.d_qkv, NAMES.sums, NAMES.head_sums),
        (NAMES.part, NAMES.inbox, NAMES.dproj, NAMES.wq),
        (NAMES.sums, NAMES.head_sums),
    )
    d_qkv1 = lax.psum_scatter(held[NAMES.d_qkv], "seq", scatter_dimension=1, tiled=True)
    d_out1 = lax.psum_scatter(d_out1, "seq", scatter_dimension=1, tiled=True)
    sums = sums + held[NAMES.sums]
    held[NAMES.head_sums_in] = held[NAMES.head_sums]
    run(
        mlp_back_phase,
        (NAMES.dm0, NAMES.act0, NAMES.slope0, NAMES.m0, NAMES.x1, NAMES.g5, NAMES.br0, NAMES.params_full, NAMES.w_up, NAMES.w_down),
        (NAMES.g6, NAMES.dbr0, NAMES.d_up, NAMES.d_down, NAMES.sums),
        (NAMES.part, NAMES.inbox, NAMES.dpre, NAMES.wu, NAMES.wd),
        (NAMES.sums,),
    )
    d_up0 = lax.psum_scatter(held[NAMES.d_up], "seq", scatter_dimension=0, tiled=True)
    d_down0 = lax.psum_scatter(held[NAMES.d_down], "seq", scatter_dimension=1, tiled=True)
    held[NAMES.sums_in] = sums + held[NAMES.sums]
    run(
        last_phase,
        (NAMES.dbr0, NAMES.att0, NAMES.raw0, NAMES.q0, NAMES.k0, NAMES.v0, NAMES.h0, NAMES.x0, NAMES.g6, NAMES.params_full, NAMES.head_params, NAMES.sums_in, NAMES.head_sums_in, NAMES.w_out, NAMES.w_qkv),
        (NAMES.grad_rows, NAMES.d_qkv, NAMES.d_out, NAMES.small),
        (NAMES.part, NAMES.inbox, NAMES.dproj, NAMES.final, NAMES.messages, NAMES.letters, NAMES.sums, NAMES.head_sums, NAMES.wo, NAMES.wq),
    )
    d_qkv0 = lax.psum_scatter(held[NAMES.d_qkv], "seq", scatter_dimension=1, tiled=True)
    d_out0 = lax.psum_scatter(held[NAMES.d_out], "seq", scatter_dimension=1, tiled=True)

    def both(first, second):
        return jnp.stack([first, second]).astype(F32)

    return {
        NAMES.out_rows: held[NAMES.out_rows],
        NAMES.grad_rows: held[NAMES.grad_rows].astype(F32),
        NAMES.small_out: lax.psum(held[NAMES.small], "seq"),
        NAMES.grad_w_qkv: both(d_qkv0, d_qkv1),
        NAMES.grad_w_out: both(d_out0, d_out1),
        NAMES.grad_w_up: both(d_up0, d_up1),
        NAMES.grad_w_down: both(d_down0, d_down1),
    }


def per_device(
    tokens,
    grad_out,
    frame_counts,
    slot_frames,
    block_norm_multiplier,
    block_norm_bias,
    qk_gain,
    qk_bias,
    w_qkv,
    w_out,
    w_up,
    w_down,
    layer_scale,
):
    depth = w_qkv.shape[2]
    hidden = w_up.shape[2]
    given = {
        NAMES.tokens: tokens,
        NAMES.grad_out: grad_out,
        NAMES.w_qkv: w_qkv,
        NAMES.w_out: w_out,
        NAMES.w_up: w_up,
        NAMES.w_down: w_down,
    }
    if lax.axis_size("seq") == 8:
        given.update(
            frame_counts=frame_counts,
            slot_frames=slot_frames,
            block_norm_multiplier=block_norm_multiplier,
            block_norm_bias=block_norm_bias,
            qk_gain=qk_gain,
            qk_bias=qk_bias,
            layer_scale=layer_scale,
        )
        return whole(given, depth, hidden)

    heads_here = WIDE // HD
    frame_total = slot_frames.shape[0]
    frame_ids = jnp.arange(frame_total, dtype=jnp.int32)
    scene_ends = jnp.cumsum(frame_counts)
    scene_of_frame = jnp.sum((scene_ends[None, :] <= frame_ids[:, None]).astype(jnp.int32), axis=1)
    scene_table = jnp.sum(
        jnp.where(slot_frames[:, None] == frame_ids[None, :], scene_of_frame[None, :], 0), axis=1
    )
    same_scene = scene_table[:, None] == scene_table[None, :]
    given[NAMES.params] = jnp.concatenate(
        [
            block_norm_multiplier.reshape(4, WIDE),
            block_norm_bias.reshape(4, WIDE),
            layer_scale.reshape(4, WIDE),
            jnp.zeros((4, WIDE), F32),
        ]
    )
    given[NAMES.head_params] = jnp.tile(
        jnp.concatenate([qk_gain.reshape(4, HD), qk_bias.reshape(4, HD)]), (1, heads_here)
    )
    out = by_phases(given, same_scene, depth, hidden)
    small = out[NAMES.small_out]
    head_grads = small[16:24].reshape(2, 2, 2, heads_here, HD).sum(axis=3)
    return (
        out[NAMES.out_rows][:TOK],
        out[NAMES.grad_rows][:TOK],
        small[0:4].reshape(2, 2, WIDE),
        small[4:6],
        small[6:8],
        head_grads[:, 0],
        head_grads[:, 1],
        out[NAMES.grad_w_qkv],
        out[NAMES.grad_w_out],
        out[NAMES.grad_w_up],
        out[NAMES.grad_w_down],
        small[8:12].reshape(2, 2, WIDE),
    )


def solution(mesh):
    in_specs = (
        P("seq", "mp"),
        P("seq", "mp"),
        P(),
        P(),
        P(None, None, "mp"),
        P(None, None, "mp"),
        P(),
        P(),
        P(None, None, None, "mp"),
        P(None, "mp", None),
        P(None, None, "mp"),
        P(None, "mp", None),
        P(None, None, "mp"),
    )
    out_specs = (
        P("seq", "mp"),
        P("seq", "mp"),
        P(None, None, "mp"),
        P(None, "mp"),
        P(None, "mp"),
        P(),
        P(),
        P(None, None, "seq", "mp"),
        P(None, "mp", "seq"),
        P(None, "seq", "mp"),
        P(None, "mp", "seq"),
        P(None, None, "mp"),
    )
    return jax.shard_map(
        per_device, mesh=mesh, in_specs=in_specs, out_specs=out_specs, check_vma=False
    )
```
